32 devices in a mesh: dp: 4 (over z), row: 4 (over y, x), col: 2 (over core).
Axes of the slice: x: 2, y: 2, z: 4, core: 2. Of those that a mesh axis runs over, the one named last changes fastest.
Arguments:
- layer_in: bfloat16 [8192, 768], P(('dp', 'row')), may hold values from -6 to 6
- w_qkv: bfloat16 [3, 768, 768], P(None, 'col', 'row'), may hold values from -0.21875 to 0.21875
- w_proj: bfloat16 [768, 768], P('row', 'col'), may hold values from -3.5 to 3.5
- rel_bias: float32 [12, 32], replicated, may hold values from -4 to 4
- rel_bucket: int32 [2047], replicated, may hold values from 0 to 31
- segment_ids: int32 [8, 1024], P(('dp', 'col')), may hold values from 0 to 2, never falling along the last dimension, each value on 1 to 512 neighbouring positions
- gain_attn: float32 [768], replicated, may hold values from 0.1 to 1.9
- gain_ffn: float32 [768], replicated, may hold values from 0.1 to 1.9
- w_router: float32 [768, 16], replicated, may hold values from -0.109375 to 0.109375
- routes: int32 [8192, 1], P(('dp', 'row')), may hold values from 0 to 15; in each aligned block of 512 rows (0 to 511, 512 to 1023, ...) at most 64 rows name the same one
- w_up: bfloat16 [16, 3072, 768], P(('row', 'col')), may hold values from -0.21875 to 0.21875
- w_down: bfloat16 [16, 3072, 768], P(('row', 'col')), may hold values from -2.5 to 2.5
- d_layer: bfloat16 [8192, 768], P(('dp', 'row'), 'col'), may hold values from -6 to 6
Outputs:
- layer_out: float32 [8192, 768], P(('dp', 'row'), 'col')
- d_layer_in: float32 [8192, 768], P(('dp', 'row'), 'col')
- d_w_qkv: float32 [3, 768, 768], P(None, 'col', 'row')
- d_w_proj: float32 [768, 768], P('row', 'col')
- d_rel_bias: float32 [12, 32], replicated
- d_gain_attn: float32 [768], replicated
- d_gain_ffn: float32 [768], replicated
- d_w_router: float32 [768, 16], replicated
- d_w_up: float32 [16, 3072, 768], P(('row', 'col'), 'dp')
- d_w_down: float32 [16, 3072, 768], P(('row', 'col'), 'dp')
The draws below stay inside these ranges and needn't reach their ends.
Inputs may be any that keep to these rules, and one draw needn't show every extreme that they name: `routes`: in each aligned block of 512 rows (the rows of one device) no expert is named by more than 64 rows. `segment_ids`: within each sequence the ids never fall; a document has 1 to 512 tokens.
All inputs are finite; a program needn't handle non-finite values.
Results may differ from the reference program's by a relative error of at most 0.017.
Values may be sent and summed in bfloat16 or wider, within the bound.
No kernel may reach another device: no remote copies, remote signals or barrier semaphores. Data moves between devices by JAX's collectives and lax.ppermute only.
A program may use at most 192 MiB of HBM per device.

```python
import math
import jax
import jax.numpy as jnp
import numpy as np
from jax import lax

D = 768
H = 12
HD = 64
FF = 3072
NB = 32
LENGTH = 1024
E = 16
SEQS = 8
TOKENS = 8192
TOK_DEV = 512
CAP = 64
DOCS = 3
DOC_MOST = 512


def set_ends(entries, own_key, smallest, top_value):
    place = [jax.random.randint(jax.random.fold_in(own_key, axis), (), 0, length) for axis, length in enumerate(entries.shape)]
    main_axis = entries.shape.index(max(entries.shape))
    beside = place[:main_axis] + [(place[main_axis] + 1) % entries.shape[main_axis]] + place[main_axis + 1:]
    return entries.at[tuple(place)].set(smallest).at[tuple(beside)].set(top_value)


def block_levels(own_key, dims, cuts, least, largest):
    level = 1.0
    for dim, parts in cuts:
        heights = jax.random.uniform(jax.random.fold_in(jax.random.fold_in(own_key, 6), dim), (parts,), jnp.float32, least / len(cuts), largest / len(cuts))
        level = level * jnp.repeat(jnp.exp(heights), dims[dim] // parts).reshape((-1,) + (1,) * (len(dims) - 1 - dim))
    return level


def length_profile(amount, total, reach, slope):
    loads = [(1 << 20) // math.isqrt(grade ** slope) + 1 for grade in range(2, amount + 1)]
    spare, given = total - reach - (amount - 1), [1] * (amount - 1)
    while spare > 0:
        free = [i for i in range(amount - 1) if given[i] < reach]
        pool, budget = sum([loads[i] for i in free]), spare
        for i in free:
            extra = min(reach - given[i], max(1, budget * loads[i] // pool), spare)
            given[i] = given[i] + extra
            spare = spare - extra
    return np.array([reach] + given)


def ragged(stream_key, number_of, total, limit, skew):
    if number_of == 2:
        one = jax.random.randint(stream_key, (), max(1, total - limit), min(limit, total - 1) + 1)
        return jnp.stack([one, total - one])
    tallies = jnp.asarray(length_profile(number_of, total, limit, skew), jnp.int32)
    couples = (number_of - 1) // 2
    source_of, taker = tallies[1:1 + 2 * couples:2], tallies[2:2 + 2 * couples:2]
    margin = jnp.minimum(source_of - 1, limit - taker)
    moved = jax.random.randint(jax.random.fold_in(stream_key, 1), (couples,), 0, 1 << 20) % (margin + 1)
    tallies = tallies.at[1:1 + 2 * couples:2].set(source_of - moved).at[2:2 + 2 * couples:2].set(taker + moved)
    return tallies[jax.random.permutation(jax.random.fold_in(stream_key, 2), number_of)]


def deal_out(stream_key, own, number, rows, number_of, top, bound, skew):
    sequence = jax.random.permutation(stream_key, number_of)
    crowded, usual = shares(number_of, rows * top, bound, skew, True), shares(number_of, rows * top, bound, skew, False)
    places = jnp.arange(number_of)

    def named(sizes, turn):
        used = int((sizes > 0).sum())
        fixed = max(1, used // 4)
        shifted = fixed + (places - fixed + turn * (used - fixed)) % max(1, number_of - fixed)
        return jnp.zeros((number_of,), jnp.int32).at[sequence[jnp.where(places < fixed, places, shifted)]].set(jnp.asarray(sizes, jnp.int32))

    sizes = jnp.where(number % 4 == 0, named(crowded, number // 4), named(usual, number - number // 4 - 1))
    mixed = jax.random.permutation(jax.random.fold_in(own, 3), number_of)
    source_of, sink = mixed[0:number_of // 2 * 2:2], mixed[1:number_of // 2 * 2:2]
    room = jnp.minimum(sizes[source_of] - 1, bound - sizes[sink]) // 2
    room = jnp.where((source_of == sequence[0]) | (sink == sequence[0]) | (sizes[sink] == 0), 0, jnp.maximum(room, 0))
    shifted = jax.random.randint(jax.random.fold_in(own, 4), (number_of // 2,), 0, 1 << 20) % (room + 1)
    sizes = sizes.at[source_of].add(-shifted).at[sink].add(shifted)
    labels = jnp.searchsorted(jnp.cumsum(sizes), jnp.arange(rows * top), side="right").astype(jnp.int32)
    table = labels.reshape(top, rows).T
    table = table[jax.random.permutation(jax.random.fold_in(own, 1), rows)]
    turn = jax.random.randint(jax.random.fold_in(own, 2), (rows, 1), 0, top)
    return jnp.take_along_axis(table, (jnp.arange(top)[None, :] + turn) % top, axis=1)


def shares(amount, total, bound, skew, full):
    loads = [(1 << 20) // math.isqrt(standing ** skew) + 1 for standing in range(1, amount + 1)]
    largest = bound if full else min(bound, max(-(-total // amount), total * loads[0] // sum(loads)))
    least = 1 if total - largest >= amount - 1 else 0
    given, surplus = [largest] + [least] * (amount - 1), total - largest - least * (amount - 1)
    while surplus > 0:
        candidates = [i for i in range(1, amount) if given[i] < largest] or [i for i in range(1, amount) if given[i] < bound]
        whole, left = sum([loads[i] for i in candidates]), surplus
        for i in candidates:
            addition = min(bound - given[i], max(1, left * loads[i] // whole), surplus)
            given[i] = given[i] + addition
            surplus = surplus - addition
    return np.array(given)


def normal_values(rng, extent, width, most, shards=(), kind=jnp.bfloat16):
    values = jax.random.normal(rng, extent, jnp.float32) * width
    if len(shards) > 0:
        values = block_levels(rng, extent, shards, -0.22, 0.18) * values
    return jnp.clip(values, min=-most, max=most).astype(kind)


def setup_inputs(seed: int = 0) -> dict:
    key_list = jax.random.split(jax.random.key(seed), 14)
    layer_in = normal_values(key_list[0], (TOKENS, D), 1.0, 6.0, ((0, 16),))
    w_qkv = normal_values(key_list[1], (3, D, D), D ** -0.5, 0.21875, ((1, 2), (2, 4)))
    w_proj = normal_values(key_list[2], (D, D), (max(1, D // 256)) ** -0.5, 3.5, ((0, 4), (1, 2)))
    rel_bias = normal_values(key_list[3], (H, NB), 1.0, 4.0, (), jnp.float32)
    rel_bucket = set_ends(jax.random.randint(key_list[4], (2 * LENGTH - 1,), 0, NB), jax.random.fold_in(key_list[4], 1), 0, NB - 1).astype(jnp.int32)
    segment_ids = jax.vmap(lambda own: jnp.searchsorted(jnp.cumsum(ragged(own, DOCS, LENGTH, DOC_MOST, 0)), jnp.arange(LENGTH), side="right"))(jax.random.split(key_list[5], SEQS)).reshape((SEQS, LENGTH)).astype(jnp.int32)
    gain_attn = jnp.clip(1.0 + 0.18 * jax.random.normal(key_list[6], (D,), jnp.float32), 0.1, 1.9)
    gain_ffn = jnp.clip(1.0 + 0.18 * jax.random.normal(key_list[7], (D,), jnp.float32), 0.1, 1.9)
    w_router = normal_values(key_list[8], (D, E), (4 * D) ** -0.5, 0.109375, (), jnp.float32)
    routes_keys = jax.random.split(jax.random.fold_in(key_list[9], 1), TOKENS // TOK_DEV)
    routes_turns = jax.random.permutation(jax.random.fold_in(key_list[9], 3), TOKENS // TOK_DEV)
    routes = jax.vmap(lambda own, number: deal_out(jax.random.fold_in(key_list[9], 2), own, number, TOK_DEV, E, 1, CAP, 2))(routes_keys, routes_turns).reshape((TOKENS, 1))
    w_up = normal_values(key_list[10], (E, FF, D), D ** -0.5, 0.21875, ((0, 8),))
    w_down = normal_values(key_list[11], (E, FF, D), (max(1, FF // 512)) ** -0.5, 2.5, ((0, 8),))
    d_layer = normal_values(key_list[12], (TOKENS, D), 1.0, 6.0, ((0, 16), (1, 2)))
    return dict(layer_in=layer_in, w_qkv=w_qkv, w_proj=w_proj, rel_bias=rel_bias, rel_bucket=rel_bucket, segment_ids=segment_ids, gain_attn=gain_attn, gain_ffn=gain_ffn, w_router=w_router, routes=routes, w_up=w_up, w_down=w_down, d_layer=d_layer)


@jax.custom_vjp
def low(v):
    return lax.optimization_barrier(v.astype(jnp.bfloat16)).astype(jnp.float32)

@jax.custom_vjp
def low_back(v):
    return v

def low_keep(v):
    return (low(v), None)

def low_pass(kept, grad):
    return (grad,)

def back_keep(v):
    return (v, None)

def back_low(kept, grad):
    return (low(grad),)
low.defvjp(low_keep, low_pass)
low_back.defvjp(back_keep, back_low)
highest = lax.Precision.HIGHEST
epsilon = 1e-06

def rms_scale(tensor):
    return lax.rsqrt(lax.optimization_barrier(jnp.mean(tensor * tensor, axis=-1, keepdims=True)) + epsilon)

def attend_sequence(packed, bias_table):
    qkv_seq, segments = packed
    queries = qkv_seq[:, 0]
    keys_all = qkv_seq[:, 1]
    values_all = qkv_seq[:, 2]
    block_rows = min(512, LENGTH)
    starts = jnp.arange(LENGTH // block_rows, dtype=jnp.int32) * block_rows

    def one_block(begin_at):
        query_rows = lax.dynamic_slice_in_dim(queries, begin_at, block_rows, 0)
        seg_rows = lax.dynamic_slice_in_dim(segments, begin_at, block_rows, 0)
        raw_scores = low_back(jnp.einsum('qhd,khd->hqk', query_rows, keys_all, precision=highest))
        offset = jnp.arange(LENGTH, dtype=jnp.int32)[None, :] - (begin_at + jnp.arange(block_rows, dtype=jnp.int32))[:, None] + (LENGTH - 1)
        scores = raw_scores * HD ** (-0.5) + jnp.take(bias_table, offset, axis=1)
        same_doc = seg_rows[:, None] == segments[None, :]
        scores = jnp.where(same_doc[None], scores, -1000000000.0)
        row_max = lax.optimization_barrier(jnp.max(scores, axis=-1, keepdims=True))
        weights = jnp.exp(scores - row_max)
        attn_probs = weights / lax.optimization_barrier(jnp.sum(weights, axis=-1, keepdims=True))
        return jnp.einsum('hqk,khd->qhd', low(attn_probs), values_all, precision=highest)
    outputs = lax.map(jax.checkpoint(one_block), starts)
    return outputs.reshape(LENGTH, H * HD)

def expert_apply(packed):
    token_rows, up_rows, down_rows = packed
    pre_act = low_back(jnp.einsum('tk,fk->tf', token_rows, up_rows, precision=highest))
    activated = low(jax.nn.gelu(pre_act, approximate=True))
    return low_back(jnp.einsum('tf,fk->tk', activated, down_rows, precision=highest))

def forward(layer_in, w_qkv, w_proj, rel_bias, gain_attn, gain_ffn, w_router, w_up, w_down, rel_bucket, segment_ids, routes):
    normed = low(layer_in * rms_scale(layer_in) * gain_attn)
    qkv_all = jnp.einsum('td,kde->tke', normed, w_qkv, precision=highest)
    qkv_all = low(low_back(qkv_all)).reshape(SEQS, LENGTH, 3, H, HD)
    bias_table = rel_bias[:, rel_bucket]
    head_out = lax.map(lambda packed: attend_sequence(packed, bias_table), (qkv_all, segment_ids))
    head_out = low(low_back(head_out.reshape(TOKENS, D)))
    attn_out = low_back(jnp.dot(head_out, w_proj, precision=highest))
    middle = layer_in + attn_out
    hidden = middle * rms_scale(middle) * gain_ffn
    gate_probs = jax.nn.softmax(jnp.dot(hidden, w_router, precision=highest), axis=-1)
    routed = routes[:, 0]
    chosen = routed[:, None] == jnp.arange(E, dtype=jnp.int32)[None, :]
    gating = lax.optimization_barrier(jnp.sum(jnp.where(chosen, gate_probs, 0.0), axis=-1))
    blocks = TOKENS // TOK_DEV
    counts = jnp.cumsum(chosen.astype(jnp.int32).reshape(blocks, TOK_DEV, E), axis=1).reshape(TOKENS, E)
    slot_index = (lax.optimization_barrier(jnp.sum(jnp.where(chosen, counts, 0), axis=-1)) - 1).astype(jnp.int32)
    block_of = jnp.arange(TOKENS, dtype=jnp.int32) // TOK_DEV
    placed = ((routed * blocks + block_of) * CAP + slot_index).astype(jnp.int32)
    buffer = jnp.zeros((E * blocks * CAP, D), jnp.float32).at[placed].set(low(hidden))
    expert_out = lax.map(jax.checkpoint(expert_apply), (buffer.reshape(E, blocks * CAP, D), w_up, w_down))
    return middle + gating[:, None] * expert_out.reshape(E * blocks * CAP, D)[placed]

def reference(layer_in, w_qkv, w_proj, rel_bias, rel_bucket, segment_ids, gain_attn, gain_ffn, w_router, routes, w_up, w_down, d_layer):
    floats = (layer_in, w_qkv, w_proj, rel_bias, gain_attn, gain_ffn, w_router, w_up, w_down)
    floats = tuple((member.astype(jnp.float32) for member in floats))

    def layer_fn(*params):
        return forward(*params, rel_bucket, segment_ids, routes)
    layer_out, pullback = jax.vjp(layer_fn, *floats)
    gradients = pullback(d_layer.astype(jnp.float32))
    return (layer_out, gradients[0], gradients[1], gradients[2], gradients[3], gradients[4], gradients[5], gradients[6], gradients[7], gradients[8])
```

```python
from functools import partial

import jax
import jax.numpy as jnp
from jax import lax
from jax.experimental import pallas as pl
from jax.experimental.pallas import tpu as pltpu
from jax.sharding import PartitionSpec as P

H = 12
HD = 64
NB = 32
EXP_DEV = 2
SUB = 128

epsilon = 1e-06
highest = lax.Precision.HIGHEST
f32 = jnp.float32
bf16 = jnp.bfloat16
group = ("row", "col")

NT = (((1,), (1,)), ((), ()))
NN = (((1,), (0,)), ((), ()))
TN = (((0,), (0,)), ((), ()))


def mm(a, b, dims=NN):
    return lax.dot_general(a, b, dims, preferred_element_type=f32)


def fill_strip(table_ref, strip_ref):
    heads, _, span = strip_ref.shape
    for h in range(heads):
        rows = jnp.broadcast_to(table_ref[h : h + 1, :], (SUB, table_ref.shape[1]))
        rolled = pltpu.roll(rows, table_ref.shape[1] - (SUB - 1), 1, stride=1, stride_axis=0)
        strip_ref[h] = rolled[:, :span]


def strip_at(step, part, parts, length):
    begin = length - SUB * (step * parts + part + 1)
    return pl.ds(pl.multiple_of(begin, SUB), length)


def forward_kernel(
    qkv_ref, table_ref, seg_col_ref, seg_row_ref, out_ref, lse_ref, strip_ref, *, rows, heads
):
    step = pl.program_id(0)
    length = qkv_ref.shape[0]
    inner = heads * HD

    @pl.when(step == 0)
    def _():
        fill_strip(table_ref, strip_ref)

    here = pl.ds(pl.multiple_of(step * rows, rows), rows)
    same = seg_col_ref[here, :] == seg_row_ref[...]
    q_all = qkv_ref[here, :inner] * jnp.asarray(HD**-0.5, bf16)
    lane = lax.broadcasted_iota(jnp.int32, lse_ref.shape, 1)
    lse = jnp.zeros(lse_ref.shape, f32)
    outs = []
    parts = rows // SUB
    for h in range(heads):
        lo = h * HD
        keys = qkv_ref[:, inner + lo : inner + lo + HD]
        values = qkv_ref[:, 2 * inner + lo : 2 * inner + lo + HD]
        scores = mm(q_all[:, lo : lo + HD], keys, NT)
        bias = jnp.concatenate(
            [strip_ref[h, :, strip_at(step, u, parts, length)] for u in range(parts)], axis=0
        )
        scores = jnp.where(same, scores + bias, -1e9)
        top = jnp.max(scores, axis=1, keepdims=True)
        weights = jnp.exp(scores - top)
        total = jnp.sum(weights, axis=1, keepdims=True)
        outs.append(mm(weights.astype(bf16), values) / total)
        lse = jnp.where(lane == h, top + jnp.log(total), lse)
    out_ref[...] = jnp.concatenate(outs, axis=1).astype(bf16)
    lse_ref[...] = lse


def whole(shape):
    return pl.BlockSpec(shape, lambda *_: (0,) * len(shape))


def attend_forward(qkv, table, segments, heads):
    length = qkv.shape[0]
    rows = min(256, length)
    inner = heads * HD
    return pl.pallas_call(
        partial(forward_kernel, rows=rows, heads=heads),
        grid=(length // rows,),
        in_specs=[
            whole(qkv.shape),
            whole(table.shape),
            whole((length, 1)),
            whole((1, length)),
        ],
        out_specs=[
            pl.BlockSpec((rows, inner), lambda i: (i, 0)),
            pl.BlockSpec((rows, SUB), lambda i: (i, 0)),
        ],
        out_shape=[
            jax.ShapeDtypeStruct((length, inner), bf16),
            jax.ShapeDtypeStruct((length, SUB), f32),
        ],
        scratch_shapes=[pltpu.VMEM((heads, SUB, 2 * length - SUB), f32)],
        compiler_params=pltpu.CompilerParams(vmem_limit_bytes=40 * 1024 * 1024),
        cost_estimate=pl.CostEstimate(
            flops=4 * length * length * inner,
            bytes_accessed=10 * length * inner,
            transcendentals=length * length * heads,
        ),
        name="attend_forward",
    )(qkv, table, segments[:, None], segments[None, :])


def backward_kernel(
    qkv_ref,
    grad_ref,
    lse_ref,
    table_ref,
    seg_col_ref,
    seg_row_ref,
    out_ref,
    d_table_ref,
    strip_ref,
    d_strip_ref,
    d_keys_ref,
    d_values_ref,
    *,
    rows,
    heads,
):
    step = pl.program_id(0)
    length = qkv_ref.shape[0]
    inner = heads * HD

    @pl.when(step == 0)
    def _():
        fill_strip(table_ref, strip_ref)
        d_strip_ref[...] = jnp.zeros_like(d_strip_ref)
        d_keys_ref[...] = jnp.zeros_like(d_keys_ref)
        d_values_ref[...] = jnp.zeros_like(d_values_ref)

    here = pl.ds(pl.multiple_of(step * rows, rows), rows)
    same = seg_col_ref[here, :] == seg_row_ref[...]
    q_all = qkv_ref[here, :inner] * jnp.asarray(HD**-0.5, bf16)
    parts = rows // SUB
    d_queries = []
    for h in range(heads):
        lo = h * HD
        keys = qkv_ref[:, inner + lo : inner + lo + HD]
        values = qkv_ref[:, 2 * inner + lo : 2 * inner + lo + HD]
        grads = grad_ref[here, lo : lo + HD]
        queries = q_all[:, lo : lo + HD]
        bias = jnp.concatenate(
            [strip_ref[h, :, strip_at(step, u, parts, length)] for u in range(parts)], axis=0
        )
        scores = mm(queries, keys, NT) + bias - lse_ref[:, h : h + 1]
        probs = jnp.where(same, jnp.exp(jnp.where(same, scores, 0.0)), 0.0)
        d_values_ref[lo : lo + HD, :] += mm(grads, probs.astype(bf16), TN)
        d_probs = mm(grads, values, NT)
        pulled = probs * d_probs
        d_scores = pulled - probs * jnp.sum(pulled, axis=1, keepdims=True)
        for u in range(parts):
            at = strip_at(step, u, parts, length)
            d_strip_ref[h, :, at] += d_scores[u * SUB : (u + 1) * SUB]
        d_raw = d_scores.astype(bf16)
        d_queries.append(mm(d_raw, keys) * HD**-0.5)
        d_keys_ref[lo : lo + HD, :] += mm(queries, d_raw, TN)
    out_ref[here, :inner] = jnp.concatenate(d_queries, axis=1).astype(bf16)

    @pl.when(step == pl.num_programs(0) - 1)
    def _():
        for h in range(heads):
            lo = h * HD
            out_ref[:, inner + lo : inner + lo + HD] = d_keys_ref[lo : lo + HD, :].T.astype(bf16)
            out_ref[:, 2 * inner + lo : 2 * inner + lo + HD] = d_values_ref[
                lo : lo + HD, :
            ].T.astype(bf16)
            summed = jnp.concatenate([d_strip_ref[h], jnp.zeros((SUB, SUB), f32)], axis=1)
            count = SUB
            while count > 1:
                count //= 2
                summed = summed[count:] + pltpu.roll(summed[:count], count, 1)
            d_table_ref[h : h + 1, :] = summed


def attend_backward(qkv, d_head, lse, table, segments, heads):
    length = qkv.shape[0]
    rows = min(256, length)
    inner = heads * HD
    return pl.pallas_call(
        partial(backward_kernel, rows=rows, heads=heads),
        grid=(length // rows,),
        in_specs=[
            whole(qkv.shape),
            whole(d_head.shape),
            pl.BlockSpec((rows, SUB), lambda i: (i, 0)),
            whole(table.shape),
            whole((length, 1)),
            whole((1, length)),
        ],
        out_specs=[whole(qkv.shape), whole(table.shape)],
        out_shape=[
            jax.ShapeDtypeStruct(qkv.shape, bf16),
            jax.ShapeDtypeStruct(table.shape, f32),
        ],
        scratch_shapes=[
            pltpu.VMEM((heads, SUB, 2 * length - SUB), f32),
            pltpu.VMEM((heads, SUB, 2 * length - SUB), f32),
            pltpu.VMEM((inner, length), f32),
            pltpu.VMEM((inner, length), f32),
        ],
        compiler_params=pltpu.CompilerParams(vmem_limit_bytes=48 * 1024 * 1024),
        cost_estimate=pl.CostEstimate(
            flops=10 * length * length * inner,
            bytes_accessed=16 * length * inner,
            transcendentals=length * length * heads,
        ),
        name="attend_backward",
    )(qkv, d_head, lse, table, segments[:, None], segments[None, :])


def joined(block_ref, first):
    rows, cols = block_ref.shape[0], block_ref.shape[1]
    slots, half = block_ref.shape[3], block_ref.shape[4] // 2
    lo = 0 if first else half
    return jnp.concatenate(
        [
            block_ref[:, c, 0, :, lo : lo + half].reshape(rows * slots, half)
            for c in range(cols)
        ],
        axis=1,
    )


GELU_A = 0.7978845608028654
GELU_B = 0.044715


def gelu_pair(u):
    square = u * u
    bent = jnp.tanh(GELU_A * u * (1.0 + GELU_B * square))
    value = 0.5 * u * (1.0 + bent)
    slope = 0.5 * (1.0 + bent) + (0.5 * GELU_A) * u * (1.0 - bent * bent) * (
        1.0 + 3.0 * GELU_B * square
    )
    return value, slope


def expert_kernel(got_ref, up_ref, down_ref, back_ref, x_ref, g_ref, out_ref, grad_ref):
    step = pl.program_id(1)

    @pl.when(step == 0)
    def _():
        x_ref[...] = joined(got_ref, True)
        g_ref[...] = joined(got_ref, False)

    up, down = up_ref[0], down_ref[0]
    value, slope = gelu_pair(mm(x_ref[...], up, NT))
    out = mm(value.astype(bf16), down)
    d_pre = (mm(g_ref[...], down, NT) * slope).astype(bf16)
    grad = mm(d_pre, up)

    @pl.when(step == 0)
    def _():
        out_ref[...] = out
        grad_ref[...] = grad

    @pl.when(step > 0)
    def _():
        out_ref[...] += out
        grad_ref[...] += grad

    @pl.when(step == pl.num_programs(1) - 1)
    def _():
        rows, cols, _, slots, both = back_ref.shape
        half = both // 2
        for c in range(cols):
            for lo, source in ((0, out_ref), (half, grad_ref)):
                back_ref[:, c, 0, :, lo : lo + half] = (
                    source[:, c * half : (c + 1) * half].astype(bf16).reshape(rows, slots, half)
                )


def run_experts(got, w_up, w_down):
    rows, cols, experts, slots, both = got.shape
    hidden, width = w_up.shape[1:]
    tile = 512
    block = pl.BlockSpec((rows, cols, 1, slots, both), lambda e, f: (0, 0, e, 0, 0))
    weight = pl.BlockSpec((1, tile, width), lambda e, f: (e, f, 0))
    tokens = rows * slots
    return pl.pallas_call(
        expert_kernel,
        grid=(experts, hidden // tile),
        in_specs=[block, weight, weight],
        out_specs=block,
        out_shape=jax.ShapeDtypeStruct(got.shape, bf16),
        scratch_shapes=[
            pltpu.VMEM((tokens, width), bf16),
            pltpu.VMEM((tokens, width), bf16),
            pltpu.VMEM((tokens, width), f32),
            pltpu.VMEM((tokens, width), f32),
        ],
        compiler_params=pltpu.CompilerParams(vmem_limit_bytes=40 * 1024 * 1024),
        cost_estimate=pl.CostEstimate(
            flops=8 * experts * tokens * hidden * width,
            bytes_accessed=4 * experts * hidden * width,
            transcendentals=experts * tokens * hidden,
        ),
        name="experts",
    )(got, w_up, w_down)


def weight_kernel(at_ref, got_ref, up_ref, down_ref, d_up_ref, d_down_ref):
    step = pl.program_id(1)
    block = got_ref.at[0]
    x, g = joined(block, True), joined(block, False)
    value, slope = gelu_pair(mm(up_ref[0], x, NT))
    d_pre = (mm(down_ref[0], g, NT) * slope).astype(bf16)
    d_down = mm(value.astype(bf16), g)
    d_up = mm(d_pre, x)

    @pl.when(step == 0)
    def _():
        d_up_ref[0] = d_up
        d_down_ref[0] = d_down

    @pl.when(step > 0)
    def _():
        d_up_ref[0] += d_up
        d_down_ref[0] += d_down


def weight_grads(got_all, w_up, w_down, dp_at):
    parts, rows, cols, experts, slots, both = got_all.shape
    hidden, width = w_up.shape[1:]
    own = hidden // parts
    weight = pl.BlockSpec((1, own, width), lambda e, n, at: (e, at[0], 0))
    result = pl.BlockSpec((1, own, width), lambda e, n, at: (e, 0, 0))
    shape = jax.ShapeDtypeStruct((experts, own, width), f32)
    return pl.pallas_call(
        weight_kernel,
        grid_spec=pltpu.PrefetchScalarGridSpec(
            num_scalar_prefetch=1,
            grid=(experts, parts),
            in_specs=[
                pl.BlockSpec(
                    (1, rows, cols, 1, slots, both), lambda e, n, at: (n, 0, 0, e, 0, 0)
                ),
                weight,
                weight,
            ],
            out_specs=[result, result],
        ),
        out_shape=[shape, shape],
        compiler_params=pltpu.CompilerParams(vmem_limit_bytes=40 * 1024 * 1024),
        cost_estimate=pl.CostEstimate(
            flops=8 * experts * parts * rows * slots * own * width,
            bytes_accessed=12 * experts * own * width + 2 * got_all.size,
            transcendentals=experts * parts * rows * slots * own,
        ),
        name="weight_grads",
    )(dp_at[None], got_all, w_up, w_down)


def pairs_out(k):
    return [
        (r * 2 + c, ((2 * (r % 2) + c) ^ k) * 2 + r // 2) for r in range(4) for c in range(2)
    ]


def pairs_home(k):
    return [(b, a) for a, b in pairs_out(k)]


def swap_col(array):
    return lax.ppermute(array, "col", [(0, 1), (1, 0)])


def total_over(array, axis):
    count = lax.axis_size(axis)
    stride = 1
    while stride < count:
        array = array + lax.ppermute(array, axis, [(i, i ^ stride) for i in range(count)])
        stride *= 2
    return array


def shards(
    layer_in,
    w_qkv,
    w_proj,
    rel_bias,
    rel_bucket,
    segment_ids,
    gain_attn,
    gain_ffn,
    w_router,
    routes,
    w_up,
    w_down,
    d_layer,
):
    row_count = lax.axis_size("row")
    col_count = lax.axis_size("col")
    dp_at = lax.axis_index("dp")
    row_at = lax.axis_index("row")
    col_at = lax.axis_index("col")
    tok_dev, width = layer_in.shape
    slot_count = max(2, tok_dev // 8)
    half_width = width // col_count
    quarter = tok_dev // 2
    length = segment_ids.shape[1]
    inner = w_qkv.shape[2]
    heads_dev = inner // HD
    experts_all = EXP_DEV * row_count * col_count
    home = 2 * (row_at % 2) + col_at
    is_first = col_at == 0

    def both_halves(mine, other, axis):
        return jnp.where(
            is_first,
            jnp.concatenate([mine, other], axis),
            jnp.concatenate([other, mine], axis),
        )

    def my_half(array, axis):
        size = array.shape[axis] // 2
        return lax.dynamic_slice_in_dim(array, col_at * size, size, axis)

    def other_half(array, axis):
        size = array.shape[axis] // 2
        return lax.dynamic_slice_in_dim(array, (1 - col_at) * size, size, axis)

    def in_order(chunks, at):
        stacked = jnp.stack(chunks)
        return jnp.concatenate(
            [lax.dynamic_index_in_dim(stacked, i ^ at, 0, False) for i in range(len(chunks))], 0
        )

    own_tokens = my_half(layer_in, 0)
    tokens_seq = in_order(
        [lax.ppermute(own_tokens, group, pairs_out(k)) for k in range(row_count)], row_at
    ).astype(f32)
    w_pair = both_halves(w_qkv, swap_col(w_qkv), 1)
    w_all = jnp.concatenate([w_pair[0], w_pair[1], w_pair[2]], axis=1)
    scale_seq = lax.rsqrt(jnp.mean(tokens_seq * tokens_seq, axis=-1, keepdims=True) + epsilon)
    normed = (tokens_seq * scale_seq * gain_attn).astype(bf16)
    qkv = mm(normed, w_all).astype(bf16)

    buckets = (rel_bucket[:, None] == jnp.arange(NB, dtype=jnp.int32)[None, :]).astype(f32)
    bias_rows = lax.dynamic_slice_in_dim(rel_bias, row_at * heads_dev, heads_dev, 0)
    bias_table = jnp.einsum("hb,ob->ho", bias_rows, buckets, precision=highest)
    table = jnp.pad(bias_table, ((0, 0), (0, 1)))
    segments = segment_ids[0]

    w_proj_late, qkv = lax.optimization_barrier((w_proj, qkv))
    proj_half = lax.all_gather(w_proj_late, "row", axis=0, tiled=False)
    proj_half = jnp.stack(
        [
            lax.dynamic_index_in_dim(proj_half, home ^ k, 0, False)
            for k in range(row_count)
        ]
    )
    proj_swapped = swap_col(proj_half)
    proj_other = jnp.stack([proj_swapped[k ^ 1] for k in range(row_count)])
    proj_all = both_halves(proj_half, proj_other, 2).reshape(row_count * inner, width)
    grads_in = both_halves(d_layer, swap_col(d_layer), 1).astype(f32)

    head_out, lse = attend_forward(qkv, table, segments, heads_dev)

    head_blocks = head_out.reshape(2, tok_dev, inner)
    heads = jnp.concatenate(
        [
            lax.ppermute(
                lax.dynamic_index_in_dim(head_blocks, (row_at ^ k) // 2, 0, False),
                group,
                pairs_home(k),
            )
            for k in range(row_count)
        ],
        axis=1,
    )
    middle = layer_in.astype(f32) + mm(heads, proj_all)
    scale_ffn = lax.rsqrt(jnp.mean(middle * middle, axis=-1, keepdims=True) + epsilon)
    hidden = middle * scale_ffn * gain_ffn
    gate_probs = jax.nn.softmax(jnp.dot(hidden, w_router, precision=highest), axis=-1)
    routed = routes[:, 0]
    chosen = routed[:, None] == jnp.arange(experts_all, dtype=jnp.int32)[None, :]
    gating = jnp.sum(jnp.where(chosen, gate_probs, 0.0), axis=-1, keepdims=True)
    counts = jnp.cumsum(chosen.astype(jnp.int32), axis=0)
    slot_index = jnp.sum(jnp.where(chosen, counts, 0), axis=-1) - 1
    placed = routed * slot_count + slot_index
    slots_all = experts_all * slot_count
    placing = (jnp.arange(slots_all, dtype=jnp.int32)[:, None] == placed[None, :]).astype(bf16)

    payload = jnp.concatenate(
        [
            my_half(hidden, 1).astype(bf16),
            (gating * d_layer.astype(f32)).astype(bf16),
        ],
        axis=1,
    )
    send = mm(placing, payload).astype(bf16)
    send = send.reshape(row_count * col_count, EXP_DEV, slot_count, width)
    got = lax.all_to_all(send, group, split_axis=0, concat_axis=0, tiled=True)
    got_all = lax.all_gather(got, "dp", axis=0, tiled=False)
    block_shape = (row_count, col_count, EXP_DEV, slot_count, width)
    back = run_experts(got.reshape(block_shape), w_up, w_down)
    back = lax.all_to_all(
        back.reshape(send.shape), group, split_axis=0, concat_axis=0, tiled=True
    )
    mine = mm(placing, back.reshape(slots_all, width), TN).astype(bf16)
    other = swap_col(mine)
    expert_out = both_halves(mine[:, :half_width], other[:, :half_width], 1).astype(f32)
    d_hidden = both_halves(mine[:, half_width:], other[:, half_width:], 1).astype(f32)

    layer_out = my_half(middle, 1) + gating * mine[:, :half_width].astype(f32)
    d_gating = jnp.sum(grads_in * expert_out, axis=-1, keepdims=True)
    d_logits = d_gating * gate_probs * (chosen.astype(f32) - gating)
    d_hidden = d_hidden + jnp.einsum("tn,dn->td", d_logits, w_router, precision=highest)
    d_router = 0.5 * jnp.einsum("tn,td->nd", d_logits, hidden, precision=highest)
    d_gain_ffn = 0.5 * jnp.sum(middle * scale_ffn * d_hidden, axis=0)
    scaled_ffn = d_hidden * gain_ffn
    d_middle = (
        grads_in
        + scale_ffn * scaled_ffn
        - middle * scale_ffn**3 * jnp.mean(scaled_ffn * middle, axis=-1, keepdims=True)
    )
    d_attn = d_middle.astype(bf16)
    d_heads = mm(my_half(d_attn, 0), proj_all, NT).astype(bf16)
    d_head = in_order(
        [
            lax.ppermute(d_heads[:, k * inner : (k + 1) * inner], group, pairs_out(k))
            for k in range(row_count)
        ],
        row_at,
    )
    d_proj = mm(heads, my_half(d_attn, 1), TN).astype(bf16).reshape(row_count, inner, half_width)
    d_proj = in_order([d_proj[k] for k in range(row_count)], home)
    d_proj = lax.psum_scatter(d_proj, "row", scatter_dimension=0, tiled=True)
    d_proj = lax.psum(d_proj, "dp").astype(f32)

    d_qkv, d_table = attend_backward(qkv, d_head, lse, table, segments, heads_dev)

    part_normed = mm(d_qkv, w_all, NT).astype(bf16).reshape(row_count, quarter, width)
    d_normed = sum(
        lax.ppermute(
            lax.dynamic_index_in_dim(part_normed, row_at ^ k, 0, False), group, pairs_home(k)
        ).astype(f32)
        for k in range(row_count)
    )

    d_w = mm(normed, d_qkv, TN)
    gain_part = jnp.sum(d_w * w_all.astype(f32), axis=1) / gain_attn
    d_w = my_half(d_w, 0) + swap_col(other_half(d_w, 0).astype(bf16)).astype(f32)
    d_w = lax.psum(d_w.astype(bf16), "dp").astype(f32)
    d_w_qkv = d_w.reshape(half_width, 3, inner).transpose(1, 0, 2)

    d_rel_part = jnp.einsum("ho,ob->hb", d_table[:, : 2 * length - 1], buckets, precision=highest)
    rel_whole = lax.dynamic_update_slice_in_dim(
        jnp.zeros((H, NB), f32), d_rel_part, row_at * heads_dev, 0
    )
    rel_row = jnp.pad(rel_whole.reshape(1, H * NB), ((0, 0), (0, width - H * NB)))
    small = jnp.concatenate([d_router, d_gain_ffn[None], gain_part[None], rel_row], axis=0)
    small = total_over(total_over(total_over(small, "col"), "row"), "dp")
    d_w_router = small[:experts_all].T
    d_gain_ffn = small[experts_all]
    d_gain_attn = small[experts_all + 1]
    d_rel_bias = small[experts_all + 2, : H * NB].reshape(H, NB)

    own = own_tokens.astype(f32)
    scale_own = lax.rsqrt(jnp.mean(own * own, axis=-1, keepdims=True) + epsilon)
    scaled_attn = d_normed * gain_attn
    d_own = (
        my_half(d_middle, 0)
        + scale_own * scaled_attn
        - own * scale_own**3 * jnp.mean(scaled_attn * own, axis=-1, keepdims=True)
    )
    d_layer_in = both_halves(my_half(d_own, 1), swap_col(other_half(d_own, 1)), 0)

    d_up, d_down = weight_grads(
        got_all.reshape((got_all.shape[0],) + block_shape), w_up, w_down, dp_at
    )
    return (
        layer_out,
        d_layer_in,
        d_w_qkv,
        d_proj,
        d_rel_bias,
        d_gain_attn,
        d_gain_ffn,
        d_w_router,
        d_up,
        d_down,
    )


def solution(mesh):
    placed = (
        P(("dp", "row"), None),
        P(None, "col", "row"),
        P("row", "col"),
        P(),
        P(),
        P(("dp", "col"), None),
        P(),
        P(),
        P(),
        P(("dp", "row"), None),
        P(("row", "col"), None, None),
        P(("row", "col"), None, None),
        P(("dp", "row"), "col"),
    )
    return jax.shard_map(
        shards,
        mesh=mesh,
        in_specs=placed,
        out_specs=(
            P(("dp", "row"), "col"),
            P(("dp", "row"), "col"),
            P(None, "col", "row"),
            P("row", "col"),
            P(),
            P(),
            P(),
            P(),
            P(("row", "col"), "dp", None),
            P(("row", "col"), "dp", None),
        ),
        check_vma=False,
    )
```

```python
from functools import partial

import jax
import jax.numpy as jnp
from jax import lax
from jax.experimental import pallas as pl
from jax.experimental.pallas import tpu as pltpu
from jax.sharding import PartitionSpec as P

H = 12
HD = 64
NB = 32
EXP_DEV = 2
SUB = 128

epsilon = 1e-06
highest = lax.Precision.HIGHEST
f32 = jnp.float32
bf16 = jnp.bfloat16
group = ("row", "col")

NT = (((1,), (1,)), ((), ()))
NN = (((1,), (0,)), ((), ()))
TN = (((0,), (0,)), ((), ()))


def mm(a, b, dims=NN):
    return lax.dot_general(a, b, dims, preferred_element_type=f32)


def fill_strip(table_ref, strip_ref):
    heads, _, span = strip_ref.shape
    for h in range(heads):
        rows = jnp.broadcast_to(table_ref[h : h + 1, :], (SUB, table_ref.shape[1]))
        rolled = pltpu.roll(rows, table_ref.shape[1] - (SUB - 1), 1, stride=1, stride_axis=0)
        strip_ref[h] = rolled[:, :span]


def strip_at(step, part, parts, length):
    begin = length - SUB * (step * parts + part + 1)
    return pl.ds(pl.multiple_of(begin, SUB), length)


def forward_kernel(
    qkv_ref, table_ref, seg_col_ref, seg_row_ref, out_ref, lse_ref, strip_ref, *, rows, heads
):
    step = pl.program_id(0)
    length = qkv_ref.shape[0]
    inner = heads * HD

    @pl.when(step == 0)
    def _():
        fill_strip(table_ref, strip_ref)

    here = pl.ds(pl.multiple_of(step * rows, rows), rows)
    same = seg_col_ref[here, :] == seg_row_ref[...]
    q_all = qkv_ref[here, :inner] * jnp.asarray(HD**-0.5, bf16)
    lane = lax.broadcasted_iota(jnp.int32, lse_ref.shape, 1)
    lse = jnp.zeros(lse_ref.shape, f32)
    outs = []
    parts = rows // SUB
    for h in range(heads):
        lo = h * HD
        keys = qkv_ref[:, inner + lo : inner + lo + HD]
        values = qkv_ref[:, 2 * inner + lo : 2 * inner + lo + HD]
        scores = mm(q_all[:, lo : lo + HD], keys, NT)
        bias = jnp.concatenate(
            [strip_ref[h, :, strip_at(step, u, parts, length)] for u in range(parts)], axis=0
        )
        scores = jnp.where(same, scores + bias, -1e9)
        top = jnp.max(scores, axis=1, keepdims=True)
        weights = jnp.exp(scores - top)
        total = jnp.sum(weights, axis=1, keepdims=True)
        outs.append(mm(weights.astype(bf16), values) / total)
        lse = jnp.where(lane == h, top + jnp.log(total), lse)
    out_ref[...] = jnp.concatenate(outs, axis=1).astype(bf16)
    lse_ref[...] = lse


def whole(shape):
    return pl.BlockSpec(shape, lambda *_: (0,) * len(shape))


def attend_forward(qkv, table, segments, heads):
    length = qkv.shape[0]
    rows = min(256, length)
    inner = heads * HD
    return pl.pallas_call(
        partial(forward_kernel, rows=rows, heads=heads),
        grid=(length // rows,),
        in_specs=[
            whole(qkv.shape),
            whole(table.shape),
            whole((length, 1)),
            whole((1, length)),
        ],
        out_specs=[
            pl.BlockSpec((rows, inner), lambda i: (i, 0)),
            pl.BlockSpec((rows, SUB), lambda i: (i, 0)),
        ],
        out_shape=[
            jax.ShapeDtypeStruct((length, inner), bf16),
            jax.ShapeDtypeStruct((length, SUB), f32),
        ],
        scratch_shapes=[pltpu.VMEM((heads, SUB, 2 * length - SUB), f32)],
        compiler_params=pltpu.CompilerParams(vmem_limit_bytes=40 * 1024 * 1024),
        cost_estimate=pl.CostEstimate(
            flops=4 * length * length * inner,
            bytes_accessed=10 * length * inner,
            transcendentals=length * length * heads,
        ),
        name="attend_forward",
    )(qkv, table, segments[:, None], segments[None, :])


def backward_kernel(
    qkv_ref,
    grad_ref,
    lse_ref,
    table_ref,
    seg_col_ref,
    seg_row_ref,
    out_ref,
    d_table_ref,
    strip_ref,
    d_strip_ref,
    d_keys_ref,
    d_values_ref,
    *,
    rows,
    heads,
):
    step = pl.program_id(0)
    length = qkv_ref.shape[0]
    inner = heads * HD

    @pl.when(step == 0)
    def _():
        fill_strip(table_ref, strip_ref)
        d_strip_ref[...] = jnp.zeros_like(d_strip_ref)
        d_keys_ref[...] = jnp.zeros_like(d_keys_ref)
        d_values_ref[...] = jnp.zeros_like(d_values_ref)

    here = pl.ds(pl.multiple_of(step * rows, rows), rows)
    same = seg_col_ref[here, :] == seg_row_ref[...]
    q_all = qkv_ref[here, :inner] * jnp.asarray(HD**-0.5, bf16)
    parts = rows // SUB
    d_queries = []
    for h in range(heads):
        lo = h * HD
        keys = qkv_ref[:, inner + lo : inner + lo + HD]
        values = qkv_ref[:, 2 * inner + lo : 2 * inner + lo + HD]
        grads = grad_ref[here, lo : lo + HD]
        queries = q_all[:, lo : lo + HD]
        bias = jnp.concatenate(
            [strip_ref[h, :, strip_at(step, u, parts, length)] for u in range(parts)], axis=0
        )
        scores = mm(queries, keys, NT) + bias - lse_ref[:, h : h + 1]
        probs = jnp.where(same, jnp.exp(jnp.where(same, scores, 0.0)), 0.0)
        d_values_ref[lo : lo + HD, :] += mm(grads, probs.astype(bf16), TN)
        d_probs = mm(grads, values, NT)
        pulled = probs * d_probs
        d_scores = pulled - probs * jnp.sum(pulled, axis=1, keepdims=True)
        for u in range(parts):
            at = strip_at(step, u, parts, length)
            d_strip_ref[h, :, at] += d_scores[u * SUB : (u + 1) * SUB]
        d_raw = d_scores.astype(bf16)
        d_queries.append(mm(d_raw, keys) * HD**-0.5)
        d_keys_ref[lo : lo + HD, :] += mm(queries, d_raw, TN)
    out_ref[here, :inner] = jnp.concatenate(d_queries, axis=1).astype(bf16)

    @pl.when(step == pl.num_programs(0) - 1)
    def _():
        for h in range(heads):
            lo = h * HD
            out_ref[:, inner + lo : inner + lo + HD] = d_keys_ref[lo : lo + HD, :].T.astype(bf16)
            out_ref[:, 2 * inner + lo : 2 * inner + lo + HD] = d_values_ref[
                lo : lo + HD, :
            ].T.astype(bf16)
            summed = jnp.concatenate([d_strip_ref[h], jnp.zeros((SUB, SUB), f32)], axis=1)
            count = SUB
            while count > 1:
                count //= 2
                summed = summed[count:] + pltpu.roll(summed[:count], count, 1)
            d_table_ref[h : h + 1, :] = summed


def attend_backward(qkv, d_head, lse, table, segments, heads):
    length = qkv.shape[0]
    rows = min(256, length)
    inner = heads * HD
    return pl.pallas_call(
        partial(backward_kernel, rows=rows, heads=heads),
        grid=(length // rows,),
        in_specs=[
            whole(qkv.shape),
            whole(d_head.shape),
            pl.BlockSpec((rows, SUB), lambda i: (i, 0)),
            whole(table.shape),
            whole((length, 1)),
            whole((1, length)),
        ],
        out_specs=[whole(qkv.shape), whole(table.shape)],
        out_shape=[
            jax.ShapeDtypeStruct(qkv.shape, bf16),
            jax.ShapeDtypeStruct(table.shape, f32),
        ],
        scratch_shapes=[
            pltpu.VMEM((heads, SUB, 2 * length - SUB), f32),
            pltpu.VMEM((heads, SUB, 2 * length - SUB), f32),
            pltpu.VMEM((inner, length), f32),
            pltpu.VMEM((inner, length), f32),
        ],
        compiler_params=pltpu.CompilerParams(vmem_limit_bytes=48 * 1024 * 1024),
        cost_estimate=pl.CostEstimate(
            flops=10 * length * length * inner,
            bytes_accessed=16 * length * inner,
            transcendentals=length * length * heads,
        ),
        name="attend_backward",
    )(qkv, d_head, lse, table, segments[:, None], segments[None, :])


def joined(block_ref):
    rows, cols, _, slots, half = block_ref.shape
    return jnp.concatenate(
        [block_ref[:, c, 0].reshape(rows * slots, half) for c in range(cols)], axis=1
    )


GELU_A = 0.7978845608028654
GELU_B = 0.044715


def gelu_pair(u):
    square = u * u
    factor = 0.5 * jnp.tanh(u * (GELU_A + (GELU_A * GELU_B) * square)) + 0.5
    value = u * factor
    slope = factor + value * (1.0 - factor) * (2 * GELU_A + (6 * GELU_A * GELU_B) * square)
    return value, slope


def router_probs(x, router_ref):
    weights = router_ref[...]
    high = weights.astype(bf16)
    low = (weights - high.astype(f32)).astype(bf16)
    logits = mm(x, high) + mm(x, low)
    exped = jnp.exp(logits - jnp.max(logits, axis=1, keepdims=True))
    return exped / jnp.sum(exped, axis=1, keepdims=True)


def gate(probs, expert):
    picked = lax.broadcasted_iota(jnp.int32, probs.shape, 1) == expert
    return picked, jnp.sum(jnp.where(picked, probs, 0.0), axis=1, keepdims=True)


def expert_kernel(
    first_ref,
    x_in_ref,
    g_in_ref,
    router_ref,
    up_ref,
    down_ref,
    out_ref,
    grad_ref,
    d_router_ref,
    x_ref,
    g_ref,
    probs_ref,
    out_acc_ref,
    grad_acc_ref,
):
    expert = pl.program_id(0)
    step = pl.program_id(1)

    @pl.when(step == 0)
    def _():
        x = joined(x_in_ref)
        probs = router_probs(x, router_ref)
        _, gating = gate(probs, first_ref[0] + expert)
        x_ref[...] = x
        g_ref[...] = (gating * joined(g_in_ref).astype(f32)).astype(bf16)
        probs_ref[...] = probs
        out_acc_ref[...] = jnp.zeros_like(out_acc_ref)
        grad_acc_ref[...] = jnp.zeros_like(grad_acc_ref)

    parts = 3
    tile = up_ref.shape[1] // parts
    activated, d_pre = [], []
    for i in range(parts):
        here = slice(i * tile, (i + 1) * tile)
        value, slope = gelu_pair(mm(x_ref[...], up_ref[0, here], NT))
        activated.append(value.astype(bf16))
        d_pre.append((mm(g_ref[...], down_ref[0, here], NT) * slope).astype(bf16))
    out_acc_ref[...] += mm(jnp.concatenate(activated, axis=1), down_ref[0])
    grad_acc_ref[...] += mm(jnp.concatenate(d_pre, axis=1), up_ref[0])

    @pl.when(step == pl.num_programs(1) - 1)
    def _():
        out = out_acc_ref[...]
        probs = probs_ref[...]
        picked, gating = gate(probs, first_ref[0] + expert)
        d_gating = jnp.sum(joined(g_in_ref).astype(f32) * out, axis=1, keepdims=True)
        d_logits = d_gating * probs * (picked.astype(f32) - gating)
        grad = grad_acc_ref[...] + lax.dot_general(
            d_logits, router_ref[...], NT, precision=highest, preferred_element_type=f32
        )
        d_router = lax.dot_general(
            d_logits,
            x_ref[...].astype(f32),
            TN,
            precision=highest,
            preferred_element_type=f32,
        )
        rows, cols, _, slots, half = out_ref.shape
        for c in range(cols):
            for target, source in ((out_ref, out), (grad_ref, grad)):
                target[:, c, 0] = (
                    source[:, c * half : (c + 1) * half].astype(bf16).reshape(rows, slots, half)
                )

        @pl.when(expert == 0)
        def _():
            d_router_ref[...] = d_router

        @pl.when(expert > 0)
        def _():
            d_router_ref[...] += d_router


def run_experts(got_x, got_g, w_router, w_up, w_down, first):
    rows, cols, experts, slots, half = got_x.shape
    hidden, width = w_up.shape[1:]
    tile = 768
    block = pl.BlockSpec((rows, cols, 1, slots, half), lambda e, f, at: (0, 0, e, 0, 0))
    weight = pl.BlockSpec((1, tile, width), lambda e, f, at: (e, f, 0))
    tokens = rows * slots
    shape = jax.ShapeDtypeStruct(got_x.shape, bf16)
    router_shape = (w_router.shape[1], width)
    return pl.pallas_call(
        expert_kernel,
        grid_spec=pltpu.PrefetchScalarGridSpec(
            num_scalar_prefetch=1,
            grid=(experts, hidden // tile),
            in_specs=[block, block, whole(w_router.shape), weight, weight],
            out_specs=[block, block, whole(router_shape)],
            scratch_shapes=[
                pltpu.VMEM((tokens, width), bf16),
                pltpu.VMEM((tokens, width), bf16),
                pltpu.VMEM((tokens, w_router.shape[1]), f32),
                pltpu.VMEM((tokens, width), f32),
                pltpu.VMEM((tokens, width), f32),
            ],
        ),
        out_shape=[shape, shape, jax.ShapeDtypeStruct(router_shape, f32)],
        compiler_params=pltpu.CompilerParams(vmem_limit_bytes=56 * 1024 * 1024),
        cost_estimate=pl.CostEstimate(
            flops=8 * experts * tokens * hidden * width,
            bytes_accessed=4 * experts * hidden * width,
            transcendentals=experts * tokens * hidden,
        ),
        name="experts",
    )(first[None], got_x, got_g, w_router, w_up, w_down)


def weight_kernel(
    at_ref, x_in_ref, g_in_ref, router_ref, up_ref, down_ref, *refs, expert
):
    d_up_ref, d_down_ref = refs[-2:]
    step = pl.program_id(0)
    parts = x_in_ref.shape[0]
    x = jnp.concatenate([joined(x_in_ref.at[i]) for i in range(parts)], axis=0)
    g = jnp.concatenate([joined(g_in_ref.at[i]) for i in range(parts)], axis=0)
    _, gating = gate(router_probs(x, router_ref), at_ref[1] + expert)
    g = (gating * g.astype(f32)).astype(bf16)
    own = up_ref.shape[1]
    tile = own // 3 if own % 768 == 0 else own
    for i in range(own // tile):
        here = slice(i * tile, (i + 1) * tile)
        value, slope = gelu_pair(mm(up_ref[0, here], x, NT))
        d_pre = (mm(down_ref[0, here], g, NT) * slope).astype(bf16)
        d_down = mm(value.astype(bf16), g)
        d_up = mm(d_pre, x)

        @pl.when(step == 0)
        def _():
            d_up_ref[0, here] = d_up
            d_down_ref[0, here] = d_down

        @pl.when(step > 0)
        def _():
            d_up_ref[0, here] += d_up
            d_down_ref[0, here] += d_down


def weight_grads(expert, all_x, all_g, w_router, w_up, w_down, at, earlier):
    parts, rows, cols, experts, slots, half = all_x.shape
    hidden, width = w_up.shape[1:]
    own = hidden // parts
    each = min(4, parts)
    block = pl.BlockSpec(
        (each, rows, cols, 1, slots, half), lambda n, at: (n, 0, 0, expert, 0, 0)
    )
    weight = pl.BlockSpec((1, own, width), lambda n, at: (expert, at[0], 0))
    result = pl.BlockSpec((1, own, width), lambda n, at: (expert, 0, 0))
    shape = jax.ShapeDtypeStruct((experts, own, width), f32)
    return pl.pallas_call(
        partial(weight_kernel, expert=expert),
        grid_spec=pltpu.PrefetchScalarGridSpec(
            num_scalar_prefetch=1,
            grid=(parts // each,),
            in_specs=[block, block, whole(w_router.shape), weight, weight]
            + [pl.BlockSpec(memory_space=pl.ANY)] * len(earlier),
            out_specs=[result, result],
        ),
        out_shape=[shape, shape],
        input_output_aliases={6 + i: i for i in range(len(earlier))},
        compiler_params=pltpu.CompilerParams(vmem_limit_bytes=56 * 1024 * 1024),
        cost_estimate=pl.CostEstimate(
            flops=8 * parts * rows * slots * own * width,
            bytes_accessed=12 * own * width + 2 * all_x.size,
            transcendentals=parts * rows * slots * own,
        ),
        name="weight_grads",
    )(at, all_x, all_g, w_router, w_up, w_down, *earlier)


def pairs_out(k):
    return [
        (r * 2 + c, ((2 * (r % 2) + c) ^ k) * 2 + r // 2) for r in range(4) for c in range(2)
    ]


def pairs_home(k):
    return [(b, a) for a, b in pairs_out(k)]


def swap_col(array):
    return lax.ppermute(array, "col", [(0, 1), (1, 0)])


def shift(array, axis, bits):
    if bits == 0:
        return array
    count = lax.axis_size(axis)
    return lax.ppermute(array, axis, [(i, i ^ bits) for i in range(count)])


def total_over(array, axis):
    count = lax.axis_size(axis)
    stride = 1
    while stride < count:
        if 4 * stride <= count:
            near, far, last = (shift(array, axis, stride * i) for i in (1, 2, 3))
            array = (array + near) + (far + last)
            stride *= 4
        else:
            array = array + shift(array, axis, stride)
            stride *= 2
    return array


def shards(
    layer_in,
    w_qkv,
    w_proj,
    rel_bias,
    rel_bucket,
    segment_ids,
    gain_attn,
    gain_ffn,
    w_router,
    routes,
    w_up,
    w_down,
    d_layer,
):
    row_count = lax.axis_size("row")
    col_count = lax.axis_size("col")
    dp_count = lax.axis_size("dp")
    dp_at = lax.axis_index("dp")
    row_at = lax.axis_index("row")
    col_at = lax.axis_index("col")
    tok_dev, width = layer_in.shape
    slot_count = max(2, tok_dev // 8)
    half_width = width // col_count
    quarter = tok_dev // 2
    length = segment_ids.shape[1]
    inner = w_qkv.shape[2]
    heads_dev = inner // HD
    experts_all = EXP_DEV * row_count * col_count
    home = 2 * (row_at % 2) + col_at
    is_first = col_at == 0

    def both_halves(mine, other, axis):
        return jnp.where(
            is_first,
            jnp.concatenate([mine, other], axis),
            jnp.concatenate([other, mine], axis),
        )

    def my_half(array, axis):
        size = array.shape[axis] // 2
        return lax.dynamic_slice_in_dim(array, col_at * size, size, axis)

    def other_half(array, axis):
        size = array.shape[axis] // 2
        return lax.dynamic_slice_in_dim(array, (1 - col_at) * size, size, axis)

    def in_order(chunks, at):
        stacked = jnp.stack(chunks)
        return jnp.concatenate(
            [lax.dynamic_index_in_dim(stacked, i ^ at, 0, False) for i in range(len(chunks))], 0
        )

    own_tokens = my_half(layer_in, 0)
    tokens_seq = in_order(
        [lax.ppermute(own_tokens, group, pairs_out(k)) for k in range(row_count)], row_at
    ).astype(f32)
    w_pair = both_halves(w_qkv, swap_col(w_qkv), 1)
    w_all = jnp.concatenate([w_pair[0], w_pair[1], w_pair[2]], axis=1)
    scale_seq = lax.rsqrt(jnp.mean(tokens_seq * tokens_seq, axis=-1, keepdims=True) + epsilon)
    normed = (tokens_seq * scale_seq * gain_attn).astype(bf16)
    qkv = mm(normed, w_all).astype(bf16)

    buckets = (rel_bucket[:, None] == jnp.arange(NB, dtype=jnp.int32)[None, :]).astype(f32)
    bias_rows = lax.dynamic_slice_in_dim(rel_bias, row_at * heads_dev, heads_dev, 0)
    bias_table = jnp.einsum("hb,ob->ho", bias_rows, buckets, precision=highest)
    table = jnp.pad(bias_table, ((0, 0), (0, 1)))
    segments = segment_ids[0]

    routed = routes[:, 0]
    chosen = routed[:, None] == jnp.arange(experts_all, dtype=jnp.int32)[None, :]
    counts = jnp.cumsum(chosen.astype(jnp.int32), axis=0)
    slot_index = jnp.sum(jnp.where(chosen, counts, 0), axis=-1) - 1
    placed = routed * slot_count + slot_index
    slots_all = experts_all * slot_count
    placing = (jnp.arange(slots_all, dtype=jnp.int32)[:, None] == placed[None, :]).astype(bf16)
    first = (row_at * col_count + col_at) * EXP_DEV
    send_shape = (row_count * col_count, EXP_DEV, slot_count, half_width)
    block_shape = (row_count, col_count, EXP_DEV, slot_count, half_width)

    def all_to_all(array):
        return lax.all_to_all(array, group, split_axis=0, concat_axis=0, tiled=True)

    def for_row(array, j):
        return lax.dynamic_index_in_dim(array, row_at ^ j, 0, False)

    def placed_slots(array):
        return mm(placing, array).astype(bf16).reshape(send_shape)

    def placed_back(array):
        return mm(placing, array.reshape(slots_all, half_width), TN).astype(bf16)

    w_proj_late, d_layer_late, qkv = lax.optimization_barrier((w_proj, d_layer, qkv))
    slots_dev = EXP_DEV * slot_count
    g_slots = placed_slots(d_layer_late).reshape(row_count, col_count * slots_dev, half_width)
    by_row = [
        shift(jnp.concatenate([w_proj_late, for_row(g_slots, j)], axis=0), "row", j)
        for j in range(row_count)
    ]
    head_out, lse = attend_forward(qkv, table, segments, heads_dev)
    by_row, head_out = lax.optimization_barrier((by_row, head_out))
    by_row = jnp.stack(by_row)
    proj_half = jnp.concatenate(
        [
            lax.dynamic_index_in_dim(by_row[:, :inner], row_at ^ home ^ k, 0, False)
            for k in range(row_count)
        ],
        axis=0,
    )
    g_slots = by_row[:, inner:].reshape(row_count, col_count, slots_dev, half_width)
    g_kept = lax.dynamic_index_in_dim(g_slots, col_at, 1, False)
    g_given = lax.dynamic_index_in_dim(g_slots, 1 - col_at, 1, False)
    swapped = swap_col(
        jnp.concatenate([proj_half, g_given.reshape(-1, half_width), d_layer_late], axis=0)
    )
    proj_other = swapped[: row_count * inner].reshape(row_count, inner, half_width)
    proj_other = jnp.concatenate([proj_other[k ^ 1] for k in range(row_count)], axis=0)
    proj_all = both_halves(proj_half, proj_other, 1)
    g_other = swapped[row_count * inner : -tok_dev].reshape(g_kept.shape)
    got_g = both_halves(g_kept[:, None], g_other[:, None], 1)
    got_g = in_order([got_g[j] for j in range(row_count)], row_at).reshape(send_shape)
    all_g = lax.all_gather(got_g, "dp", axis=0, tiled=False)
    grads_in = both_halves(d_layer_late, swapped[-tok_dev:], 1).astype(f32)

    head_blocks = head_out.reshape(2, tok_dev, inner)
    heads = jnp.concatenate(
        [
            lax.ppermute(
                lax.dynamic_index_in_dim(head_blocks, (row_at ^ k) // 2, 0, False),
                group,
                pairs_home(k),
            )
            for k in range(row_count)
        ],
        axis=1,
    )
    middle = layer_in.astype(f32) + mm(heads, proj_all)
    scale_ffn = lax.rsqrt(jnp.mean(middle * middle, axis=-1, keepdims=True) + epsilon)
    hidden = middle * scale_ffn * gain_ffn
    got_x = all_to_all(placed_slots(my_half(hidden, 1).astype(bf16)))
    all_x = lax.all_gather(got_x, "dp", axis=0, tiled=False)
    out_slots, grad_slots, d_router = run_experts(
        got_x.reshape(block_shape), got_g.reshape(block_shape), w_router, w_up, w_down, first
    )
    mine = placed_back(all_to_all(grad_slots.reshape(send_shape)))
    d_hidden = both_halves(mine, swap_col(mine), 1).astype(f32)
    d_gain_ffn = 0.5 * jnp.sum(middle * scale_ffn * d_hidden, axis=0)
    scaled_ffn = d_hidden * gain_ffn
    d_middle = (
        grads_in
        + scale_ffn * scaled_ffn
        - middle * scale_ffn**3 * jnp.mean(scaled_ffn * middle, axis=-1, keepdims=True)
    )
    d_attn = d_middle.astype(bf16)
    d_heads = mm(my_half(d_attn, 0), proj_all, NT).astype(bf16)
    d_head = in_order(
        [
            lax.ppermute(d_heads[:, k * inner : (k + 1) * inner], group, pairs_out(k))
            for k in range(row_count)
        ],
        row_at,
    )

    hidden_late, d_attn_late, out_late, d_heads = lax.optimization_barrier(
        (hidden, d_attn, out_slots, d_heads)
    )
    out_late = out_late.reshape(row_count, col_count, slots_dev, half_width)
    out_kept = lax.dynamic_index_in_dim(out_late, col_at, 1, False)
    out_other = swap_col(lax.dynamic_index_in_dim(out_late, 1 - col_at, 1, False))
    out_rows = both_halves(out_kept, out_other, 1)
    gate_probs = jax.nn.softmax(jnp.dot(hidden_late, w_router, precision=highest), axis=-1)
    gating = jnp.sum(jnp.where(chosen, gate_probs, 0.0), axis=-1, keepdims=True)
    d_proj = mm(heads, my_half(d_attn_late, 1), TN).astype(bf16)
    d_proj = d_proj.reshape(row_count, inner, half_width)
    d_proj, out_rows, d_head = lax.optimization_barrier((d_proj, out_rows, d_head))
    late_parts = [
        shift(
            jnp.concatenate(
                [
                    lax.dynamic_index_in_dim(d_proj, home ^ row_at ^ j, 0, False),
                    for_row(out_rows, j),
                ],
                axis=0,
            ),
            "row",
            j,
        )
        for j in range(row_count)
    ]

    d_qkv, d_table = attend_backward(qkv, d_head, lse, table, segments, heads_dev)

    late_parts, d_qkv = lax.optimization_barrier((late_parts, d_qkv))
    d_w = mm(normed, d_qkv, TN)
    d_w_sent = swap_col(other_half(d_w, 0).astype(bf16))
    part_normed = mm(d_qkv, w_all, NT).astype(bf16).reshape(row_count, quarter, width)
    normed_parts = [
        lax.ppermute(
            lax.dynamic_index_in_dim(part_normed, row_at ^ k, 0, False), group, pairs_home(k)
        )
        for k in range(row_count)
    ]

    gain_part = jnp.sum(d_w * w_all.astype(f32), axis=1) / gain_attn
    d_rel_part = jnp.einsum("ho,ob->hb", d_table[:, : 2 * length - 1], buckets, precision=highest)
    rel_whole = lax.dynamic_update_slice_in_dim(
        jnp.zeros((H, NB), f32), d_rel_part, row_at * heads_dev, 0
    )
    rel_row = jnp.pad(rel_whole.reshape(1, H * NB), ((0, 0), (0, width - H * NB)))
    small = jnp.concatenate([d_router, d_gain_ffn[None], gain_part[None], rel_row], axis=0)
    small = small + swap_col(small)

    d_proj = sum(part[:inner].astype(f32) for part in late_parts)
    d_proj = d_proj.reshape(half_width, inner)
    d_w = my_half(d_w, 0) + d_w_sent.astype(f32)
    packed = jnp.concatenate([d_w, d_proj], axis=1).astype(bf16)
    pieces = packed.reshape(dp_count, half_width // dp_count, packed.shape[1])
    small_low = small.astype(bf16)
    piece_parts = [
        shift(
            jnp.concatenate(
                [lax.dynamic_index_in_dim(pieces, dp_at ^ j, 0, False), small_low], axis=0
            ),
            "dp",
            j,
        )
        for j in range(dp_count)
    ]

    whole_shape = (dp_count,) + block_shape
    all_x, all_g = all_x.reshape(whole_shape), all_g.reshape(whole_shape)
    at = jnp.stack([dp_at, first])
    at, pieces = lax.optimization_barrier((at, pieces))
    weights = (w_router, w_up, w_down)
    grads_up_down = weight_grads(0, all_x, all_g, *weights, at, ())
    *piece_parts, grads_up_down = lax.optimization_barrier((*piece_parts, grads_up_down))
    piece_parts = jnp.stack(piece_parts)
    piece_parts = sum(
        lax.dynamic_index_in_dim(piece_parts, i ^ dp_at, 0, False).astype(f32)
        for i in range(dp_count)
    )
    own_rows = pieces.shape[1]
    piece, small = piece_parts[:own_rows].astype(bf16), piece_parts[own_rows:]
    summed_parts = [shift(piece, "dp", j) for j in range(dp_count)]

    at, piece = lax.optimization_barrier((at, piece))
    d_up, d_down = weight_grads(1, all_x, all_g, *weights, at, grads_up_down)
    summed_parts, small, normed_parts, late_parts, d_up, d_down = lax.optimization_barrier(
        (summed_parts, small, normed_parts, late_parts, d_up, d_down)
    )
    small = total_over(small, "row")

    summed = in_order(summed_parts, dp_at).astype(f32)
    d_w_qkv = jnp.stack([summed[:, i * inner : (i + 1) * inner] for i in range(3)])
    d_proj = summed[:, 3 * inner :].reshape(inner, half_width)
    d_w_router = small[:experts_all].T
    d_gain_ffn = small[experts_all]
    d_gain_attn = small[experts_all + 1]
    d_rel_bias = small[experts_all + 2, : H * NB].reshape(H, NB)
    d_normed = sum(part.astype(f32) for part in normed_parts)
    out_back = in_order([part[inner:] for part in late_parts], row_at)
    layer_out = my_half(middle, 1) + gating * placed_back(out_back).astype(f32)

    own = own_tokens.astype(f32)
    scale_own = lax.rsqrt(jnp.mean(own * own, axis=-1, keepdims=True) + epsilon)
    scaled_attn = d_normed * gain_attn
    d_own = (
        my_half(d_middle, 0)
        + scale_own * scaled_attn
        - own * scale_own**3 * jnp.mean(scaled_attn * own, axis=-1, keepdims=True)
    )
    d_layer_in = both_halves(my_half(d_own, 1), swap_col(other_half(d_own, 1)), 0)

    return (
        layer_out,
        d_layer_in,
        d_w_qkv,
        d_proj,
        d_rel_bias,
        d_gain_attn,
        d_gain_ffn,
        d_w_router,
        d_up,
        d_down,
    )


def solution(mesh):
    placed = (
        P(("dp", "row"), None),
        P(None, "col", "row"),
        P("row", "col"),
        P(),
        P(),
        P(("dp", "col"), None),
        P(),
        P(),
        P(),
        P(("dp", "row"), None),
        P(("row", "col"), None, None),
        P(("row", "col"), None, None),
        P(("dp", "row"), "col"),
    )
    return jax.shard_map(
        shards,
        mesh=mesh,
        in_specs=placed,
        out_specs=(
            P(("dp", "row"), "col"),
            P(("dp", "row"), "col"),
            P(None, "col", "row"),
            P("row", "col"),
            P(),
            P(),
            P(),
            P(),
            P(("row", "col"), "dp", None),
            P(("row", "col"), "dp", None),
        ),
        check_vma=False,
    )
```

```python
from functools import partial

import jax
import jax.numpy as jnp
from jax import lax
from jax.experimental import pallas as pl
from jax.experimental.pallas import tpu as pltpu
from jax.sharding import PartitionSpec as P

H = 12
HD = 64
NB = 32
EXP_DEV = 2
SUB = 128

epsilon = 1e-06
highest = lax.Precision.HIGHEST
f32 = jnp.float32
bf16 = jnp.bfloat16
group = ("row", "col")

NT = (((1,), (1,)), ((), ()))
NN = (((1,), (0,)), ((), ()))
TN = (((0,), (0,)), ((), ()))


def mm(a, b, dims=NN):
    return lax.dot_general(a, b, dims, preferred_element_type=f32)


def fill_strip(table_ref, strip_ref):
    heads, _, span = strip_ref.shape
    for h in range(heads):
        rows = jnp.broadcast_to(table_ref[h : h + 1, :], (SUB, table_ref.shape[1]))
        rolled = pltpu.roll(rows, table_ref.shape[1] - (SUB - 1), 1, stride=1, stride_axis=0)
        strip_ref[h] = rolled[:, :span]


def strip_at(step, part, parts, keys_at, width, length):
    begin = length - SUB * (step * parts + part + 1) + keys_at
    return pl.ds(pl.multiple_of(begin, SUB), width)


def tiles_meet(ids_ref, step, rows, keys_at, width):
    begin = step * rows
    above = ids_ref[keys_at + width - 1] >= ids_ref[begin]
    below = ids_ref[keys_at] <= ids_ref[begin + rows - 1]
    return jnp.logical_and(above, below)


def forward_kernel(
    ids_ref,
    qkv_ref,
    table_ref,
    seg_col_ref,
    seg_row_ref,
    out_ref,
    lse_ref,
    strip_ref,
    top_ref,
    total_ref,
    acc_ref,
    *,
    rows,
    heads,
):
    step = pl.program_id(0)
    length = qkv_ref.shape[0]
    inner = heads * HD
    parts = rows // SUB

    @pl.when(step == 0)
    def _():
        fill_strip(table_ref, strip_ref)

    here = pl.ds(pl.multiple_of(step * rows, rows), rows)
    top_ref[...] = jnp.full(top_ref.shape, -2e9, f32)
    total_ref[...] = jnp.zeros(total_ref.shape, f32)
    acc_ref[...] = jnp.zeros(acc_ref.shape, f32)

    for at in range(0, length, rows):

        @pl.when(tiles_meet(ids_ref, step, rows, at, rows))
        def _():
            same = seg_col_ref[here, :] == seg_row_ref[:, at : at + rows]
            for h in range(heads):
                lo = h * HD
                queries = qkv_ref[here, lo : lo + HD] * jnp.asarray(HD**-0.5, bf16)
                keys = qkv_ref[at : at + rows, inner + lo : inner + lo + HD]
                values = qkv_ref[at : at + rows, 2 * inner + lo : 2 * inner + lo + HD]
                bias = jnp.concatenate(
                    [
                        strip_ref[h, :, strip_at(step, u, parts, at, rows, length)]
                        for u in range(parts)
                    ],
                    axis=0,
                )
                scores = jnp.where(same, mm(queries, keys, NT) + bias, -1e9)
                old = top_ref[:, h : h + 1]
                top = jnp.maximum(old, jnp.max(scores, axis=1, keepdims=True))
                weights = jnp.exp(scores - top)
                keep = jnp.exp(old - top)
                top_ref[:, h : h + 1] = top
                total_ref[:, h : h + 1] = keep * total_ref[:, h : h + 1] + jnp.sum(
                    weights, axis=1, keepdims=True
                )
                acc_ref[h] = keep * acc_ref[h] + mm(weights.astype(bf16), values)

    outs = [acc_ref[h] / total_ref[:, h : h + 1] for h in range(heads)]
    out_ref[...] = jnp.concatenate(outs, axis=1).astype(bf16)
    lse_ref[...] = top_ref[...] + jnp.log(jnp.maximum(total_ref[...], 1e-30))


def whole(shape):
    return pl.BlockSpec(shape, lambda *_: (0,) * len(shape))


def attend_forward(qkv, table, segments, heads):
    length = qkv.shape[0]
    rows = min(256, length)
    inner = heads * HD
    return pl.pallas_call(
        partial(forward_kernel, rows=rows, heads=heads),
        grid_spec=pltpu.PrefetchScalarGridSpec(
            num_scalar_prefetch=1,
            grid=(length // rows,),
            in_specs=[
                whole(qkv.shape),
                whole(table.shape),
                whole((length, 1)),
                whole((1, length)),
            ],
            out_specs=[
                pl.BlockSpec((rows, inner), lambda i, ids: (i, 0)),
                pl.BlockSpec((rows, SUB), lambda i, ids: (i, 0)),
            ],
            scratch_shapes=[
                pltpu.VMEM((heads, SUB, 2 * length - SUB), f32),
                pltpu.VMEM((rows, SUB), f32),
                pltpu.VMEM((rows, SUB), f32),
                pltpu.VMEM((heads, rows, HD), f32),
            ],
        ),
        out_shape=[
            jax.ShapeDtypeStruct((length, inner), bf16),
            jax.ShapeDtypeStruct((length, SUB), f32),
        ],
        compiler_params=pltpu.CompilerParams(vmem_limit_bytes=40 * 1024 * 1024),
        cost_estimate=pl.CostEstimate(
            flops=4 * length * length * inner,
            bytes_accessed=10 * length * inner,
            transcendentals=length * length * heads,
        ),
        name="attend_forward",
    )(segments, qkv, table, segments[:, None], segments[None, :])


def backward_kernel(
    ids_ref,
    qkv_ref,
    out_in_ref,
    grad_ref,
    lse_ref,
    table_ref,
    seg_col_ref,
    seg_row_ref,
    out_ref,
    d_table_ref,
    strip_ref,
    d_strip_ref,
    d_keys_ref,
    d_values_ref,
    d_queries_ref,
    *,
    rows,
    heads,
):
    step = pl.program_id(0)
    length = qkv_ref.shape[0]
    inner = heads * HD
    parts = rows // SUB

    @pl.when(step == 0)
    def _():
        fill_strip(table_ref, strip_ref)
        d_strip_ref[...] = jnp.zeros_like(d_strip_ref)
        d_keys_ref[...] = jnp.zeros_like(d_keys_ref)
        d_values_ref[...] = jnp.zeros_like(d_values_ref)

    here = pl.ds(pl.multiple_of(step * rows, rows), rows)
    product = grad_ref[here, :].astype(f32) * out_in_ref[here, :].astype(f32)
    deltas = [
        jnp.sum(product[:, h * HD : (h + 1) * HD], axis=1, keepdims=True) for h in range(heads)
    ]
    d_queries_ref[...] = jnp.zeros_like(d_queries_ref)

    for at in range(0, length, rows):

        @pl.when(tiles_meet(ids_ref, step, rows, at, rows))
        def _():
            same = seg_col_ref[here, :] == seg_row_ref[:, at : at + rows]
            for h in range(heads):
                lo = h * HD
                queries = qkv_ref[here, lo : lo + HD] * jnp.asarray(HD**-0.5, bf16)
                keys = qkv_ref[at : at + rows, inner + lo : inner + lo + HD]
                values = qkv_ref[at : at + rows, 2 * inner + lo : 2 * inner + lo + HD]
                grads = grad_ref[here, lo : lo + HD]
                bias = jnp.concatenate(
                    [
                        strip_ref[h, :, strip_at(step, u, parts, at, rows, length)]
                        for u in range(parts)
                    ],
                    axis=0,
                )
                scores = mm(queries, keys, NT) + bias - lse_ref[:, h : h + 1]
                probs = jnp.exp(jnp.where(same, scores, -1e9))
                d_values_ref[lo : lo + HD, at : at + rows] += mm(grads, probs.astype(bf16), TN)
                d_scores = probs * (mm(grads, values, NT) - deltas[h])
                for u in range(parts):
                    span = strip_at(step, u, parts, at, rows, length)
                    d_strip_ref[h, :, span] += d_scores[u * SUB : (u + 1) * SUB]
                d_raw = d_scores.astype(bf16)
                d_queries_ref[h] += mm(d_raw, keys)
                d_keys_ref[lo : lo + HD, at : at + rows] += mm(queries, d_raw, TN)

    out_ref[here, :inner] = (
        jnp.concatenate([d_queries_ref[h] for h in range(heads)], axis=1) * HD**-0.5
    ).astype(bf16)

    @pl.when(step == pl.num_programs(0) - 1)
    def _():
        for h in range(heads):
            lo = h * HD
            out_ref[:, inner + lo : inner + lo + HD] = d_keys_ref[lo : lo + HD, :].T.astype(bf16)
            out_ref[:, 2 * inner + lo : 2 * inner + lo + HD] = d_values_ref[
                lo : lo + HD, :
            ].T.astype(bf16)
            summed = jnp.concatenate([d_strip_ref[h], jnp.zeros((SUB, SUB), f32)], axis=1)
            count = SUB
            while count > 1:
                count //= 2
                summed = summed[count:] + pltpu.roll(summed[:count], count, 1)
            d_table_ref[h : h + 1, :] = summed


def attend_backward(qkv, head_out, d_head, lse, table, segments, heads):
    length = qkv.shape[0]
    rows = min(256, length)
    inner = heads * HD
    return pl.pallas_call(
        partial(backward_kernel, rows=rows, heads=heads),
        grid_spec=pltpu.PrefetchScalarGridSpec(
            num_scalar_prefetch=1,
            grid=(length // rows,),
            in_specs=[
                whole(qkv.shape),
                whole(head_out.shape),
                whole(d_head.shape),
                pl.BlockSpec((rows, SUB), lambda i, ids: (i, 0)),
                whole(table.shape),
                whole((length, 1)),
                whole((1, length)),
            ],
            out_specs=[whole(qkv.shape), whole(table.shape)],
            scratch_shapes=[
                pltpu.VMEM((heads, SUB, 2 * length - SUB), f32),
                pltpu.VMEM((heads, SUB, 2 * length - SUB), f32),
                pltpu.VMEM((inner, length), f32),
                pltpu.VMEM((inner, length), f32),
                pltpu.VMEM((heads, rows, HD), f32),
            ],
        ),
        out_shape=[
            jax.ShapeDtypeStruct(qkv.shape, bf16),
            jax.ShapeDtypeStruct(table.shape, f32),
        ],
        compiler_params=pltpu.CompilerParams(vmem_limit_bytes=48 * 1024 * 1024),
        cost_estimate=pl.CostEstimate(
            flops=10 * length * length * inner,
            bytes_accessed=16 * length * inner,
            transcendentals=length * length * heads,
        ),
        name="attend_backward",
    )(segments, qkv, head_out, d_head, lse, table, segments[:, None], segments[None, :])


def joined(block_ref, at):
    rows, cols, _, slots, half = block_ref.shape
    return jnp.concatenate(
        [
            jnp.concatenate([block_ref[at ^ j, c, 0] for c in range(cols)], axis=1)
            for j in range(rows)
        ],
        axis=0,
    )


def halves(own, other, col):
    return jnp.where(
        col == 0,
        jnp.concatenate([own, other], axis=1),
        jnp.concatenate([other, own], axis=1),
    )


def flat(block):
    return block.reshape(-1, block.shape[-1]).astype(f32)


GELU_A = 0.7978845608028654
GELU_B = 0.044715


def gelu_pair(u):
    square = u * u
    factor = 0.5 * jnp.tanh(u * (GELU_A + (GELU_A * GELU_B) * square)) + 0.5
    value = u * factor
    slope = factor + value * (1.0 - factor) * (2 * GELU_A + (6 * GELU_A * GELU_B) * square)
    return value, slope


def router_probs(x, router_ref):
    weights = router_ref[...]
    high = weights.astype(bf16)
    low = (weights - high.astype(f32)).astype(bf16)
    logits = mm(x, high) + mm(x, low)
    exped = jnp.exp(logits - jnp.max(logits, axis=1, keepdims=True))
    return exped / jnp.sum(exped, axis=1, keepdims=True)


def gate(probs, expert):
    picked = lax.broadcasted_iota(jnp.int32, probs.shape, 1) == expert
    return picked, jnp.sum(jnp.where(picked, probs, 0.0), axis=1, keepdims=True)


def expert_kernel(
    at_ref,
    x_in_ref,
    own_ref,
    other_ref,
    router_ref,
    up_ref,
    down_ref,
    out_ref,
    grad_ref,
    d_router_ref,
    x_ref,
    g_ref,
    x_turned_ref,
    g_turned_ref,
    probs_ref,
    out_acc_ref,
    grad_acc_ref,
):
    expert = pl.program_id(0)
    step = pl.program_id(1)
    col = at_ref[1]
    row = at_ref[2]
    first = at_ref[3]

    @pl.when(step == 0)
    def _():
        x = joined(x_in_ref, row)
        probs = router_probs(x, router_ref)
        _, gating = gate(probs, first + expert)
        g = halves(flat(own_ref[:, 0, 0]), flat(other_ref[:, 0, 0]), col)
        x_ref[...] = x
        g_ref[...] = g
        x_turned_ref[...] = x.T
        g_turned_ref[...] = (gating * g).astype(bf16).T
        probs_ref[...] = probs
        out_acc_ref[...] = jnp.zeros_like(out_acc_ref)
        grad_acc_ref[...] = jnp.zeros_like(grad_acc_ref)

    parts = 3
    tile = up_ref.shape[1] // parts
    activated, d_pre = [], []
    for i in range(parts):
        here = slice(i * tile, (i + 1) * tile)
        value, slope = gelu_pair(mm(up_ref[0, here], x_turned_ref[...]))
        activated.append(value.astype(bf16))
        d_pre.append((mm(down_ref[0, here], g_turned_ref[...]) * slope).astype(bf16))
    out_acc_ref[...] += mm(jnp.concatenate(activated, axis=0), down_ref[0], TN)
    grad_acc_ref[...] += mm(jnp.concatenate(d_pre, axis=0), up_ref[0], TN)

    @pl.when(step == pl.num_programs(1) - 1)
    def _():
        out = out_acc_ref[...]
        probs = probs_ref[...]
        picked, gating = gate(probs, first + expert)
        d_gating = jnp.sum(g_ref[...] * out, axis=1, keepdims=True)
        d_logits = d_gating * probs * (picked.astype(f32) - gating)
        grad = grad_acc_ref[...] + lax.dot_general(
            d_logits, router_ref[...], NT, precision=highest, preferred_element_type=f32
        )
        d_router = lax.dot_general(
            d_logits,
            x_ref[...].astype(f32),
            TN,
            precision=highest,
            preferred_element_type=f32,
        )
        rows, cols, _, slots, half = grad_ref.shape
        out = out.astype(bf16)
        grad = grad.astype(bf16)
        first_half, last_half = out[:, :half], out[:, half:]
        own = jnp.where(col == 0, first_half, last_half)
        other = jnp.where(col == 0, last_half, first_half)
        out_ref[:, 0, 0] = own.reshape(rows, slots, half)
        out_ref[:, 1, 0] = other.reshape(rows, slots, half)
        for j in range(rows):
            for c in range(cols):
                grad_ref[row ^ j, c, 0] = grad[
                    j * slots : (j + 1) * slots, c * half : (c + 1) * half
                ]

        @pl.when(expert == 0)
        def _():
            d_router_ref[...] = d_router

        @pl.when(expert > 0)
        def _():
            d_router_ref[...] += d_router


def run_experts(at, got_x, g_own, g_other, w_router, w_up, w_down):
    rows, cols, experts, slots, half = got_x.shape
    hidden, width = w_up.shape[1:]
    tile = 768
    block = pl.BlockSpec((rows, cols, 1, slots, half), lambda e, f, at: (0, 0, e, 0, 0))
    part = pl.BlockSpec((rows, 1, 1, slots, half), lambda e, f, at: (0, 0, e, 0, 0))
    weight = pl.BlockSpec((1, tile, width), lambda e, f, at: (e, f, 0))
    tokens = rows * slots
    shape = jax.ShapeDtypeStruct(got_x.shape, bf16)
    router_shape = (w_router.shape[1], width)
    return pl.pallas_call(
        expert_kernel,
        grid_spec=pltpu.PrefetchScalarGridSpec(
            num_scalar_prefetch=1,
            grid=(experts, hidden // tile),
            in_specs=[block, part, part, whole(w_router.shape), weight, weight],
            out_specs=[block, block, whole(router_shape)],
            scratch_shapes=[
                pltpu.VMEM((tokens, width), bf16),
                pltpu.VMEM((tokens, width), f32),
                pltpu.VMEM((width, tokens), bf16),
                pltpu.VMEM((width, tokens), bf16),
                pltpu.VMEM((tokens, w_router.shape[1]), f32),
                pltpu.VMEM((tokens, width), f32),
                pltpu.VMEM((tokens, width), f32),
            ],
        ),
        out_shape=[shape, shape, jax.ShapeDtypeStruct(router_shape, f32)],
        compiler_params=pltpu.CompilerParams(vmem_limit_bytes=56 * 1024 * 1024),
        cost_estimate=pl.CostEstimate(
            flops=8 * experts * tokens * hidden * width,
            bytes_accessed=4 * experts * hidden * width,
            transcendentals=experts * tokens * hidden,
        ),
        name="experts",
    )(at, got_x, g_own, g_other, w_router, w_up, w_down)


def weight_kernel(
    at_ref, x_in_ref, own_ref, other_ref, router_ref, up_ref, down_ref, *refs, expert
):
    d_up_ref, d_down_ref = refs[-2:]
    step = pl.program_id(0)
    parts = x_in_ref.shape[0]
    x = jnp.concatenate([joined(x_in_ref.at[i], at_ref[2]) for i in range(parts)], axis=0)
    g = halves(flat(own_ref[:, :, 0, 0]), flat(other_ref[:, :, 0, 0]), at_ref[1])
    _, gating = gate(router_probs(x, router_ref), at_ref[3] + expert)
    g = (gating * g).astype(bf16)
    x_turned, g_turned = x.T, g.T
    own = up_ref.shape[1]
    tile = own // 3 if own % 768 == 0 else own
    for i in range(own // tile):
        here = slice(i * tile, (i + 1) * tile)
        value, slope = gelu_pair(mm(up_ref[0, here], x_turned))
        d_pre = (mm(down_ref[0, here], g_turned) * slope).astype(bf16)
        d_down = mm(value.astype(bf16), g)
        d_up = mm(d_pre, x)

        @pl.when(step == 0)
        def _():
            d_up_ref[0, here] = d_up
            d_down_ref[0, here] = d_down

        @pl.when(step > 0)
        def _():
            d_up_ref[0, here] += d_up
            d_down_ref[0, here] += d_down


def weight_grads(expert, at, all_x, g_own, g_other, w_router, w_up, w_down, earlier):
    parts, rows, cols, experts, slots, half = all_x.shape
    hidden, width = w_up.shape[1:]
    own = hidden // parts
    each = min(4, parts)
    block = pl.BlockSpec(
        (each, rows, cols, 1, slots, half), lambda n, at: (n, 0, 0, expert, 0, 0)
    )
    part = pl.BlockSpec((each, rows, 1, 1, slots, half), lambda n, at: (n, 0, 0, expert, 0, 0))
    weight = pl.BlockSpec((1, own, width), lambda n, at: (expert, at[0], 0))
    result = pl.BlockSpec((1, own, width), lambda n, at: (expert, 0, 0))
    shape = jax.ShapeDtypeStruct((experts, own, width), f32)
    return pl.pallas_call(
        partial(weight_kernel, expert=expert),
        grid_spec=pltpu.PrefetchScalarGridSpec(
            num_scalar_prefetch=1,
            grid=(parts // each,),
            in_specs=[block, part, part, whole(w_router.shape), weight, weight]
            + [pl.BlockSpec(memory_space=pl.ANY)] * len(earlier),
            out_specs=[result, result],
        ),
        out_shape=[shape, shape],
        input_output_aliases={7 + i: i for i in range(len(earlier))},
        compiler_params=pltpu.CompilerParams(vmem_limit_bytes=56 * 1024 * 1024),
        cost_estimate=pl.CostEstimate(
            flops=8 * parts * rows * slots * own * width,
            bytes_accessed=12 * own * width + 2 * all_x.size,
            transcendentals=parts * rows * slots * own,
        ),
        name="weight_grads",
    )(at, all_x, g_own, g_other, w_router, w_up, w_down, *earlier)


def pairs_out(k):
    return [
        (r * 2 + c, ((2 * (r % 2) + c) ^ k) * 2 + r // 2) for r in range(4) for c in range(2)
    ]


def pairs_home(k):
    return [(b, a) for a, b in pairs_out(k)]


def blocks_home(x):
    return [
        (r * 2 + s, (2 * s + ((r // 2) ^ x)) * 2 + r % 2) for r in range(4) for s in range(2)
    ]


def swap_col(array):
    return lax.ppermute(array, "col", [(0, 1), (1, 0)])


def shift(array, axis, bits):
    if bits == 0:
        return array
    count = lax.axis_size(axis)
    return lax.ppermute(array, axis, [(i, i ^ bits) for i in range(count)])


def total_over(array, axis):
    count = lax.axis_size(axis)
    stride = 1
    while stride < count:
        if 4 * stride <= count:
            near, far, last = (shift(array, axis, stride * i) for i in (1, 2, 3))
            array = (array + near) + (far + last)
            stride *= 4
        else:
            array = array + shift(array, axis, stride)
            stride *= 2
    return array


def shards(
    layer_in,
    w_qkv,
    w_proj,
    rel_bias,
    rel_bucket,
    segment_ids,
    gain_attn,
    gain_ffn,
    w_router,
    routes,
    w_up,
    w_down,
    d_layer,
):
    row_count = lax.axis_size("row")
    col_count = lax.axis_size("col")
    dp_count = lax.axis_size("dp")
    dp_at = lax.axis_index("dp")
    row_at = lax.axis_index("row")
    col_at = lax.axis_index("col")
    tok_dev, width = layer_in.shape
    slot_count = max(2, tok_dev // 8)
    half_width = width // col_count
    quarter = tok_dev // 2
    length = segment_ids.shape[1]
    inner = w_qkv.shape[2]
    heads_dev = inner // HD
    experts_all = EXP_DEV * row_count * col_count
    home = 2 * (row_at % 2) + col_at
    is_first = col_at == 0

    def both_halves(mine, other, axis):
        return jnp.where(
            is_first,
            jnp.concatenate([mine, other], axis),
            jnp.concatenate([other, mine], axis),
        )

    def my_half(array, axis):
        size = array.shape[axis] // 2
        return lax.dynamic_slice_in_dim(array, col_at * size, size, axis)

    def other_half(array, axis):
        size = array.shape[axis] // 2
        return lax.dynamic_slice_in_dim(array, (1 - col_at) * size, size, axis)

    def own_first(array, axis):
        return jnp.concatenate([my_half(array, axis), other_half(array, axis)], axis)

    def in_order(chunks, at):
        stacked = jnp.stack(chunks)
        return jnp.concatenate(
            [lax.dynamic_index_in_dim(stacked, i ^ at, 0, False) for i in range(len(chunks))], 0
        )

    own_tokens = my_half(layer_in, 0)
    token_parts = [lax.ppermute(own_tokens, group, pairs_out(k)) for k in range(row_count)]
    w_pair = both_halves(w_qkv, swap_col(w_qkv), 1)

    me = row_at * col_count + col_at
    first = me * EXP_DEV
    at = jnp.stack([dp_at, col_at, row_at, first])
    routed = routes[:, 0]
    chosen = routed[:, None] == jnp.arange(experts_all, dtype=jnp.int32)[None, :]
    counts = jnp.cumsum(chosen.astype(jnp.int32), axis=0)
    slot_index = jnp.sum(jnp.where(chosen, counts, 0), axis=-1) - 1
    slots_all = experts_all * slot_count
    slots_dev = EXP_DEV * slot_count
    send_shape = (row_count * col_count, EXP_DEV, slot_count, half_width)
    block_shape = (row_count, col_count, EXP_DEV, slot_count, half_width)

    def one_hot(devices):
        placed = (devices * EXP_DEV + routed % EXP_DEV) * slot_count + slot_index
        slots = jnp.arange(slots_all, dtype=jnp.int32)[:, None]
        return (slots == placed[None, :]).astype(bf16)

    placing = one_hot(routed // EXP_DEV)
    placing_near = one_hot((routed // EXP_DEV) ^ me)

    def all_to_all(array):
        return lax.all_to_all(array, group, split_axis=0, concat_axis=0, tiled=True)

    g_slots = mm(placing_near, d_layer).astype(bf16)
    g_slots = g_slots.reshape(row_count, col_count * slots_dev, half_width)
    early = [jnp.concatenate([w_proj, g_slots[j]], axis=0) for j in range(row_count)]
    token_parts[0], early = lax.optimization_barrier((token_parts[0], early))
    early = [shift(early[j], "row", j) for j in range(row_count)]
    gains = own_first(gain_ffn, 0)
    router = own_first(w_router, 0)
    input_near = own_first(layer_in, 1).astype(f32)

    tokens_seq = in_order(token_parts, row_at).astype(f32)
    w_all = jnp.concatenate([w_pair[0], w_pair[1], w_pair[2]], axis=1)
    scale_seq = lax.rsqrt(jnp.mean(tokens_seq * tokens_seq, axis=-1, keepdims=True) + epsilon)
    normed = (tokens_seq * scale_seq * gain_attn).astype(bf16)
    qkv = mm(normed, w_all).astype(bf16)

    buckets = (rel_bucket[:, None] == jnp.arange(NB, dtype=jnp.int32)[None, :]).astype(f32)
    bias_rows = lax.dynamic_slice_in_dim(rel_bias, row_at * heads_dev, heads_dev, 0)
    bias_table = jnp.einsum("hb,ob->ho", bias_rows, buckets, precision=highest)
    table = jnp.pad(bias_table, ((0, 0), (0, 1)))
    segments = segment_ids[0]
    head_out, lse = attend_forward(qkv, table, segments, heads_dev)

    head_blocks = head_out.reshape(2, tok_dev, inner)
    head_parts = [
        lax.ppermute(
            lax.dynamic_index_in_dim(head_blocks, (row_at ^ k) // 2, 0, False),
            group,
            pairs_home(k),
        )
        for k in range(row_count)
    ]

    early, d_layer_late, _ = lax.optimization_barrier((early, d_layer, head_out))
    early = jnp.stack(early)
    g_near = early[:, inner:].reshape(block_shape)
    all_g = lax.all_gather(g_near, "dp", axis=0, tiled=False)
    proj_own = jnp.concatenate(
        [
            lax.dynamic_index_in_dim(early[:, :inner], row_at ^ home ^ k, 0, False)
            for k in range(row_count)
        ],
        axis=0,
    )
    proj_other = swap_col(proj_own).reshape(row_count, inner, half_width)
    proj_other = jnp.concatenate([proj_other[k ^ 1] for k in range(row_count)], axis=0)
    proj_all = jnp.concatenate([proj_own, proj_other], axis=1)
    g_other = swap_col(g_near[:, 1:])
    grads_in = jnp.concatenate([d_layer_late, swap_col(d_layer_late)], axis=1).astype(f32)

    heads = jnp.concatenate(head_parts, axis=1)
    middle = input_near + mm(heads, proj_all)
    scale_ffn = lax.rsqrt(jnp.mean(middle * middle, axis=-1, keepdims=True) + epsilon)
    hidden = middle * scale_ffn * gains
    x_slots = mm(placing, hidden[:, :half_width].astype(bf16)).astype(bf16).reshape(send_shape)
    got_x = all_to_all(x_slots)
    all_x = lax.all_gather(got_x, "dp", axis=0, tiled=False)
    out_slots, grad_slots, d_router = run_experts(
        at, got_x.reshape(block_shape), g_near, g_other, w_router, w_up, w_down
    )
    got_grad = all_to_all(grad_slots.reshape(send_shape)).reshape(slots_all, half_width)
    mine = mm(placing, got_grad, TN).astype(bf16)
    d_hidden = jnp.concatenate([mine, swap_col(mine)], axis=1).astype(f32)
    d_gain_ffn = 0.5 * both_halves(
        jnp.sum((middle * scale_ffn * d_hidden)[:, :half_width], axis=0),
        jnp.sum((middle * scale_ffn * d_hidden)[:, half_width:], axis=0),
        0,
    )
    scaled_ffn = d_hidden * gains
    d_middle = (
        grads_in
        + scale_ffn * scaled_ffn
        - middle * scale_ffn**3 * jnp.mean(scaled_ffn * middle, axis=-1, keepdims=True)
    )
    d_attn = d_middle.astype(bf16)
    d_heads = mm(my_half(d_attn, 0), proj_all, NT).astype(bf16)
    d_head = in_order(
        [
            lax.ppermute(d_heads[:, k * inner : (k + 1) * inner], group, pairs_out(k))
            for k in range(row_count)
        ],
        row_at,
    )

    hidden_late, d_attn_late, out_late, d_heads = lax.optimization_barrier(
        (hidden, d_attn, out_slots, d_heads)
    )
    gate_probs = jax.nn.softmax(jnp.dot(hidden_late, router, precision=highest), axis=-1)
    gating = jnp.sum(jnp.where(chosen, gate_probs, 0.0), axis=-1, keepdims=True)
    d_proj = mm(heads, d_attn_late[:, :half_width], TN).astype(bf16)
    d_proj = d_proj.reshape(row_count, inner, half_width)
    out_late, d_proj, d_head = lax.optimization_barrier((out_late, d_proj, d_head))
    out_parts = [shift(out_late[j], "row", j) for j in range(row_count)]
    proj_parts = [
        shift(lax.dynamic_index_in_dim(d_proj, home ^ row_at ^ j, 0, False), "row", j)
        for j in range(row_count)
    ]

    d_qkv, d_table = attend_backward(qkv, head_out, d_head, lse, table, segments, heads_dev)

    out_parts, proj_parts, d_qkv = lax.optimization_barrier((out_parts, proj_parts, d_qkv))
    all_g_other = swap_col(all_g[:, :, 1:])
    d_w = mm(normed, d_qkv, TN)
    d_w_other = swap_col(other_half(d_w, 0).astype(bf16))
    gain_part = jnp.sum(d_w * w_all.astype(f32), axis=1) / gain_attn
    d_rel_part = jnp.einsum("ho,ob->hb", d_table[:, : 2 * length - 1], buckets, precision=highest)
    rel_whole = lax.dynamic_update_slice_in_dim(
        jnp.zeros((H, NB), f32), d_rel_part, row_at * heads_dev, 0
    )
    rel_row = jnp.pad(rel_whole.reshape(1, H * NB), ((0, 0), (0, width - H * NB)))
    small = jnp.concatenate([d_router, d_gain_ffn[None], gain_part[None], rel_row], axis=0)
    small = total_over(small, "col").astype(bf16)

    part_normed = mm(d_qkv, w_all, NT).astype(bf16).reshape(2, tok_dev, width)
    normed_parts = [
        lax.ppermute(
            lax.dynamic_index_in_dim(part_normed, (row_at // 2) ^ x, 0, False),
            group,
            blocks_home(x),
        )
        for x in range(2)
    ]

    d_proj = sum(part.astype(f32) for part in proj_parts).reshape(half_width, inner)
    d_w = my_half(d_w, 0) + d_w_other.astype(f32)
    packed = jnp.concatenate([d_w, d_proj], axis=1).astype(bf16)
    own_rows = half_width // dp_count
    pieces = packed.reshape(dp_count, own_rows, packed.shape[1])
    pieces = [
        jnp.concatenate([lax.dynamic_index_in_dim(pieces, dp_at ^ j, 0, False), small], axis=0)
        for j in range(dp_count)
    ]
    piece_parts = [shift(pieces[j], "dp", j) for j in range(dp_count)]

    all_x = all_x.reshape((dp_count,) + block_shape)
    at, pieces = lax.optimization_barrier((at, pieces))
    weights = (w_router, w_up, w_down)
    d_up_down = weight_grads(0, at, all_x, all_g, all_g_other, *weights, ())
    *piece_parts, d_up_down = lax.optimization_barrier((*piece_parts, d_up_down))
    piece_parts = jnp.stack(piece_parts)
    piece_sum = sum(
        lax.dynamic_index_in_dim(piece_parts, i ^ dp_at, 0, False).astype(f32)
        for i in range(dp_count)
    )
    piece, small = piece_sum[:own_rows].astype(bf16), piece_sum[own_rows:]
    summed_parts = [shift(piece, "dp", j) for j in range(dp_count)]
    normed_sum = normed_parts[0].astype(f32) + normed_parts[1].astype(f32)
    normed_other = swap_col(other_half(normed_sum, 0).astype(bf16))

    at, piece, normed_sum = lax.optimization_barrier((at, piece, normed_sum))
    d_up, d_down = weight_grads(1, at, all_x, all_g, all_g_other, *weights, d_up_down)
    summed_parts, small, normed_other, out_parts, d_up, d_down = lax.optimization_barrier(
        (summed_parts, small, normed_other, out_parts, d_up, d_down)
    )
    small = total_over(small, "row")
    out_stack = jnp.stack(out_parts).reshape(row_count, col_count, slots_dev, half_width)
    out_other = swap_col(out_stack[:, 1])
    out_back = jnp.stack([out_stack[:, 0], out_other], axis=1).reshape(slots_all, half_width)
    layer_out = middle[:, :half_width] + gating * mm(placing_near, out_back, TN)
    summed = in_order(summed_parts, dp_at)
    summed = summed.astype(f32)
    d_w_qkv = jnp.stack([summed[:, i * inner : (i + 1) * inner] for i in range(3)])
    d_proj = summed[:, 3 * inner :].reshape(inner, half_width)
    d_w_router = small[:experts_all].T
    d_gain_ffn = small[experts_all]
    d_gain_attn = small[experts_all + 1]
    d_rel_bias = small[experts_all + 2, : H * NB].reshape(H, NB)

    d_normed = my_half(normed_sum, 0) + normed_other.astype(f32)
    own = own_tokens.astype(f32)
    scale_own = lax.rsqrt(jnp.mean(own * own, axis=-1, keepdims=True) + epsilon)
    scaled_attn = d_normed * gain_attn
    d_own = scale_own * scaled_attn - own * scale_own**3 * jnp.mean(
        scaled_attn * own, axis=-1, keepdims=True
    )
    d_middle_own = my_half(d_middle, 0)
    d_layer_in = both_halves(
        d_middle_own[:, :half_width] + my_half(d_own, 1),
        swap_col(d_middle_own[:, half_width:] + other_half(d_own, 1)),
        0,
    )
    return (
        layer_out,
        d_layer_in,
        d_w_qkv,
        d_proj,
        d_rel_bias,
        d_gain_attn,
        d_gain_ffn,
        d_w_router,
        d_up,
        d_down,
    )


def solution(mesh):
    placed = (
        P(("dp", "row"), None),
        P(None, "col", "row"),
        P("row", "col"),
        P(),
        P(),
        P(("dp", "col"), None),
        P(),
        P(),
        P(),
        P(("dp", "row"), None),
        P(("row", "col"), None, None),
        P(("row", "col"), None, None),
        P(("dp", "row"), "col"),
    )
    return jax.shard_map(
        shards,
        mesh=mesh,
        in_specs=placed,
        out_specs=(
            P(("dp", "row"), "col"),
            P(("dp", "row"), "col"),
            P(None, "col", "row"),
            P("row", "col"),
            P(),
            P(),
            P(),
            P(),
            P(("row", "col"), "dp", None),
            P(("row", "col"), "dp", None),
        ),
        check_vma=False,
    )
```

```python
from functools import partial

import jax
import jax.numpy as jnp
from jax import lax
from jax.experimental import pallas as pl
from jax.experimental.pallas import tpu as pltpu
from jax.sharding import PartitionSpec as P

H = 12
HD = 64
NB = 32
EXP_DEV = 2
SUB = 128

epsilon = 1e-06
highest = lax.Precision.HIGHEST
f32 = jnp.float32
bf16 = jnp.bfloat16
group = ("row", "col")

NT = (((1,), (1,)), ((), ()))
NN = (((1,), (0,)), ((), ()))
TN = (((0,), (0,)), ((), ()))


def mm(a, b, dims=NN):
    return lax.dot_general(a, b, dims, preferred_element_type=f32)


def fill_strip(table_ref, strip_ref):
    heads, _, span = strip_ref.shape
    for h in range(heads):
        rows = jnp.broadcast_to(table_ref[h : h + 1, :], (SUB, table_ref.shape[1]))
        rolled = pltpu.roll(rows, table_ref.shape[1] - (SUB - 1), 1, stride=1, stride_axis=0)
        strip_ref[h] = rolled[:, :span]


def strip_at(step, part, parts, keys_at, width, length):
    begin = length - SUB * (step * parts + part + 1) + keys_at
    return pl.ds(pl.multiple_of(begin, SUB), width)


def each_window(ids_ref, step, rows, length, body):
    tiles = length // rows
    first = ids_ref[step * rows]
    last = ids_ref[step * rows + rows - 1]
    lo = jnp.int32(0)
    hi = jnp.int32(0)
    for i in range(tiles):
        lo = lo + (ids_ref[i * rows + rows - 1] < first).astype(jnp.int32)
        hi = hi + (ids_ref[i * rows] <= last).astype(jnp.int32)
    count = hi - lo
    sizes = sorted({min(2, tiles), min(3, tiles), tiles})
    for i, size in enumerate(sizes):
        fits = count <= size if i == 0 else jnp.logical_and(count > sizes[i - 1], count <= size)

        @pl.when(fits)
        def _():
            begin = jnp.minimum(lo, tiles - size) * rows
            body(pl.multiple_of(begin, rows), size * rows)


def forward_kernel(
    ids_ref,
    qkv_ref,
    table_ref,
    seg_col_ref,
    seg_row_ref,
    out_ref,
    lse_ref,
    strip_ref,
    *,
    rows,
    heads,
):
    step = pl.program_id(0)
    length = qkv_ref.shape[0]
    inner = heads * HD
    parts = rows // SUB

    @pl.when(step == 0)
    def _():
        fill_strip(table_ref, strip_ref)

    here = pl.ds(pl.multiple_of(step * rows, rows), rows)

    def window(begin, width):
        there = pl.ds(begin, width)
        same = seg_col_ref[here, :] == seg_row_ref[:, there]
        q_all = qkv_ref[here, :inner] * jnp.asarray(HD**-0.5, bf16)
        lane = lax.broadcasted_iota(jnp.int32, lse_ref.shape, 1)
        lse = jnp.zeros(lse_ref.shape, f32)
        outs = []
        for h in range(heads):
            lo = h * HD
            keys = qkv_ref[there, inner + lo : inner + lo + HD]
            values = qkv_ref[there, 2 * inner + lo : 2 * inner + lo + HD]
            bias = jnp.concatenate(
                [
                    strip_ref[h, :, strip_at(step, u, parts, begin, width, length)]
                    for u in range(parts)
                ],
                axis=0,
            )
            scores = jnp.where(same, mm(q_all[:, lo : lo + HD], keys, NT) + bias, -1e9)
            top = jnp.max(scores, axis=1, keepdims=True)
            weights = jnp.exp(scores - top)
            total = jnp.sum(weights, axis=1, keepdims=True)
            outs.append(mm(weights.astype(bf16), values) / total)
            lse = jnp.where(lane == h, top + jnp.log(total), lse)
        out_ref[...] = jnp.concatenate(outs, axis=1).astype(bf16)
        lse_ref[...] = lse

    each_window(ids_ref, step, rows, length, window)


def whole(shape):
    return pl.BlockSpec(shape, lambda *_: (0,) * len(shape))


def attend_forward(qkv, table, segments, heads):
    length = qkv.shape[0]
    rows = min(256, length)
    inner = heads * HD
    return pl.pallas_call(
        partial(forward_kernel, rows=rows, heads=heads),
        grid_spec=pltpu.PrefetchScalarGridSpec(
            num_scalar_prefetch=1,
            grid=(length // rows,),
            in_specs=[
                whole(qkv.shape),
                whole(table.shape),
                whole((length, 1)),
                whole((1, length)),
            ],
            out_specs=[
                pl.BlockSpec((rows, inner), lambda i, ids: (i, 0)),
                pl.BlockSpec((rows, SUB), lambda i, ids: (i, 0)),
            ],
            scratch_shapes=[
                pltpu.VMEM((heads, SUB, 2 * length - SUB), f32),
            ],
        ),
        out_shape=[
            jax.ShapeDtypeStruct((length, inner), bf16),
            jax.ShapeDtypeStruct((length, SUB), f32),
        ],
        compiler_params=pltpu.CompilerParams(vmem_limit_bytes=40 * 1024 * 1024),
        cost_estimate=pl.CostEstimate(
            flops=4 * length * length * inner,
            bytes_accessed=10 * length * inner,
            transcendentals=length * length * heads,
        ),
        name="attend_forward",
    )(segments, qkv, table, segments[:, None], segments[None, :])


def backward_kernel(
    ids_ref,
    qkv_ref,
    out_in_ref,
    grad_ref,
    lse_ref,
    table_ref,
    seg_col_ref,
    seg_row_ref,
    out_ref,
    d_table_ref,
    strip_ref,
    d_strip_ref,
    d_keys_ref,
    d_values_ref,
    *,
    rows,
    heads,
):
    step = pl.program_id(0)
    length = qkv_ref.shape[0]
    inner = heads * HD
    parts = rows // SUB

    @pl.when(step == 0)
    def _():
        fill_strip(table_ref, strip_ref)
        d_strip_ref[...] = jnp.zeros_like(d_strip_ref)
        d_keys_ref[...] = jnp.zeros_like(d_keys_ref)
        d_values_ref[...] = jnp.zeros_like(d_values_ref)

    here = pl.ds(pl.multiple_of(step * rows, rows), rows)
    product = grad_ref[here, :].astype(f32) * out_in_ref[here, :].astype(f32)
    deltas = [
        jnp.sum(product[:, h * HD : (h + 1) * HD], axis=1, keepdims=True) for h in range(heads)
    ]

    def window(begin, width):
        there = pl.ds(begin, width)
        same = seg_col_ref[here, :] == seg_row_ref[:, there]
        q_all = qkv_ref[here, :inner] * jnp.asarray(HD**-0.5, bf16)
        d_queries = []
        for h in range(heads):
            lo = h * HD
            keys = qkv_ref[there, inner + lo : inner + lo + HD]
            values = qkv_ref[there, 2 * inner + lo : 2 * inner + lo + HD]
            grads = grad_ref[here, lo : lo + HD]
            queries = q_all[:, lo : lo + HD]
            bias = jnp.concatenate(
                [
                    strip_ref[h, :, strip_at(step, u, parts, begin, width, length)]
                    for u in range(parts)
                ],
                axis=0,
            )
            scores = mm(queries, keys, NT) + bias - lse_ref[:, h : h + 1]
            probs = jnp.exp(jnp.where(same, scores, -1e9))
            d_values_ref[lo : lo + HD, there] += mm(grads, probs.astype(bf16), TN)
            d_scores = probs * (mm(grads, values, NT) - deltas[h])
            for u in range(parts):
                span = strip_at(step, u, parts, begin, width, length)
                d_strip_ref[h, :, span] += d_scores[u * SUB : (u + 1) * SUB]
            d_raw = d_scores.astype(bf16)
            d_queries.append(mm(d_raw, keys) * HD**-0.5)
            d_keys_ref[lo : lo + HD, there] += mm(queries, d_raw, TN)
        out_ref[here, :inner] = jnp.concatenate(d_queries, axis=1).astype(bf16)

    each_window(ids_ref, step, rows, length, window)

    @pl.when(step == pl.num_programs(0) - 1)
    def _():
        for h in range(heads):
            lo = h * HD
            out_ref[:, inner + lo : inner + lo + HD] = d_keys_ref[lo : lo + HD, :].T.astype(bf16)
            out_ref[:, 2 * inner + lo : 2 * inner + lo + HD] = d_values_ref[
                lo : lo + HD, :
            ].T.astype(bf16)
            summed = jnp.concatenate([d_strip_ref[h], jnp.zeros((SUB, SUB), f32)], axis=1)
            count = SUB
            while count > 1:
                count //= 2
                summed = summed[count:] + pltpu.roll(summed[:count], count, 1)
            d_table_ref[h : h + 1, :] = summed


def attend_backward(qkv, head_out, d_head, lse, table, segments, heads):
    length = qkv.shape[0]
    rows = min(256, length)
    inner = heads * HD
    return pl.pallas_call(
        partial(backward_kernel, rows=rows, heads=heads),
        grid_spec=pltpu.PrefetchScalarGridSpec(
            num_scalar_prefetch=1,
            grid=(length // rows,),
            in_specs=[
                whole(qkv.shape),
                whole(head_out.shape),
                whole(d_head.shape),
                pl.BlockSpec((rows, SUB), lambda i, ids: (i, 0)),
                whole(table.shape),
                whole((length, 1)),
                whole((1, length)),
            ],
            out_specs=[whole(qkv.shape), whole(table.shape)],
            scratch_shapes=[
                pltpu.VMEM((heads, SUB, 2 * length - SUB), f32),
                pltpu.VMEM((heads, SUB, 2 * length - SUB), f32),
                pltpu.VMEM((inner, length), f32),
                pltpu.VMEM((inner, length), f32),
            ],
        ),
        out_shape=[
            jax.ShapeDtypeStruct(qkv.shape, bf16),
            jax.ShapeDtypeStruct(table.shape, f32),
        ],
        compiler_params=pltpu.CompilerParams(vmem_limit_bytes=48 * 1024 * 1024),
        cost_estimate=pl.CostEstimate(
            flops=10 * length * length * inner,
            bytes_accessed=16 * length * inner,
            transcendentals=length * length * heads,
        ),
        name="attend_backward",
    )(segments, qkv, head_out, d_head, lse, table, segments[:, None], segments[None, :])


def joined(block_ref, at):
    rows, cols, _, slots, half = block_ref.shape
    return jnp.concatenate(
        [
            jnp.concatenate([block_ref[at ^ j, c, 0] for c in range(cols)], axis=1)
            for j in range(rows)
        ],
        axis=0,
    )


def halves(own, other, col):
    return jnp.where(
        col == 0,
        jnp.concatenate([own, other], axis=1),
        jnp.concatenate([other, own], axis=1),
    )


def flat(block):
    return block.reshape(-1, block.shape[-1]).astype(f32)


GELU_A = 0.7978845608028654
GELU_B = 0.044715


def gelu_pair(u):
    square = u * u
    factor = 0.5 * jnp.tanh(u * (GELU_A + (GELU_A * GELU_B) * square)) + 0.5
    value = u * factor
    slope = factor + value * (1.0 - factor) * (2 * GELU_A + (6 * GELU_A * GELU_B) * square)
    return value, slope


def router_probs(x, router_ref):
    weights = router_ref[...]
    high = weights.astype(bf16)
    low = (weights - high.astype(f32)).astype(bf16)
    logits = mm(x, high) + mm(x, low)
    exped = jnp.exp(logits - jnp.max(logits, axis=1, keepdims=True))
    return exped / jnp.sum(exped, axis=1, keepdims=True)


def gate(probs, expert):
    picked = lax.broadcasted_iota(jnp.int32, probs.shape, 1) == expert
    return picked, jnp.sum(jnp.where(picked, probs, 0.0), axis=1, keepdims=True)


def expert_kernel(
    at_ref,
    x_in_ref,
    own_ref,
    other_ref,
    router_ref,
    up_ref,
    down_ref,
    out_ref,
    grad_ref,
    d_router_ref,
    x_ref,
    g_ref,
    scaled_ref,
    probs_ref,
    out_acc_ref,
    grad_acc_ref,
):
    expert = pl.program_id(0)
    step = pl.program_id(1)
    col = at_ref[1]
    row = at_ref[2]
    first = at_ref[3]

    @pl.when(step == 0)
    def _():
        x = joined(x_in_ref, row)
        probs = router_probs(x, router_ref)
        _, gating = gate(probs, first + expert)
        g = halves(flat(own_ref[:, 0, 0]), flat(other_ref[:, 0, 0]), col)
        x_ref[...] = x
        g_ref[...] = g
        scaled_ref[...] = (gating * g).astype(bf16)
        probs_ref[...] = probs
        out_acc_ref[...] = jnp.zeros_like(out_acc_ref)
        grad_acc_ref[...] = jnp.zeros_like(grad_acc_ref)

    parts = 3
    tile = up_ref.shape[1] // parts
    activated, d_pre = [], []
    for i in range(parts):
        here = slice(i * tile, (i + 1) * tile)
        value, slope = gelu_pair(mm(x_ref[...], up_ref[0, here], NT))
        activated.append(value.astype(bf16))
        d_pre.append((mm(scaled_ref[...], down_ref[0, here], NT) * slope).astype(bf16))
    out_acc_ref[...] += mm(jnp.concatenate(activated, axis=1), down_ref[0])
    grad_acc_ref[...] += mm(jnp.concatenate(d_pre, axis=1), up_ref[0])

    @pl.when(step == pl.num_programs(1) - 1)
    def _():
        out = out_acc_ref[...]
        probs = probs_ref[...]
        picked, gating = gate(probs, first + expert)
        d_gating = jnp.sum(g_ref[...] * out, axis=1, keepdims=True)
        d_logits = d_gating * probs * (picked.astype(f32) - gating)
        grad = grad_acc_ref[...] + lax.dot_general(
            d_logits, router_ref[...], NT, precision=highest, preferred_element_type=f32
        )
        d_router = lax.dot_general(
            d_logits,
            x_ref[...].astype(f32),
            TN,
            precision=highest,
            preferred_element_type=f32,
        )
        rows, cols, _, slots, half = grad_ref.shape
        out = out.astype(bf16)
        grad = grad.astype(bf16)
        first_half, last_half = out[:, :half], out[:, half:]
        own = jnp.where(col == 0, first_half, last_half)
        other = jnp.where(col == 0, last_half, first_half)
        out_ref[:, 0, 0] = own.reshape(rows, slots, half)
        out_ref[:, 1, 0] = other.reshape(rows, slots, half)
        for j in range(rows):
            for c in range(cols):
                grad_ref[row ^ j, c, 0] = grad[
                    j * slots : (j + 1) * slots, c * half : (c + 1) * half
                ]

        @pl.when(expert == 0)
        def _():
            d_router_ref[...] = d_router

        @pl.when(expert > 0)
        def _():
            d_router_ref[...] += d_router


def run_experts(at, got_x, g_own, g_other, w_router, w_up, w_down):
    rows, cols, experts, slots, half = got_x.shape
    hidden, width = w_up.shape[1:]
    tile = 768
    block = pl.BlockSpec((rows, cols, 1, slots, half), lambda e, f, at: (0, 0, e, 0, 0))
    part = pl.BlockSpec((rows, 1, 1, slots, half), lambda e, f, at: (0, 0, e, 0, 0))
    last = pl.BlockSpec((rows, 1, 1, slots, half), lambda e, f, at: (0, 1, e, 0, 0))
    weight = pl.BlockSpec((1, tile, width), lambda e, f, at: (e, f, 0))
    tokens = rows * slots
    shape = jax.ShapeDtypeStruct(got_x.shape, bf16)
    router_shape = (w_router.shape[1], width)
    return pl.pallas_call(
        expert_kernel,
        grid_spec=pltpu.PrefetchScalarGridSpec(
            num_scalar_prefetch=1,
            grid=(experts, hidden // tile),
            in_specs=[block, part, last, whole(w_router.shape), weight, weight],
            out_specs=[block, block, whole(router_shape)],
            scratch_shapes=[
                pltpu.VMEM((tokens, width), bf16),
                pltpu.VMEM((tokens, width), f32),
                pltpu.VMEM((tokens, width), bf16),
                pltpu.VMEM((tokens, w_router.shape[1]), f32),
                pltpu.VMEM((tokens, width), f32),
                pltpu.VMEM((tokens, width), f32),
            ],
        ),
        out_shape=[shape, shape, jax.ShapeDtypeStruct(router_shape, f32)],
        compiler_params=pltpu.CompilerParams(vmem_limit_bytes=56 * 1024 * 1024),
        cost_estimate=pl.CostEstimate(
            flops=8 * experts * tokens * hidden * width,
            bytes_accessed=4 * experts * hidden * width,
            transcendentals=experts * tokens * hidden,
        ),
        name="experts",
    )(at, got_x, g_own, g_other, w_router, w_up, w_down)


def weight_kernel(
    at_ref, x_in_ref, own_ref, other_ref, router_ref, up_ref, down_ref, d_up_ref, d_down_ref
):
    expert = pl.program_id(0)
    step = pl.program_id(1)
    parts = x_in_ref.shape[0]
    x = jnp.concatenate([joined(x_in_ref.at[i], at_ref[2]) for i in range(parts)], axis=0)
    g = halves(flat(own_ref[:, :, 0, 0]), flat(other_ref[:, :, 0, 0]), at_ref[1])
    _, gating = gate(router_probs(x, router_ref), at_ref[3] + expert)
    g = (gating * g).astype(bf16)
    x_turned, g_turned = x.T, g.T
    own = up_ref.shape[1]
    tile = own // 3 if own % 768 == 0 else own
    for i in range(own // tile):
        here = slice(i * tile, (i + 1) * tile)
        value, slope = gelu_pair(mm(up_ref[0, here], x_turned))
        d_pre = (mm(down_ref[0, here], g_turned) * slope).astype(bf16)
        d_down = mm(value.astype(bf16), g)
        d_up = mm(d_pre, x)

        @pl.when(step == 0)
        def _():
            d_up_ref[0, here] = d_up
            d_down_ref[0, here] = d_down

        @pl.when(step > 0)
        def _():
            d_up_ref[0, here] += d_up
            d_down_ref[0, here] += d_down


def weight_grads(at, all_x, g_own, g_other, w_router, w_up, w_down):
    parts, rows, cols, experts, slots, half = all_x.shape
    hidden, width = w_up.shape[1:]
    own = hidden // parts
    each = min(4, parts)
    block = pl.BlockSpec((each, rows, cols, 1, slots, half), lambda e, n, at: (n, 0, 0, e, 0, 0))
    part = pl.BlockSpec((each, rows, 1, 1, slots, half), lambda e, n, at: (n, 0, 0, e, 0, 0))
    last = pl.BlockSpec((each, rows, 1, 1, slots, half), lambda e, n, at: (n, 0, 1, e, 0, 0))
    weight = pl.BlockSpec((1, own, width), lambda e, n, at: (e, at[0], 0))
    result = pl.BlockSpec((1, own, width), lambda e, n, at: (e, 0, 0))
    shape = jax.ShapeDtypeStruct((experts, own, width), f32)
    return pl.pallas_call(
        weight_kernel,
        grid_spec=pltpu.PrefetchScalarGridSpec(
            num_scalar_prefetch=1,
            grid=(experts, parts // each),
            in_specs=[block, part, last, whole(w_router.shape), weight, weight],
            out_specs=[result, result],
        ),
        out_shape=[shape, shape],
        compiler_params=pltpu.CompilerParams(vmem_limit_bytes=56 * 1024 * 1024),
        cost_estimate=pl.CostEstimate(
            flops=8 * experts * parts * rows * slots * own * width,
            bytes_accessed=12 * experts * own * width + 4 * all_x.size,
            transcendentals=experts * parts * rows * slots * own,
        ),
        name="weight_grads",
    )(at, all_x, g_own, g_other, w_router, w_up, w_down)


def pairs_out(k):
    return [
        (r * 2 + c, ((2 * (r % 2) + c) ^ k) * 2 + r // 2) for r in range(4) for c in range(2)
    ]


def pairs_home(k):
    return [(b, a) for a, b in pairs_out(k)]


def blocks_home(x):
    return [
        (r * 2 + s, (2 * s + ((r // 2) ^ x)) * 2 + r % 2) for r in range(4) for s in range(2)
    ]


def swap_col(array):
    return lax.ppermute(array, "col", [(0, 1), (1, 0)])


def shift(array, axis, bits):
    if bits == 0:
        return array
    count = lax.axis_size(axis)
    return lax.ppermute(array, axis, [(i, i ^ bits) for i in range(count)])


def total_over(array, axis):
    count = lax.axis_size(axis)
    stride = 1
    while stride < count:
        if 4 * stride <= count:
            near, far, last = (shift(array, axis, stride * i) for i in (1, 2, 3))
            array = (array + near) + (far + last)
            stride *= 4
        else:
            array = array + shift(array, axis, stride)
            stride *= 2
    return array


def shards(
    layer_in,
    w_qkv,
    w_proj,
    rel_bias,
    rel_bucket,
    segment_ids,
    gain_attn,
    gain_ffn,
    w_router,
    routes,
    w_up,
    w_down,
    d_layer,
):
    row_count = lax.axis_size("row")
    col_count = lax.axis_size("col")
    dp_count = lax.axis_size("dp")
    dp_at = lax.axis_index("dp")
    row_at = lax.axis_index("row")
    col_at = lax.axis_index("col")
    tok_dev, width = layer_in.shape
    slot_count = max(2, tok_dev // 8)
    half_width = width // col_count
    quarter = tok_dev // 2
    length = segment_ids.shape[1]
    inner = w_qkv.shape[2]
    heads_dev = inner // HD
    experts_all = EXP_DEV * row_count * col_count
    home = 2 * (row_at % 2) + col_at
    is_first = col_at == 0

    def both_halves(mine, other, axis):
        return jnp.where(
            is_first,
            jnp.concatenate([mine, other], axis),
            jnp.concatenate([other, mine], axis),
        )

    def my_half(array, axis):
        size = array.shape[axis] // 2
        return lax.dynamic_slice_in_dim(array, col_at * size, size, axis)

    def other_half(array, axis):
        size = array.shape[axis] // 2
        return lax.dynamic_slice_in_dim(array, (1 - col_at) * size, size, axis)

    def own_first(array, axis):
        return jnp.concatenate([my_half(array, axis), other_half(array, axis)], axis)

    def in_order(chunks, at):
        stacked = jnp.stack(chunks)
        return jnp.concatenate(
            [lax.dynamic_index_in_dim(stacked, i ^ at, 0, False) for i in range(len(chunks))], 0
        )

    own_tokens = my_half(layer_in, 0)
    token_parts = [lax.ppermute(own_tokens, group, pairs_out(k)) for k in range(row_count)]
    w_pair = both_halves(w_qkv, swap_col(w_qkv), 1)

    me = row_at * col_count + col_at
    first = me * EXP_DEV
    at = jnp.stack([dp_at, col_at, row_at, first])
    routed = routes[:, 0]
    chosen = routed[:, None] == jnp.arange(experts_all, dtype=jnp.int32)[None, :]
    counts = jnp.cumsum(chosen.astype(jnp.int32), axis=0)
    slot_index = jnp.sum(jnp.where(chosen, counts, 0), axis=-1) - 1
    slots_all = experts_all * slot_count
    slots_dev = EXP_DEV * slot_count
    send_shape = (row_count * col_count, EXP_DEV, slot_count, half_width)
    block_shape = (row_count, col_count, EXP_DEV, slot_count, half_width)

    def one_hot(devices):
        placed = (devices * EXP_DEV + routed % EXP_DEV) * slot_count + slot_index
        slots = jnp.arange(slots_all, dtype=jnp.int32)[:, None]
        return (slots == placed[None, :]).astype(bf16)

    placing = one_hot(routed // EXP_DEV)
    placing_near = one_hot((routed // EXP_DEV) ^ me)

    def all_to_all(array):
        return lax.all_to_all(array, group, split_axis=0, concat_axis=0, tiled=True)

    g_slots = mm(placing_near, d_layer).astype(bf16)
    g_slots = g_slots.reshape(row_count, col_count * slots_dev, half_width)
    early = [jnp.concatenate([w_proj, g_slots[j]], axis=0) for j in range(row_count)]
    token_parts[0], early = lax.optimization_barrier((token_parts[0], early))
    early = [shift(early[j], "row", j) for j in range(row_count)]
    gains = own_first(gain_ffn, 0)
    router = own_first(w_router, 0)
    input_near = own_first(layer_in, 1).astype(f32)

    tokens_seq = in_order(token_parts, row_at).astype(f32)
    w_all = jnp.concatenate([w_pair[0], w_pair[1], w_pair[2]], axis=1)
    scale_seq = lax.rsqrt(jnp.mean(tokens_seq * tokens_seq, axis=-1, keepdims=True) + epsilon)
    normed = (tokens_seq * scale_seq * gain_attn).astype(bf16)
    qkv = mm(normed, w_all).astype(bf16)

    buckets = (rel_bucket[:, None] == jnp.arange(NB, dtype=jnp.int32)[None, :]).astype(f32)
    bias_rows = lax.dynamic_slice_in_dim(rel_bias, row_at * heads_dev, heads_dev, 0)
    bias_table = jnp.einsum("hb,ob->ho", bias_rows, buckets, precision=highest)
    table = jnp.pad(bias_table, ((0, 0), (0, 1)))
    segments = segment_ids[0]

    g_near = jnp.stack([part[inner:] for part in early]).reshape(block_shape)
    proj_own = jnp.stack([part[:inner] for part in early])
    proj_own = jnp.concatenate(
        [
            lax.dynamic_index_in_dim(proj_own, row_at ^ home ^ k, 0, False)
            for k in range(row_count)
        ],
        axis=0,
    )
    qkv, g_near, proj_own, d_layer_late = lax.optimization_barrier(
        (qkv, g_near, proj_own, d_layer)
    )
    head_out, lse = attend_forward(qkv, table, segments, heads_dev)

    head_blocks = head_out.reshape(2, tok_dev, inner)
    head_parts = [
        lax.ppermute(
            lax.dynamic_index_in_dim(head_blocks, (row_at ^ k) // 2, 0, False),
            group,
            pairs_home(k),
        )
        for k in range(row_count)
    ]

    all_g = lax.all_gather(g_near, "dp", axis=0, tiled=False)
    proj_other = swap_col(proj_own).reshape(row_count, inner, half_width)
    proj_other = jnp.concatenate([proj_other[k ^ 1] for k in range(row_count)], axis=0)
    proj_all = jnp.concatenate([proj_own, proj_other], axis=1)
    g_other = swap_col(g_near)
    grads_in = jnp.concatenate([d_layer_late, swap_col(d_layer_late)], axis=1).astype(f32)

    heads = jnp.concatenate(head_parts, axis=1)
    middle = input_near + mm(heads, proj_all)
    scale_ffn = lax.rsqrt(jnp.mean(middle * middle, axis=-1, keepdims=True) + epsilon)
    hidden = middle * scale_ffn * gains
    x_slots = mm(placing, hidden[:, :half_width].astype(bf16)).astype(bf16).reshape(send_shape)
    got_x = all_to_all(x_slots)
    all_x = lax.all_gather(got_x, "dp", axis=0, tiled=False)
    out_slots, grad_slots, d_router = run_experts(
        at, got_x.reshape(block_shape), g_near, g_other, w_router, w_up, w_down
    )
    got_grad = all_to_all(grad_slots.reshape(send_shape)).reshape(slots_all, half_width)
    mine = mm(placing, got_grad, TN).astype(bf16)
    d_hidden = jnp.concatenate([mine, swap_col(mine)], axis=1).astype(f32)
    d_gain_ffn = 0.5 * both_halves(
        jnp.sum((middle * scale_ffn * d_hidden)[:, :half_width], axis=0),
        jnp.sum((middle * scale_ffn * d_hidden)[:, half_width:], axis=0),
        0,
    )
    scaled_ffn = d_hidden * gains
    d_middle = (
        grads_in
        + scale_ffn * scaled_ffn
        - middle * scale_ffn**3 * jnp.mean(scaled_ffn * middle, axis=-1, keepdims=True)
    )
    d_attn = d_middle.astype(bf16)
    d_heads = mm(my_half(d_attn, 0), proj_all, NT).astype(bf16)
    d_head = in_order(
        [
            lax.ppermute(d_heads[:, k * inner : (k + 1) * inner], group, pairs_out(k))
            for k in range(row_count)
        ],
        row_at,
    )

    d_attn_late, out_late, d_heads = lax.optimization_barrier((d_attn, out_slots, d_heads))
    d_proj = mm(heads, d_attn_late[:, :half_width], TN).astype(bf16)
    d_proj = d_proj.reshape(row_count, inner, half_width)
    out_late, d_proj, d_head = lax.optimization_barrier((out_late, d_proj, d_head))
    out_parts = [shift(out_late[j], "row", j) for j in range(row_count)]
    proj_parts = [
        shift(lax.dynamic_index_in_dim(d_proj, home ^ row_at ^ j, 0, False), "row", j)
        for j in range(row_count)
    ]

    d_qkv, d_table = attend_backward(qkv, head_out, d_head, lse, table, segments, heads_dev)

    out_parts, proj_parts, d_qkv, all_x, all_g = lax.optimization_barrier(
        (out_parts, proj_parts, d_qkv, all_x, all_g)
    )
    all_g_other = swap_col(all_g)
    part_normed = mm(d_qkv, w_all, NT).astype(bf16).reshape(2, tok_dev, width)
    part_normed, d_qkv = lax.optimization_barrier((part_normed, d_qkv))
    d_w = mm(normed, d_qkv, TN)
    d_w_other = swap_col(other_half(d_w, 0).astype(bf16))
    gain_part = jnp.sum(d_w * w_all.astype(f32), axis=1) / gain_attn
    d_rel_part = jnp.einsum("ho,ob->hb", d_table[:, : 2 * length - 1], buckets, precision=highest)
    rel_whole = lax.dynamic_update_slice_in_dim(
        jnp.zeros((H, NB), f32), d_rel_part, row_at * heads_dev, 0
    )
    rel_row = jnp.pad(rel_whole.reshape(1, H * NB), ((0, 0), (0, width - H * NB)))
    small = jnp.concatenate([d_router, d_gain_ffn[None], gain_part[None], rel_row], axis=0)
    small = total_over(total_over(small, "col"), "row")
    small = jnp.pad(small, ((0, -small.shape[0] % 16), (0, 0)))

    normed_parts = [
        lax.ppermute(
            lax.dynamic_index_in_dim(part_normed, (row_at // 2) ^ x, 0, False),
            group,
            blocks_home(x),
        )
        for x in range(2)
    ]

    d_proj = sum(part.astype(f32) for part in proj_parts).reshape(half_width, inner)
    d_w = my_half(d_w, 0) + d_w_other.astype(f32)
    packed = jnp.concatenate([jnp.concatenate([d_w, d_proj], axis=1), small], axis=0)
    packed = packed.astype(bf16)
    summed = lax.psum(packed, "dp")

    at, packed = lax.optimization_barrier((at, packed))
    d_up, d_down = weight_grads(
        at,
        all_x.reshape((dp_count,) + block_shape),
        all_g,
        all_g_other,
        w_router,
        w_up,
        w_down,
    )
    hidden, normed_parts, out_parts, d_up, d_down = lax.optimization_barrier(
        (hidden, normed_parts, out_parts, d_up, d_down)
    )
    normed_sum = normed_parts[0].astype(f32) + normed_parts[1].astype(f32)
    normed_other = swap_col(other_half(normed_sum, 0).astype(bf16))
    gate_probs = jax.nn.softmax(jnp.dot(hidden, router, precision=highest), axis=-1)
    gating = jnp.sum(jnp.where(chosen, gate_probs, 0.0), axis=-1, keepdims=True)
    out_stack = jnp.stack(out_parts).reshape(row_count, col_count, slots_dev, half_width)
    out_other = swap_col(out_stack[:, 1])
    out_back = jnp.stack([out_stack[:, 0], out_other], axis=1).reshape(slots_all, half_width)
    layer_out = middle[:, :half_width] + gating * mm(placing_near, out_back, TN)
    d_normed = my_half(normed_sum, 0) + normed_other.astype(f32)
    own = own_tokens.astype(f32)
    scale_own = lax.rsqrt(jnp.mean(own * own, axis=-1, keepdims=True) + epsilon)
    scaled_attn = d_normed * gain_attn
    d_own = scale_own * scaled_attn - own * scale_own**3 * jnp.mean(
        scaled_attn * own, axis=-1, keepdims=True
    )
    d_middle_own = my_half(d_middle, 0)
    d_layer_in = both_halves(
        d_middle_own[:, :half_width] + my_half(d_own, 1),
        swap_col(d_middle_own[:, half_width:] + other_half(d_own, 1)),
        0,
    )
    summed, layer_out, d_layer_in = lax.optimization_barrier((summed, layer_out, d_layer_in))
    summed = summed.astype(f32)
    small = summed[half_width:]
    summed = summed[:half_width]
    d_w_qkv = jnp.stack([summed[:, i * inner : (i + 1) * inner] for i in range(3)])
    d_proj = summed[:, 3 * inner :].reshape(inner, half_width)
    d_w_router = small[:experts_all].T
    d_gain_ffn = small[experts_all]
    d_gain_attn = small[experts_all + 1]
    d_rel_bias = small[experts_all + 2, : H * NB].reshape(H, NB)
    return (
        layer_out,
        d_layer_in,
        d_w_qkv,
        d_proj,
        d_rel_bias,
        d_gain_attn,
        d_gain_ffn,
        d_w_router,
        d_up,
        d_down,
    )


def solution(mesh):
    placed = (
        P(("dp", "row"), None),
        P(None, "col", "row"),
        P("row", "col"),
        P(),
        P(),
        P(("dp", "col"), None),
        P(),
        P(),
        P(),
        P(("dp", "row"), None),
        P(("row", "col"), None, None),
        P(("row", "col"), None, None),
        P(("dp", "row"), "col"),
    )
    return jax.shard_map(
        shards,
        mesh=mesh,
        in_specs=placed,
        out_specs=(
            P(("dp", "row"), "col"),
            P(("dp", "row"), "col"),
            P(None, "col", "row"),
            P("row", "col"),
            P(),
            P(),
            P(),
            P(),
            P(("row", "col"), "dp", None),
            P(("row", "col"), "dp", None),
        ),
        check_vma=False,
    )
```

```python
from functools import partial

import jax
import jax.numpy as jnp
from jax import lax
from jax.experimental import pallas as pl
from jax.experimental.pallas import tpu as pltpu
from jax.sharding import PartitionSpec as P

H = 12
HD = 64
NB = 32
EXP_DEV = 2
SUB = 128

epsilon = 1e-06
highest = lax.Precision.HIGHEST
f32 = jnp.float32
bf16 = jnp.bfloat16
group = ("row", "col")

NT = (((1,), (1,)), ((), ()))
NN = (((1,), (0,)), ((), ()))
TN = (((0,), (0,)), ((), ()))


def mm(a, b, dims=NN):
    return lax.dot_general(a, b, dims, preferred_element_type=f32)


def fill_strip(table_ref, strip_ref):
    heads, _, span = strip_ref.shape
    for h in range(heads):
        rows = jnp.broadcast_to(table_ref[h : h + 1, :], (SUB, table_ref.shape[1]))
        rolled = pltpu.roll(rows, table_ref.shape[1] - (SUB - 1), 1, stride=1, stride_axis=0)
        strip_ref[h] = rolled[:, :span]


def strip_at(step, part, parts, keys_at, width, length):
    begin = length - SUB * (step * parts + part + 1) + keys_at
    return pl.ds(pl.multiple_of(begin, SUB), width)


def each_window(ids_ref, step, rows, length, body):
    tiles = length // rows
    first = ids_ref[step * rows]
    last = ids_ref[step * rows + rows - 1]
    lo = jnp.int32(0)
    hi = jnp.int32(0)
    for i in range(tiles):
        lo = lo + (ids_ref[i * rows + rows - 1] < first).astype(jnp.int32)
        hi = hi + (ids_ref[i * rows] <= last).astype(jnp.int32)
    count = hi - lo
    sizes = sorted({min(2, tiles), min(3, tiles), tiles})
    for i, size in enumerate(sizes):
        fits = count <= size if i == 0 else jnp.logical_and(count > sizes[i - 1], count <= size)

        @pl.when(fits)
        def _():
            begin = jnp.minimum(lo, tiles - size) * rows
            body(pl.multiple_of(begin, rows), size * rows)


def forward_kernel(
    ids_ref,
    qkv_ref,
    table_ref,
    seg_col_ref,
    seg_row_ref,
    out_ref,
    lse_ref,
    strip_ref,
    *,
    rows,
    heads,
):
    step = pl.program_id(0)
    length = qkv_ref.shape[0]
    inner = heads * HD
    parts = rows // SUB

    @pl.when(step == 0)
    def _():
        fill_strip(table_ref, strip_ref)

    here = pl.ds(pl.multiple_of(step * rows, rows), rows)

    def window(begin, width):
        there = pl.ds(begin, width)
        same = seg_col_ref[here, :] == seg_row_ref[:, there]
        q_all = qkv_ref[here, :inner] * jnp.asarray(HD**-0.5, bf16)
        lane = lax.broadcasted_iota(jnp.int32, lse_ref.shape, 1)
        lse = jnp.zeros(lse_ref.shape, f32)
        outs = []
        for h in range(heads):
            lo = h * HD
            keys = qkv_ref[there, inner + lo : inner + lo + HD]
            values = qkv_ref[there, 2 * inner + lo : 2 * inner + lo + HD]
            bias = jnp.concatenate(
                [
                    strip_ref[h, :, strip_at(step, u, parts, begin, width, length)]
                    for u in range(parts)
                ],
                axis=0,
            )
            scores = jnp.where(same, mm(q_all[:, lo : lo + HD], keys, NT) + bias, -1e9)
            top = jnp.max(scores, axis=1, keepdims=True)
            weights = jnp.exp(scores - top)
            total = jnp.sum(weights, axis=1, keepdims=True)
            outs.append(mm(weights.astype(bf16), values) / total)
            lse = jnp.where(lane == h, top + jnp.log(total), lse)
        out_ref[...] = jnp.concatenate(outs, axis=1).astype(bf16)
        lse_ref[...] = lse

    each_window(ids_ref, step, rows, length, window)


def whole(shape):
    return pl.BlockSpec(shape, lambda *_: (0,) * len(shape))


def attend_forward(qkv, table, segments, heads):
    length = qkv.shape[0]
    rows = min(256, length)
    inner = heads * HD
    return pl.pallas_call(
        partial(forward_kernel, rows=rows, heads=heads),
        grid_spec=pltpu.PrefetchScalarGridSpec(
            num_scalar_prefetch=1,
            grid=(length // rows,),
            in_specs=[
                whole(qkv.shape),
                whole(table.shape),
                whole((length, 1)),
                whole((1, length)),
            ],
            out_specs=[
                pl.BlockSpec((rows, inner), lambda i, ids: (i, 0)),
                pl.BlockSpec((rows, SUB), lambda i, ids: (i, 0)),
            ],
            scratch_shapes=[
                pltpu.VMEM((heads, SUB, 2 * length - SUB), f32),
            ],
        ),
        out_shape=[
            jax.ShapeDtypeStruct((length, inner), bf16),
            jax.ShapeDtypeStruct((length, SUB), f32),
        ],
        compiler_params=pltpu.CompilerParams(vmem_limit_bytes=40 * 1024 * 1024),
        cost_estimate=pl.CostEstimate(
            flops=4 * length * length * inner,
            bytes_accessed=10 * length * inner,
            transcendentals=length * length * heads,
        ),
        name="attend_forward",
    )(segments, qkv, table, segments[:, None], segments[None, :])


def backward_kernel(
    ids_ref,
    qkv_ref,
    out_in_ref,
    grad_ref,
    lse_ref,
    table_ref,
    seg_col_ref,
    seg_row_ref,
    out_ref,
    d_table_ref,
    strip_ref,
    d_strip_ref,
    d_keys_ref,
    d_values_ref,
    *,
    rows,
    heads,
):
    step = pl.program_id(0)
    length = qkv_ref.shape[0]
    inner = heads * HD
    parts = rows // SUB

    @pl.when(step == 0)
    def _():
        fill_strip(table_ref, strip_ref)
        d_strip_ref[...] = jnp.zeros_like(d_strip_ref)
        d_keys_ref[...] = jnp.zeros_like(d_keys_ref)
        d_values_ref[...] = jnp.zeros_like(d_values_ref)

    here = pl.ds(pl.multiple_of(step * rows, rows), rows)
    product = grad_ref[here, :].astype(f32) * out_in_ref[here, :].astype(f32)
    deltas = [
        jnp.sum(product[:, h * HD : (h + 1) * HD], axis=1, keepdims=True) for h in range(heads)
    ]

    def window(begin, width):
        there = pl.ds(begin, width)
        same = seg_col_ref[here, :] == seg_row_ref[:, there]
        q_all = qkv_ref[here, :inner] * jnp.asarray(HD**-0.5, bf16)
        d_queries = []
        for h in range(heads):
            lo = h * HD
            keys = qkv_ref[there, inner + lo : inner + lo + HD]
            values = qkv_ref[there, 2 * inner + lo : 2 * inner + lo + HD]
            grads = grad_ref[here, lo : lo + HD]
            queries = q_all[:, lo : lo + HD]
            bias = jnp.concatenate(
                [
                    strip_ref[h, :, strip_at(step, u, parts, begin, width, length)]
                    for u in range(parts)
                ],
                axis=0,
            )
            scores = mm(queries, keys, NT) + bias - lse_ref[:, h : h + 1]
            probs = jnp.exp(jnp.where(same, scores, -1e9))
            d_values_ref[lo : lo + HD, there] += mm(grads, probs.astype(bf16), TN)
            d_scores = probs * (mm(grads, values, NT) - deltas[h])
            for u in range(parts):
                span = strip_at(step, u, parts, begin, width, length)
                d_strip_ref[h, :, span] += d_scores[u * SUB : (u + 1) * SUB]
            d_raw = d_scores.astype(bf16)
            d_queries.append(mm(d_raw, keys) * HD**-0.5)
            d_keys_ref[lo : lo + HD, there] += mm(queries, d_raw, TN)
        out_ref[here, :inner] = jnp.concatenate(d_queries, axis=1).astype(bf16)

    each_window(ids_ref, step, rows, length, window)

    @pl.when(step == pl.num_programs(0) - 1)
    def _():
        for h in range(heads):
            lo = h * HD
            out_ref[:, inner + lo : inner + lo + HD] = d_keys_ref[lo : lo + HD, :].T.astype(bf16)
            out_ref[:, 2 * inner + lo : 2 * inner + lo + HD] = d_values_ref[
                lo : lo + HD, :
            ].T.astype(bf16)
            summed = jnp.concatenate([d_strip_ref[h], jnp.zeros((SUB, SUB), f32)], axis=1)
            count = SUB
            while count > 1:
                count //= 2
                summed = summed[count:] + pltpu.roll(summed[:count], count, 1)
            d_table_ref[h : h + 1, :] = summed


def attend_backward(qkv, head_out, d_head, lse, table, segments, heads):
    length = qkv.shape[0]
    rows = min(256, length)
    inner = heads * HD
    return pl.pallas_call(
        partial(backward_kernel, rows=rows, heads=heads),
        grid_spec=pltpu.PrefetchScalarGridSpec(
            num_scalar_prefetch=1,
            grid=(length // rows,),
            in_specs=[
                whole(qkv.shape),
                whole(head_out.shape),
                whole(d_head.shape),
                pl.BlockSpec((rows, SUB), lambda i, ids: (i, 0)),
                whole(table.shape),
                whole((length, 1)),
                whole((1, length)),
            ],
            out_specs=[whole(qkv.shape), whole(table.shape)],
            scratch_shapes=[
                pltpu.VMEM((heads, SUB, 2 * length - SUB), f32),
                pltpu.VMEM((heads, SUB, 2 * length - SUB), f32),
                pltpu.VMEM((inner, length), f32),
                pltpu.VMEM((inner, length), f32),
            ],
        ),
        out_shape=[
            jax.ShapeDtypeStruct(qkv.shape, bf16),
            jax.ShapeDtypeStruct(table.shape, f32),
        ],
        compiler_params=pltpu.CompilerParams(vmem_limit_bytes=48 * 1024 * 1024),
        cost_estimate=pl.CostEstimate(
            flops=10 * length * length * inner,
            bytes_accessed=16 * length * inner,
            transcendentals=length * length * heads,
        ),
        name="attend_backward",
    )(segments, qkv, head_out, d_head, lse, table, segments[:, None], segments[None, :])


def joined(block_ref, at):
    rows, cols, _, slots, half = block_ref.shape
    return jnp.concatenate(
        [
            jnp.concatenate([block_ref[at ^ j, c, 0] for c in range(cols)], axis=1)
            for j in range(rows)
        ],
        axis=0,
    )


def halves(own, other, col):
    return jnp.where(
        col == 0,
        jnp.concatenate([own, other], axis=1),
        jnp.concatenate([other, own], axis=1),
    )


def flat(block):
    return block.reshape(-1, block.shape[-1]).astype(f32)


GELU_A = 0.7978845608028654
GELU_B = 0.044715


def gelu_pair(u):
    square = u * u
    factor = 0.5 * jnp.tanh(u * (GELU_A + (GELU_A * GELU_B) * square)) + 0.5
    value = u * factor
    slope = factor + value * (1.0 - factor) * (2 * GELU_A + (6 * GELU_A * GELU_B) * square)
    return value, slope


def router_probs(x, router_ref):
    weights = router_ref[...]
    high = weights.astype(bf16)
    low = (weights - high.astype(f32)).astype(bf16)
    logits = mm(x, high) + mm(x, low)
    exped = jnp.exp(logits - jnp.max(logits, axis=1, keepdims=True))
    return exped / jnp.sum(exped, axis=1, keepdims=True)


def gate(probs, expert):
    picked = lax.broadcasted_iota(jnp.int32, probs.shape, 1) == expert
    return picked, jnp.sum(jnp.where(picked, probs, 0.0), axis=1, keepdims=True)


def expert_kernel(
    at_ref,
    x_in_ref,
    own_ref,
    other_ref,
    router_ref,
    up_ref,
    down_ref,
    out_ref,
    grad_ref,
    d_router_ref,
    x_ref,
    g_ref,
    scaled_ref,
    probs_ref,
    out_acc_ref,
    grad_acc_ref,
):
    expert = pl.program_id(0)
    step = pl.program_id(1)
    col = at_ref[1]
    row = at_ref[2]
    first = at_ref[3]

    @pl.when(step == 0)
    def _():
        x = joined(x_in_ref, row)
        probs = router_probs(x, router_ref)
        _, gating = gate(probs, first + expert)
        g = halves(flat(own_ref[:, 0, 0]), flat(other_ref[:, 0, 0]), col)
        x_ref[...] = x
        g_ref[...] = g
        scaled_ref[...] = (gating * g).astype(bf16)
        probs_ref[...] = probs
        out_acc_ref[...] = jnp.zeros_like(out_acc_ref)
        grad_acc_ref[...] = jnp.zeros_like(grad_acc_ref)

    parts = 3
    tile = up_ref.shape[1] // parts
    activated, d_pre = [], []
    for i in range(parts):
        here = slice(i * tile, (i + 1) * tile)
        value, slope = gelu_pair(mm(x_ref[...], up_ref[0, here], NT))
        activated.append(value.astype(bf16))
        d_pre.append((mm(scaled_ref[...], down_ref[0, here], NT) * slope).astype(bf16))
    out_acc_ref[...] += mm(jnp.concatenate(activated, axis=1), down_ref[0])
    grad_acc_ref[...] += mm(jnp.concatenate(d_pre, axis=1), up_ref[0])

    @pl.when(step == pl.num_programs(1) - 1)
    def _():
        out = out_acc_ref[...]
        probs = probs_ref[...]
        picked, gating = gate(probs, first + expert)
        d_gating = jnp.sum(g_ref[...] * out, axis=1, keepdims=True)
        d_logits = d_gating * probs * (picked.astype(f32) - gating)
        grad = grad_acc_ref[...] + lax.dot_general(
            d_logits, router_ref[...], NT, precision=highest, preferred_element_type=f32
        )
        d_router = lax.dot_general(
            d_logits,
            x_ref[...].astype(f32),
            TN,
            precision=highest,
            preferred_element_type=f32,
        )
        rows, cols, _, slots, half = grad_ref.shape
        out = out.astype(bf16)
        grad = grad.astype(bf16)
        first_half, last_half = out[:, :half], out[:, half:]
        own = jnp.where(col == 0, first_half, last_half)
        other = jnp.where(col == 0, last_half, first_half)
        out_ref[:, 0, 0] = own.reshape(rows, slots, half)
        out_ref[:, 1, 0] = other.reshape(rows, slots, half)
        for j in range(rows):
            for c in range(cols):
                grad_ref[row ^ j, c, 0] = grad[
                    j * slots : (j + 1) * slots, c * half : (c + 1) * half
                ]

        @pl.when(expert == 0)
        def _():
            d_router_ref[...] = d_router

        @pl.when(expert > 0)
        def _():
            d_router_ref[...] += d_router


def run_experts(at, got_x, g_own, g_other, w_router, w_up, w_down):
    rows, cols, experts, slots, half = got_x.shape
    hidden, width = w_up.shape[1:]
    tile = 768
    block = pl.BlockSpec((rows, cols, 1, slots, half), lambda e, f, at: (0, 0, e, 0, 0))
    part = pl.BlockSpec((rows, 1, 1, slots, half), lambda e, f, at: (0, 0, e, 0, 0))
    last = pl.BlockSpec((rows, 1, 1, slots, half), lambda e, f, at: (0, 1, e, 0, 0))
    weight = pl.BlockSpec((1, tile, width), lambda e, f, at: (e, f, 0))
    tokens = rows * slots
    shape = jax.ShapeDtypeStruct(got_x.shape, bf16)
    router_shape = (w_router.shape[1], width)
    return pl.pallas_call(
        expert_kernel,
        grid_spec=pltpu.PrefetchScalarGridSpec(
            num_scalar_prefetch=1,
            grid=(experts, hidden // tile),
            in_specs=[block, part, last, whole(w_router.shape), weight, weight],
            out_specs=[block, block, whole(router_shape)],
            scratch_shapes=[
                pltpu.VMEM((tokens, width), bf16),
                pltpu.VMEM((tokens, width), f32),
                pltpu.VMEM((tokens, width), bf16),
                pltpu.VMEM((tokens, w_router.shape[1]), f32),
                pltpu.VMEM((tokens, width), f32),
                pltpu.VMEM((tokens, width), f32),
            ],
        ),
        out_shape=[shape, shape, jax.ShapeDtypeStruct(router_shape, f32)],
        compiler_params=pltpu.CompilerParams(vmem_limit_bytes=56 * 1024 * 1024),
        cost_estimate=pl.CostEstimate(
            flops=8 * experts * tokens * hidden * width,
            bytes_accessed=4 * experts * hidden * width,
            transcendentals=experts * tokens * hidden,
        ),
        name="experts",
    )(at, got_x, g_own, g_other, w_router, w_up, w_down)


def weight_kernel(
    at_ref,
    x_in_ref,
    own_ref,
    other_ref,
    router_ref,
    up_ref,
    down_ref,
    d_up_ref,
    d_down_ref,
    x_ref,
    g_ref,
    x_turned_ref,
    g_turned_ref,
    *,
    steps,
):
    expert = pl.program_id(0)
    tile = pl.program_id(1)
    step = pl.program_id(2)
    parts = x_in_ref.shape[0]

    @pl.when(jnp.logical_or(tile == 0, steps > 1))
    def _():
        x = jnp.concatenate([joined(x_in_ref.at[i], at_ref[2]) for i in range(parts)], axis=0)
        g = halves(flat(own_ref[:, :, 0, 0]), flat(other_ref[:, :, 0, 0]), at_ref[1])
        _, gating = gate(router_probs(x, router_ref), at_ref[3] + expert)
        g = (gating * g).astype(bf16)
        x_ref[...] = x
        g_ref[...] = g
        x_turned_ref[...] = x.T
        g_turned_ref[...] = g.T

    value, slope = gelu_pair(mm(up_ref[0], x_turned_ref[...]))
    d_pre = (mm(down_ref[0], g_turned_ref[...]) * slope).astype(bf16)
    d_down = mm(value.astype(bf16), g_ref[...])
    d_up = mm(d_pre, x_ref[...])

    @pl.when(step == 0)
    def _():
        d_up_ref[0] = d_up
        d_down_ref[0] = d_down

    @pl.when(step > 0)
    def _():
        d_up_ref[0] += d_up
        d_down_ref[0] += d_down


def weight_grads(at, all_x, g_own, g_other, w_router, w_up, w_down):
    parts, rows, cols, experts, slots, half = all_x.shape
    hidden, width = w_up.shape[1:]
    own = hidden // parts
    tile = 256 if own % 256 == 0 else own
    tiles = own // tile
    each = min(4, parts)
    steps = parts // each
    tokens = each * rows * slots
    block = pl.BlockSpec(
        (each, rows, cols, 1, slots, half), lambda e, f, n, at: (n, 0, 0, e, 0, 0)
    )
    part = pl.BlockSpec(
        (each, rows, 1, 1, slots, half), lambda e, f, n, at: (n, 0, 0, e, 0, 0)
    )
    last = pl.BlockSpec(
        (each, rows, 1, 1, slots, half), lambda e, f, n, at: (n, 0, 1, e, 0, 0)
    )
    weight = pl.BlockSpec((1, tile, width), lambda e, f, n, at: (e, at[0] * tiles + f, 0))
    result = pl.BlockSpec((1, tile, width), lambda e, f, n, at: (e, f, 0))
    shape = jax.ShapeDtypeStruct((experts, own, width), f32)
    return pl.pallas_call(
        partial(weight_kernel, steps=steps),
        grid_spec=pltpu.PrefetchScalarGridSpec(
            num_scalar_prefetch=1,
            grid=(experts, tiles, steps),
            in_specs=[block, part, last, whole(w_router.shape), weight, weight],
            out_specs=[result, result],
            scratch_shapes=[
                pltpu.VMEM((tokens, width), bf16),
                pltpu.VMEM((tokens, width), bf16),
                pltpu.VMEM((width, tokens), bf16),
                pltpu.VMEM((width, tokens), bf16),
            ],
        ),
        out_shape=[shape, shape],
        compiler_params=pltpu.CompilerParams(vmem_limit_bytes=56 * 1024 * 1024),
        cost_estimate=pl.CostEstimate(
            flops=8 * experts * parts * rows * slots * own * width,
            bytes_accessed=12 * experts * own * width + 4 * all_x.size,
            transcendentals=experts * parts * rows * slots * own,
        ),
        name="weight_grads",
    )(at, all_x, g_own, g_other, w_router, w_up, w_down)


def pairs_out(k):
    return [
        (r * 2 + c, ((2 * (r % 2) + c) ^ k) * 2 + r // 2) for r in range(4) for c in range(2)
    ]


def pairs_home(k):
    return [(b, a) for a, b in pairs_out(k)]


def blocks_home(x):
    return [
        (r * 2 + s, (2 * s + ((r // 2) ^ x)) * 2 + r % 2) for r in range(4) for s in range(2)
    ]


def swap_col(array):
    return lax.ppermute(array, "col", [(0, 1), (1, 0)])


def shift(array, axis, bits):
    if bits == 0:
        return array
    count = lax.axis_size(axis)
    return lax.ppermute(array, axis, [(i, i ^ bits) for i in range(count)])


def total_over(array, axis):
    count = lax.axis_size(axis)
    stride = 1
    while stride < count:
        if 4 * stride <= count:
            near, far, last = (shift(array, axis, stride * i) for i in (1, 2, 3))
            array = (array + near) + (far + last)
            stride *= 4
        else:
            array = array + shift(array, axis, stride)
            stride *= 2
    return array


def shards(
    layer_in,
    w_qkv,
    w_proj,
    rel_bias,
    rel_bucket,
    segment_ids,
    gain_attn,
    gain_ffn,
    w_router,
    routes,
    w_up,
    w_down,
    d_layer,
):
    row_count = lax.axis_size("row")
    col_count = lax.axis_size("col")
    dp_count = lax.axis_size("dp")
    dp_at = lax.axis_index("dp")
    row_at = lax.axis_index("row")
    col_at = lax.axis_index("col")
    tok_dev, width = layer_in.shape
    slot_count = max(2, tok_dev // 8)
    half_width = width // col_count
    quarter = tok_dev // 2
    length = segment_ids.shape[1]
    inner = w_qkv.shape[2]
    heads_dev = inner // HD
    experts_all = EXP_DEV * row_count * col_count
    home = 2 * (row_at % 2) + col_at
    is_first = col_at == 0

    def both_halves(mine, other, axis):
        return jnp.where(
            is_first,
            jnp.concatenate([mine, other], axis),
            jnp.concatenate([other, mine], axis),
        )

    def my_half(array, axis):
        size = array.shape[axis] // 2
        return lax.dynamic_slice_in_dim(array, col_at * size, size, axis)

    def other_half(array, axis):
        size = array.shape[axis] // 2
        return lax.dynamic_slice_in_dim(array, (1 - col_at) * size, size, axis)

    def own_first(array, axis):
        return jnp.concatenate([my_half(array, axis), other_half(array, axis)], axis)

    def in_order(chunks, at):
        stacked = jnp.stack(chunks)
        return jnp.concatenate(
            [lax.dynamic_index_in_dim(stacked, i ^ at, 0, False) for i in range(len(chunks))], 0
        )

    own_tokens = my_half(layer_in, 0)
    token_parts = [lax.ppermute(own_tokens, group, pairs_out(k)) for k in range(row_count)]
    w_pair = both_halves(w_qkv, swap_col(w_qkv), 1)

    me = row_at * col_count + col_at
    first = me * EXP_DEV
    at = jnp.stack([dp_at, col_at, row_at, first])
    routed = routes[:, 0]
    chosen = routed[:, None] == jnp.arange(experts_all, dtype=jnp.int32)[None, :]
    counts = jnp.cumsum(chosen.astype(jnp.int32), axis=0)
    slot_index = jnp.sum(jnp.where(chosen, counts, 0), axis=-1) - 1
    slots_all = experts_all * slot_count
    slots_dev = EXP_DEV * slot_count
    send_shape = (row_count * col_count, EXP_DEV, slot_count, half_width)
    block_shape = (row_count, col_count, EXP_DEV, slot_count, half_width)

    def one_hot(devices):
        placed = (devices * EXP_DEV + routed % EXP_DEV) * slot_count + slot_index
        slots = jnp.arange(slots_all, dtype=jnp.int32)[:, None]
        return (slots == placed[None, :]).astype(bf16)

    placing = one_hot(routed // EXP_DEV)
    placing_near = one_hot((routed // EXP_DEV) ^ me)

    def all_to_all(array):
        return lax.all_to_all(array, group, split_axis=0, concat_axis=0, tiled=True)

    g_slots = mm(placing_near, d_layer).astype(bf16)
    g_slots = g_slots.reshape(row_count, col_count * slots_dev, half_width)
    g_send = [g_slots[j] for j in range(row_count)]
    token_parts[0], g_send = lax.optimization_barrier((token_parts[0], g_send))
    g_parts = [shift(g_send[j], "row", j) for j in range(row_count)]
    g_parts[1], w_proj = lax.optimization_barrier((g_parts[1], w_proj))
    w_proj_parts = [shift(w_proj, "row", j) for j in range(row_count)]
    gains = own_first(gain_ffn, 0)
    router = own_first(w_router, 0)
    input_near = own_first(layer_in, 1).astype(f32)

    tokens_seq = in_order(token_parts, row_at).astype(f32)
    w_all = jnp.concatenate([w_pair[0], w_pair[1], w_pair[2]], axis=1)
    scale_seq = lax.rsqrt(jnp.mean(tokens_seq * tokens_seq, axis=-1, keepdims=True) + epsilon)
    normed = (tokens_seq * scale_seq * gain_attn).astype(bf16)
    qkv = mm(normed, w_all).astype(bf16)

    buckets = (rel_bucket[:, None] == jnp.arange(NB, dtype=jnp.int32)[None, :]).astype(f32)
    bias_rows = lax.dynamic_slice_in_dim(rel_bias, row_at * heads_dev, heads_dev, 0)
    bias_table = jnp.einsum("hb,ob->ho", bias_rows, buckets, precision=highest)
    table = jnp.pad(bias_table, ((0, 0), (0, 1)))
    segments = segment_ids[0]

    g_near = jnp.stack(g_parts).reshape(block_shape)
    qkv, g_near, d_layer_late = lax.optimization_barrier((qkv, g_near, d_layer))
    head_out, lse = attend_forward(qkv, table, segments, heads_dev)

    head_blocks = head_out.reshape(2, tok_dev, inner)
    head_parts = [
        lax.ppermute(
            lax.dynamic_index_in_dim(head_blocks, (row_at ^ k) // 2, 0, False),
            group,
            pairs_home(k),
        )
        for k in range(row_count)
    ]

    all_g = lax.all_gather(g_near, "dp", axis=0, tiled=False)
    w_proj_parts, _ = lax.optimization_barrier((w_proj_parts, head_out))
    proj_own = jnp.stack(w_proj_parts)
    proj_own = jnp.concatenate(
        [
            lax.dynamic_index_in_dim(proj_own, row_at ^ home ^ k, 0, False)
            for k in range(row_count)
        ],
        axis=0,
    )
    proj_other = swap_col(proj_own).reshape(row_count, inner, half_width)
    proj_other = jnp.concatenate([proj_other[k ^ 1] for k in range(row_count)], axis=0)
    proj_all = jnp.concatenate([proj_own, proj_other], axis=1)
    g_other = swap_col(g_near)
    grads_in = jnp.concatenate([d_layer_late, swap_col(d_layer_late)], axis=1).astype(f32)

    heads = jnp.concatenate(head_parts, axis=1)
    middle = input_near + mm(heads, proj_all)
    scale_ffn = lax.rsqrt(jnp.mean(middle * middle, axis=-1, keepdims=True) + epsilon)
    hidden = middle * scale_ffn * gains
    x_slots = mm(placing, hidden[:, :half_width].astype(bf16)).astype(bf16).reshape(send_shape)
    got_x = all_to_all(x_slots)
    all_x = lax.all_gather(got_x, "dp", axis=0, tiled=False)
    out_slots, grad_slots, d_router = run_experts(
        at, got_x.reshape(block_shape), g_near, g_other, w_router, w_up, w_down
    )
    got_grad = all_to_all(grad_slots.reshape(send_shape)).reshape(slots_all, half_width)
    mine = mm(placing, got_grad, TN).astype(bf16)
    d_hidden = jnp.concatenate([mine, swap_col(mine)], axis=1).astype(f32)
    d_gain_ffn = 0.5 * both_halves(
        jnp.sum((middle * scale_ffn * d_hidden)[:, :half_width], axis=0),
        jnp.sum((middle * scale_ffn * d_hidden)[:, half_width:], axis=0),
        0,
    )
    scaled_ffn = d_hidden * gains
    d_middle = (
        grads_in
        + scale_ffn * scaled_ffn
        - middle * scale_ffn**3 * jnp.mean(scaled_ffn * middle, axis=-1, keepdims=True)
    )
    d_attn = d_middle.astype(bf16)
    d_heads = mm(my_half(d_attn, 0), proj_all, NT).astype(bf16)
    d_head = in_order(
        [
            lax.ppermute(d_heads[:, k * inner : (k + 1) * inner], group, pairs_out(k))
            for k in range(row_count)
        ],
        row_at,
    )

    d_attn_late, d_heads = lax.optimization_barrier((d_attn, d_heads))
    d_proj = mm(heads, d_attn_late[:, :half_width], TN).astype(bf16)
    d_proj = d_proj.reshape(row_count, inner, half_width)
    d_proj, d_head = lax.optimization_barrier((d_proj, d_head))
    proj_parts = [
        shift(lax.dynamic_index_in_dim(d_proj, home ^ row_at ^ j, 0, False), "row", j)
        for j in range(row_count)
    ]

    d_qkv, d_table = attend_backward(qkv, head_out, d_head, lse, table, segments, heads_dev)

    proj_parts, d_qkv, all_x, all_g = lax.optimization_barrier((proj_parts, d_qkv, all_x, all_g))
    all_g_other = swap_col(all_g)
    d_w = mm(normed, d_qkv, TN)
    d_w_other = swap_col(other_half(d_w, 0).astype(bf16))
    gain_part = jnp.sum(d_w * w_all.astype(f32), axis=1) / gain_attn
    d_rel_part = jnp.einsum("ho,ob->hb", d_table[:, : 2 * length - 1], buckets, precision=highest)
    rel_whole = lax.dynamic_update_slice_in_dim(
        jnp.zeros((H, NB), f32), d_rel_part, row_at * heads_dev, 0
    )
    rel_row = jnp.pad(rel_whole.reshape(1, H * NB), ((0, 0), (0, width - H * NB)))
    small = jnp.concatenate([d_router, d_gain_ffn[None], gain_part[None], rel_row], axis=0)
    small = total_over(total_over(small, "col"), "row")
    small = jnp.pad(small, ((0, -small.shape[0] % 16), (0, 0)))

    d_proj = sum(part.astype(f32) for part in proj_parts).astype(bf16)
    d_w = (my_half(d_w, 0) + d_w_other.astype(f32)).astype(bf16)
    packed = (d_w, d_proj, small.astype(bf16))
    summed = lax.psum(packed, "dp")

    at, d_qkv, out_late, packed = lax.optimization_barrier((at, d_qkv, out_slots, packed))
    part_normed = mm(d_qkv, w_all, NT).astype(bf16).reshape(2, tok_dev, width)
    normed_parts = [
        lax.ppermute(
            lax.dynamic_index_in_dim(part_normed, (row_at // 2) ^ x, 0, False),
            group,
            blocks_home(x),
        )
        for x in range(2)
    ]
    out_parts = [shift(out_late[j], "row", j) for j in range(row_count)]
    at, part_normed = lax.optimization_barrier((at, part_normed))
    d_up, d_down = weight_grads(
        at,
        all_x.reshape((dp_count,) + block_shape),
        all_g,
        all_g_other,
        w_router,
        w_up,
        w_down,
    )
    hidden, normed_parts, out_parts, d_up, d_down = lax.optimization_barrier(
        (hidden, normed_parts, out_parts, d_up, d_down)
    )
    normed_sum = normed_parts[0].astype(f32) + normed_parts[1].astype(f32)
    normed_other = swap_col(other_half(normed_sum, 0).astype(bf16))
    gate_probs = jax.nn.softmax(jnp.dot(hidden, router, precision=highest), axis=-1)
    gating = jnp.sum(jnp.where(chosen, gate_probs, 0.0), axis=-1, keepdims=True)
    out_stack = jnp.stack(out_parts).reshape(row_count, col_count, slots_dev, half_width)
    out_other = swap_col(out_stack[:, 1])
    out_back = jnp.stack([out_stack[:, 0], out_other], axis=1).reshape(slots_all, half_width)
    layer_out = middle[:, :half_width] + gating * mm(placing_near, out_back, TN)
    d_normed = my_half(normed_sum, 0) + normed_other.astype(f32)
    own = own_tokens.astype(f32)
    scale_own = lax.rsqrt(jnp.mean(own * own, axis=-1, keepdims=True) + epsilon)
    scaled_attn = d_normed * gain_attn
    d_own = scale_own * scaled_attn - own * scale_own**3 * jnp.mean(
        scaled_attn * own, axis=-1, keepdims=True
    )
    d_middle_own = my_half(d_middle, 0)
    d_layer_in = both_halves(
        d_middle_own[:, :half_width] + my_half(d_own, 1),
        swap_col(d_middle_own[:, half_width:] + other_half(d_own, 1)),
        0,
    )
    summed, layer_out, d_layer_in = lax.optimization_barrier((summed, layer_out, d_layer_in))
    d_w, d_proj, small = (array.astype(f32) for array in summed)
    d_w_qkv = jnp.stack([d_w[:, i * inner : (i + 1) * inner] for i in range(3)])
    d_w_router = small[:experts_all].T
    d_gain_ffn = small[experts_all]
    d_gain_attn = small[experts_all + 1]
    d_rel_bias = small[experts_all + 2, : H * NB].reshape(H, NB)
    return (
        layer_out,
        d_layer_in,
        d_w_qkv,
        d_proj,
        d_rel_bias,
        d_gain_attn,
        d_gain_ffn,
        d_w_router,
        d_up,
        d_down,
    )


def solution(mesh):
    placed = (
        P(("dp", "row"), None),
        P(None, "col", "row"),
        P("row", "col"),
        P(),
        P(),
        P(("dp", "col"), None),
        P(),
        P(),
        P(),
        P(("dp", "row"), None),
        P(("row", "col"), None, None),
        P(("row", "col"), None, None),
        P(("dp", "row"), "col"),
    )
    return jax.shard_map(
        shards,
        mesh=mesh,
        in_specs=placed,
        out_specs=(
            P(("dp", "row"), "col"),
            P(("dp", "row"), "col"),
            P(None, "col", "row"),
            P("row", "col"),
            P(),
            P(),
            P(),
            P(),
            P(("row", "col"), "dp", None),
            P(("row", "col"), "dp", None),
        ),
        check_vma=False,
    )
```

```python
from functools import partial

import jax
import jax.numpy as jnp
from jax import lax
from jax.experimental import pallas as pl
from jax.experimental.pallas import tpu as pltpu
from jax.sharding import PartitionSpec as P

H = 12
HD = 64
NB = 32
EXP_DEV = 2
SUB = 128

epsilon = 1e-06
highest = lax.Precision.HIGHEST
f32 = jnp.float32
bf16 = jnp.bfloat16
group = ("row", "col")

NT = (((1,), (1,)), ((), ()))
NN = (((1,), (0,)), ((), ()))
TN = (((0,), (0,)), ((), ()))


def mm(a, b, dims=NN):
    return lax.dot_general(a, b, dims, preferred_element_type=f32)


def fill_strip(table_ref, strip_ref):
    heads, _, span = strip_ref.shape
    for h in range(heads):
        rows = jnp.broadcast_to(table_ref[h : h + 1, :], (SUB, table_ref.shape[1]))
        rolled = pltpu.roll(rows, table_ref.shape[1] - (SUB - 1), 1, stride=1, stride_axis=0)
        strip_ref[h] = rolled[:, :span]


def strip_at(step, part, parts, keys_at, width, length):
    begin = length - SUB * (step * parts + part + 1) + keys_at
    return pl.ds(pl.multiple_of(begin, SUB), width)


def each_window(ids_ref, step, rows, length, body):
    tiles = length // rows
    first = ids_ref[step * rows]
    last = ids_ref[step * rows + rows - 1]
    lo = jnp.int32(0)
    hi = jnp.int32(0)
    for i in range(tiles):
        lo = lo + (ids_ref[i * rows + rows - 1] < first).astype(jnp.int32)
        hi = hi + (ids_ref[i * rows] <= last).astype(jnp.int32)
    count = hi - lo
    sizes = sorted({min(2, tiles), min(3, tiles), tiles})
    for i, size in enumerate(sizes):
        fits = count <= size if i == 0 else jnp.logical_and(count > sizes[i - 1], count <= size)

        @pl.when(fits)
        def _():
            begin = jnp.minimum(lo, tiles - size) * rows
            body(pl.multiple_of(begin, rows), size * rows)


def forward_kernel(
    ids_ref,
    qkv_ref,
    table_ref,
    seg_col_ref,
    seg_row_ref,
    out_ref,
    lse_ref,
    strip_ref,
    *,
    rows,
    heads,
):
    step = pl.program_id(0)
    length = qkv_ref.shape[0]
    inner = heads * HD
    parts = rows // SUB

    @pl.when(step == 0)
    def _():
        fill_strip(table_ref, strip_ref)

    here = pl.ds(pl.multiple_of(step * rows, rows), rows)

    def window(begin, width):
        there = pl.ds(begin, width)
        same = seg_col_ref[here, :] == seg_row_ref[:, there]
        q_all = qkv_ref[here, :inner] * jnp.asarray(HD**-0.5, bf16)
        lane = lax.broadcasted_iota(jnp.int32, lse_ref.shape, 1)
        lse = jnp.zeros(lse_ref.shape, f32)
        outs = []
        for h in range(heads):
            lo = h * HD
            keys = qkv_ref[there, inner + lo : inner + lo + HD]
            values = qkv_ref[there, 2 * inner + lo : 2 * inner + lo + HD]
            bias = jnp.concatenate(
                [
                    strip_ref[h, :, strip_at(step, u, parts, begin, width, length)]
                    for u in range(parts)
                ],
                axis=0,
            )
            scores = jnp.where(same, mm(q_all[:, lo : lo + HD], keys, NT) + bias, -1e9)
            top = jnp.max(scores, axis=1, keepdims=True)
            weights = jnp.exp(scores - top)
            total = jnp.sum(weights, axis=1, keepdims=True)
            outs.append(mm(weights.astype(bf16), values) / total)
            lse = jnp.where(lane == h, top + jnp.log(total), lse)
        out_ref[...] = jnp.concatenate(outs, axis=1).astype(bf16)
        lse_ref[...] = lse

    each_window(ids_ref, step, rows, length, window)


def whole(shape):
    return pl.BlockSpec(shape, lambda *_: (0,) * len(shape))


def attend_forward(qkv, table, segments, heads):
    length = qkv.shape[0]
    rows = min(256, length)
    inner = heads * HD
    return pl.pallas_call(
        partial(forward_kernel, rows=rows, heads=heads),
        grid_spec=pltpu.PrefetchScalarGridSpec(
            num_scalar_prefetch=1,
            grid=(length // rows,),
            in_specs=[
                whole(qkv.shape),
                whole(table.shape),
                whole((length, 1)),
                whole((1, length)),
            ],
            out_specs=[
                pl.BlockSpec((rows, inner), lambda i, ids: (i, 0)),
                pl.BlockSpec((rows, SUB), lambda i, ids: (i, 0)),
            ],
            scratch_shapes=[
                pltpu.VMEM((heads, SUB, 2 * length - SUB), f32),
            ],
        ),
        out_shape=[
            jax.ShapeDtypeStruct((length, inner), bf16),
            jax.ShapeDtypeStruct((length, SUB), f32),
        ],
        compiler_params=pltpu.CompilerParams(vmem_limit_bytes=40 * 1024 * 1024),
        cost_estimate=pl.CostEstimate(
            flops=4 * length * length * inner,
            bytes_accessed=10 * length * inner,
            transcendentals=length * length * heads,
        ),
        name="attend_forward",
    )(segments, qkv, table, segments[:, None], segments[None, :])


def backward_kernel(
    ids_ref,
    qkv_ref,
    out_in_ref,
    grad_ref,
    lse_ref,
    table_ref,
    seg_col_ref,
    seg_row_ref,
    out_ref,
    d_table_ref,
    strip_ref,
    d_strip_ref,
    d_keys_ref,
    d_values_ref,
    *,
    rows,
    heads,
):
    step = pl.program_id(0)
    length = qkv_ref.shape[0]
    inner = heads * HD
    parts = rows // SUB

    @pl.when(step == 0)
    def _():
        fill_strip(table_ref, strip_ref)
        d_strip_ref[...] = jnp.zeros_like(d_strip_ref)
        d_keys_ref[...] = jnp.zeros_like(d_keys_ref)
        d_values_ref[...] = jnp.zeros_like(d_values_ref)

    here = pl.ds(pl.multiple_of(step * rows, rows), rows)
    product = grad_ref[here, :].astype(f32) * out_in_ref[here, :].astype(f32)
    deltas = [
        jnp.sum(product[:, h * HD : (h + 1) * HD], axis=1, keepdims=True) for h in range(heads)
    ]

    def window(begin, width):
        there = pl.ds(begin, width)
        same = seg_col_ref[here, :] == seg_row_ref[:, there]
        q_all = qkv_ref[here, :inner] * jnp.asarray(HD**-0.5, bf16)
        d_queries = []
        for h in range(heads):
            lo = h * HD
            keys = qkv_ref[there, inner + lo : inner + lo + HD]
            values = qkv_ref[there, 2 * inner + lo : 2 * inner + lo + HD]
            grads = grad_ref[here, lo : lo + HD]
            queries = q_all[:, lo : lo + HD]
            bias = jnp.concatenate(
                [
                    strip_ref[h, :, strip_at(step, u, parts, begin, width, length)]
                    for u in range(parts)
                ],
                axis=0,
            )
            scores = mm(queries, keys, NT) + bias - lse_ref[:, h : h + 1]
            probs = jnp.exp(jnp.where(same, scores, -1e9))
            d_values_ref[lo : lo + HD, there] += mm(grads, probs.astype(bf16), TN)
            d_scores = probs * (mm(grads, values, NT) - deltas[h])
            for u in range(parts):
                span = strip_at(step, u, parts, begin, width, length)
                d_strip_ref[h, :, span] += d_scores[u * SUB : (u + 1) * SUB]
            d_raw = d_scores.astype(bf16)
            d_queries.append(mm(d_raw, keys) * HD**-0.5)
            d_keys_ref[lo : lo + HD, there] += mm(queries, d_raw, TN)
        out_ref[here, :inner] = jnp.concatenate(d_queries, axis=1).astype(bf16)

    each_window(ids_ref, step, rows, length, window)

    @pl.when(step == pl.num_programs(0) - 1)
    def _():
        for h in range(heads):
            lo = h * HD
            out_ref[:, inner + lo : inner + lo + HD] = d_keys_ref[lo : lo + HD, :].T.astype(bf16)
            out_ref[:, 2 * inner + lo : 2 * inner + lo + HD] = d_values_ref[
                lo : lo + HD, :
            ].T.astype(bf16)
            summed = jnp.concatenate([d_strip_ref[h], jnp.zeros((SUB, SUB), f32)], axis=1)
            count = SUB
            while count > 1:
                count //= 2
                summed = summed[count:] + pltpu.roll(summed[:count], count, 1)
            d_table_ref[h : h + 1, :] = summed


def attend_backward(qkv, head_out, d_head, lse, table, segments, heads):
    length = qkv.shape[0]
    rows = min(256, length)
    inner = heads * HD
    return pl.pallas_call(
        partial(backward_kernel, rows=rows, heads=heads),
        grid_spec=pltpu.PrefetchScalarGridSpec(
            num_scalar_prefetch=1,
            grid=(length // rows,),
            in_specs=[
                whole(qkv.shape),
                whole(head_out.shape),
                whole(d_head.shape),
                pl.BlockSpec((rows, SUB), lambda i, ids: (i, 0)),
                whole(table.shape),
                whole((length, 1)),
                whole((1, length)),
            ],
            out_specs=[whole(qkv.shape), whole(table.shape)],
            scratch_shapes=[
                pltpu.VMEM((heads, SUB, 2 * length - SUB), f32),
                pltpu.VMEM((heads, SUB, 2 * length - SUB), f32),
                pltpu.VMEM((inner, length), f32),
                pltpu.VMEM((inner, length), f32),
            ],
        ),
        out_shape=[
            jax.ShapeDtypeStruct(qkv.shape, bf16),
            jax.ShapeDtypeStruct(table.shape, f32),
        ],
        compiler_params=pltpu.CompilerParams(vmem_limit_bytes=48 * 1024 * 1024),
        cost_estimate=pl.CostEstimate(
            flops=10 * length * length * inner,
            bytes_accessed=16 * length * inner,
            transcendentals=length * length * heads,
        ),
        name="attend_backward",
    )(segments, qkv, head_out, d_head, lse, table, segments[:, None], segments[None, :])


def joined(block_ref, at):
    rows, cols, _, slots, half = block_ref.shape
    return jnp.concatenate(
        [
            jnp.concatenate([block_ref[at ^ j, c, 0] for c in range(cols)], axis=1)
            for j in range(rows)
        ],
        axis=0,
    )


def halves(own, other, col):
    return jnp.where(
        col == 0,
        jnp.concatenate([own, other], axis=1),
        jnp.concatenate([other, own], axis=1),
    )


def flat(block):
    return block.reshape(-1, block.shape[-1]).astype(f32)


GELU_A = 0.7978845608028654
GELU_B = 0.044715


def gelu_pair(u):
    square = u * u
    factor = 0.5 * jnp.tanh(u * (GELU_A + (GELU_A * GELU_B) * square)) + 0.5
    value = u * factor
    slope = factor + value * (1.0 - factor) * (2 * GELU_A + (6 * GELU_A * GELU_B) * square)
    return value, slope


def router_probs(x, router_ref):
    weights = router_ref[...]
    high = weights.astype(bf16)
    low = (weights - high.astype(f32)).astype(bf16)
    logits = mm(x, high) + mm(x, low)
    exped = jnp.exp(logits - jnp.max(logits, axis=1, keepdims=True))
    return exped / jnp.sum(exped, axis=1, keepdims=True)


def gate(probs, expert):
    picked = lax.broadcasted_iota(jnp.int32, probs.shape, 1) == expert
    return picked, jnp.sum(jnp.where(picked, probs, 0.0), axis=1, keepdims=True)


def expert_kernel(
    at_ref,
    x_in_ref,
    own_ref,
    other_ref,
    router_ref,
    up_ref,
    down_ref,
    out_ref,
    grad_ref,
    d_router_ref,
    x_ref,
    g_ref,
    scaled_ref,
    probs_ref,
    out_acc_ref,
    grad_acc_ref,
):
    expert = pl.program_id(0)
    step = pl.program_id(1)
    col = at_ref[1]
    row = at_ref[2]
    first = at_ref[3]

    @pl.when(step == 0)
    def _():
        x = joined(x_in_ref, row)
        probs = router_probs(x, router_ref)
        _, gating = gate(probs, first + expert)
        g = halves(flat(own_ref[:, 0, 0]), flat(other_ref[:, 0, 0]), col)
        x_ref[...] = x
        g_ref[...] = g
        scaled_ref[...] = (gating * g).astype(bf16)
        probs_ref[...] = probs
        out_acc_ref[...] = jnp.zeros_like(out_acc_ref)
        grad_acc_ref[...] = jnp.zeros_like(grad_acc_ref)

    parts = 3
    tile = up_ref.shape[1] // parts
    activated, d_pre = [], []
    for i in range(parts):
        here = slice(i * tile, (i + 1) * tile)
        value, slope = gelu_pair(mm(x_ref[...], up_ref[0, here], NT))
        activated.append(value.astype(bf16))
        d_pre.append((mm(scaled_ref[...], down_ref[0, here], NT) * slope).astype(bf16))
    out_acc_ref[...] += mm(jnp.concatenate(activated, axis=1), down_ref[0])
    grad_acc_ref[...] += mm(jnp.concatenate(d_pre, axis=1), up_ref[0])

    @pl.when(step == pl.num_programs(1) - 1)
    def _():
        out = out_acc_ref[...]
        probs = probs_ref[...]
        picked, gating = gate(probs, first + expert)
        d_gating = jnp.sum(g_ref[...] * out, axis=1, keepdims=True)
        d_logits = d_gating * probs * (picked.astype(f32) - gating)
        grad = grad_acc_ref[...] + lax.dot_general(
            d_logits, router_ref[...], NT, precision=highest, preferred_element_type=f32
        )
        d_router = lax.dot_general(
            d_logits,
            x_ref[...].astype(f32),
            TN,
            precision=highest,
            preferred_element_type=f32,
        )
        rows, cols, _, slots, half = grad_ref.shape
        out = out.astype(bf16)
        grad = grad.astype(bf16)
        first_half, last_half = out[:, :half], out[:, half:]
        own = jnp.where(col == 0, first_half, last_half)
        other = jnp.where(col == 0, last_half, first_half)
        out_ref[:, 0, 0] = own.reshape(rows, slots, half)
        out_ref[:, 1, 0] = other.reshape(rows, slots, half)
        for j in range(rows):
            for c in range(cols):
                grad_ref[row ^ j, c, 0] = grad[
                    j * slots : (j + 1) * slots, c * half : (c + 1) * half
                ]

        @pl.when(expert == 0)
        def _():
            d_router_ref[...] = d_router

        @pl.when(expert > 0)
        def _():
            d_router_ref[...] += d_router


def run_experts(at, got_x, g_own, g_other, w_router, w_up, w_down):
    rows, cols, experts, slots, half = got_x.shape
    hidden, width = w_up.shape[1:]
    tile = 768
    block = pl.BlockSpec((rows, cols, 1, slots, half), lambda e, f, at: (0, 0, e, 0, 0))
    part = pl.BlockSpec((rows, 1, 1, slots, half), lambda e, f, at: (0, 0, e, 0, 0))
    last = pl.BlockSpec((rows, 1, 1, slots, half), lambda e, f, at: (0, 1, e, 0, 0))
    weight = pl.BlockSpec((1, tile, width), lambda e, f, at: (e, f, 0))
    tokens = rows * slots
    shape = jax.ShapeDtypeStruct(got_x.shape, bf16)
    router_shape = (w_router.shape[1], width)
    return pl.pallas_call(
        expert_kernel,
        grid_spec=pltpu.PrefetchScalarGridSpec(
            num_scalar_prefetch=1,
            grid=(experts, hidden // tile),
            in_specs=[block, part, last, whole(w_router.shape), weight, weight],
            out_specs=[block, block, whole(router_shape)],
            scratch_shapes=[
                pltpu.VMEM((tokens, width), bf16),
                pltpu.VMEM((tokens, width), f32),
                pltpu.VMEM((tokens, width), bf16),
                pltpu.VMEM((tokens, w_router.shape[1]), f32),
                pltpu.VMEM((tokens, width), f32),
                pltpu.VMEM((tokens, width), f32),
            ],
        ),
        out_shape=[shape, shape, jax.ShapeDtypeStruct(router_shape, f32)],
        compiler_params=pltpu.CompilerParams(vmem_limit_bytes=56 * 1024 * 1024),
        cost_estimate=pl.CostEstimate(
            flops=8 * experts * tokens * hidden * width,
            bytes_accessed=4 * experts * hidden * width,
            transcendentals=experts * tokens * hidden,
        ),
        name="experts",
    )(at, got_x, g_own, g_other, w_router, w_up, w_down)


def weight_kernel(
    at_ref,
    x_in_ref,
    own_ref,
    other_ref,
    router_ref,
    up_ref,
    down_ref,
    d_up_ref,
    d_down_ref,
    x_ref,
    g_ref,
    x_turned_ref,
    g_turned_ref,
    *,
    steps,
):
    expert = pl.program_id(0)
    tile = pl.program_id(1)
    step = pl.program_id(2)
    parts = x_in_ref.shape[0]

    @pl.when(jnp.logical_or(tile == 0, steps > 1))
    def _():
        x = jnp.concatenate([joined(x_in_ref.at[i], at_ref[2]) for i in range(parts)], axis=0)
        g = halves(flat(own_ref[:, :, 0, 0]), flat(other_ref[:, :, 0, 0]), at_ref[1])
        _, gating = gate(router_probs(x, router_ref), at_ref[3] + expert)
        g = (gating * g).astype(bf16)
        x_ref[...] = x
        g_ref[...] = g
        x_turned_ref[...] = x.T
        g_turned_ref[...] = g.T

    value, slope = gelu_pair(mm(up_ref[0], x_turned_ref[...]))
    d_pre = (mm(down_ref[0], g_turned_ref[...]) * slope).astype(bf16)
    d_down = mm(value.astype(bf16), g_ref[...])
    d_up = mm(d_pre, x_ref[...])

    @pl.when(step == 0)
    def _():
        d_up_ref[0] = d_up
        d_down_ref[0] = d_down

    @pl.when(step > 0)
    def _():
        d_up_ref[0] += d_up
        d_down_ref[0] += d_down


def weight_grads(at, all_x, g_own, g_other, w_router, w_up, w_down):
    parts, rows, cols, experts, slots, half = all_x.shape
    hidden, width = w_up.shape[1:]
    own = hidden // parts
    tile = 256 if own % 256 == 0 else own
    tiles = own // tile
    each = min(4, parts)
    steps = parts // each
    tokens = each * rows * slots
    block = pl.BlockSpec(
        (each, rows, cols, 1, slots, half), lambda e, f, n, at: (n, 0, 0, e, 0, 0)
    )
    part = pl.BlockSpec(
        (each, rows, 1, 1, slots, half), lambda e, f, n, at: (n, 0, 0, e, 0, 0)
    )
    last = pl.BlockSpec(
        (each, rows, 1, 1, slots, half), lambda e, f, n, at: (n, 0, 1, e, 0, 0)
    )
    weight = pl.BlockSpec((1, tile, width), lambda e, f, n, at: (e, at[0] * tiles + f, 0))
    result = pl.BlockSpec((1, tile, width), lambda e, f, n, at: (e, f, 0))
    shape = jax.ShapeDtypeStruct((experts, own, width), f32)
    return pl.pallas_call(
        partial(weight_kernel, steps=steps),
        grid_spec=pltpu.PrefetchScalarGridSpec(
            num_scalar_prefetch=1,
            grid=(experts, tiles, steps),
            in_specs=[block, part, last, whole(w_router.shape), weight, weight],
            out_specs=[result, result],
            scratch_shapes=[
                pltpu.VMEM((tokens, width), bf16),
                pltpu.VMEM((tokens, width), bf16),
                pltpu.VMEM((width, tokens), bf16),
                pltpu.VMEM((width, tokens), bf16),
            ],
        ),
        out_shape=[shape, shape],
        compiler_params=pltpu.CompilerParams(vmem_limit_bytes=56 * 1024 * 1024),
        cost_estimate=pl.CostEstimate(
            flops=8 * experts * parts * rows * slots * own * width,
            bytes_accessed=12 * experts * own * width + 4 * all_x.size,
            transcendentals=experts * parts * rows * slots * own,
        ),
        name="weight_grads",
    )(at, all_x, g_own, g_other, w_router, w_up, w_down)


def weights_first(r, c):
    return (r, 0) if c == 1 else (r ^ 2, 1)


def weights_second(r, c):
    return (r ^ 2, 1)


def grouped(array, route, cores):
    pairs = []
    for r in range(4):
        for c in cores:
            to_row, to_col = route(r, c)
            pairs.append((r * 2 + c, to_row * 2 + to_col))
    return lax.ppermute(array, group, pairs)


def grads_first(r, c):
    return (r, 1) if c == 0 else (r ^ 2, 0)


def swap_col(array):
    return lax.ppermute(array, "col", [(0, 1), (1, 0)])


def shift(array, axis, bits):
    if bits == 0:
        return array
    count = lax.axis_size(axis)
    return lax.ppermute(array, axis, [(i, i ^ bits) for i in range(count)])


def total_over(array, axis):
    count = lax.axis_size(axis)
    stride = 1
    while stride < count:
        if 4 * stride <= count:
            near, far, last = (shift(array, axis, stride * i) for i in (1, 2, 3))
            array = (array + near) + (far + last)
            stride *= 4
        else:
            array = array + shift(array, axis, stride)
            stride *= 2
    return array


def shards(
    layer_in,
    w_qkv,
    w_proj,
    rel_bias,
    rel_bucket,
    segment_ids,
    gain_attn,
    gain_ffn,
    w_router,
    routes,
    w_up,
    w_down,
    d_layer,
):
    row_count = lax.axis_size("row")
    col_count = lax.axis_size("col")
    dp_count = lax.axis_size("dp")
    dp_at = lax.axis_index("dp")
    row_at = lax.axis_index("row")
    col_at = lax.axis_index("col")
    tok_dev, width = layer_in.shape
    slot_count = max(2, tok_dev // 8)
    half_width = width // col_count
    length = segment_ids.shape[1]
    inner = w_qkv.shape[2]
    heads_dev = inner // HD
    experts_all = EXP_DEV * row_count * col_count
    block_at = row_at % 2
    heads_at = row_at ^ (2 * col_at)
    is_first = col_at == 0

    def both_halves(mine, other, axis):
        return jnp.where(
            is_first,
            jnp.concatenate([mine, other], axis),
            jnp.concatenate([other, mine], axis),
        )

    def my_half(array, axis):
        size = array.shape[axis] // 2
        return lax.dynamic_slice_in_dim(array, col_at * size, size, axis)

    def other_half(array, axis):
        size = array.shape[axis] // 2
        return lax.dynamic_slice_in_dim(array, (1 - col_at) * size, size, axis)

    def own_first(array, axis):
        return jnp.concatenate([my_half(array, axis), other_half(array, axis)], axis)

    def in_sequence(mine, other):
        return jnp.where(
            block_at == 0,
            jnp.concatenate([mine, other], axis=0),
            jnp.concatenate([other, mine], axis=0),
        )

    own_tokens = my_half(layer_in, 0)
    near_tokens = shift(own_tokens, "row", 1)
    w_first = grouped(w_qkv, weights_first, (0, 1))
    w_second = grouped(w_qkv, weights_second, (1,))
    segments_other = swap_col(segment_ids)

    me = row_at * col_count + col_at
    first = me * EXP_DEV
    at = jnp.stack([dp_at, col_at, row_at, first])
    routed = routes[:, 0]
    chosen = routed[:, None] == jnp.arange(experts_all, dtype=jnp.int32)[None, :]
    counts = jnp.cumsum(chosen.astype(jnp.int32), axis=0)
    slot_index = jnp.sum(jnp.where(chosen, counts, 0), axis=-1) - 1
    slots_all = experts_all * slot_count
    slots_dev = EXP_DEV * slot_count
    send_shape = (row_count * col_count, EXP_DEV, slot_count, half_width)
    block_shape = (row_count, col_count, EXP_DEV, slot_count, half_width)

    def one_hot(devices):
        placed = (devices * EXP_DEV + routed % EXP_DEV) * slot_count + slot_index
        slots = jnp.arange(slots_all, dtype=jnp.int32)[:, None]
        return (slots == placed[None, :]).astype(bf16)

    placing = one_hot(routed // EXP_DEV)
    placing_near = one_hot((routed // EXP_DEV) ^ me)

    def all_to_all(array):
        return lax.all_to_all(array, group, split_axis=0, concat_axis=0, tiled=True)

    g_slots = mm(placing_near, d_layer).astype(bf16)
    g_slots = g_slots.reshape(row_count, col_count * slots_dev, half_width)
    g_send = [g_slots[j] for j in range(row_count)]
    near_tokens, g_send = lax.optimization_barrier((near_tokens, g_send))
    g_parts = [shift(g_send[j], "row", j) for j in range(row_count)]
    g_parts[1], w_proj = lax.optimization_barrier((g_parts[1], w_proj))
    w_proj_parts = [shift(w_proj, "row", j) for j in range(row_count)]
    gains = own_first(gain_ffn, 0)
    router = own_first(w_router, 0)
    input_near = own_first(layer_in, 1).astype(f32)

    near_block = both_halves(near_tokens, swap_col(near_tokens), 0)
    tokens_seq = in_sequence(layer_in, near_block).astype(f32)
    w_pair = jnp.concatenate(
        [jnp.where(is_first, w_qkv, w_first), jnp.where(is_first, w_first, w_second)], axis=1
    )
    w_all = jnp.concatenate([w_pair[0], w_pair[1], w_pair[2]], axis=1)
    scale_seq = lax.rsqrt(jnp.mean(tokens_seq * tokens_seq, axis=-1, keepdims=True) + epsilon)
    normed = (tokens_seq * scale_seq * gain_attn).astype(bf16)
    qkv = mm(normed, w_all).astype(bf16)

    buckets = (rel_bucket[:, None] == jnp.arange(NB, dtype=jnp.int32)[None, :]).astype(f32)
    bias_rows = lax.dynamic_slice_in_dim(rel_bias, heads_at * heads_dev, heads_dev, 0)
    bias_table = jnp.einsum("hb,ob->ho", bias_rows, buckets, precision=highest)
    table = jnp.pad(bias_table, ((0, 0), (0, 1)))
    segments = jnp.where(row_at // 2 == col_at, segment_ids, segments_other)[0]

    g_near = jnp.stack(g_parts).reshape(block_shape)
    qkv, g_near, d_layer_late = lax.optimization_barrier((qkv, g_near, d_layer))
    head_out, lse = attend_forward(qkv, table, segments, heads_dev)

    head_blocks = head_out.reshape(2, tok_dev, inner)
    head_own = lax.dynamic_index_in_dim(head_blocks, block_at, 0, False)
    head_near = shift(lax.dynamic_index_in_dim(head_blocks, 1 - block_at, 0, False), "row", 1)
    head_pair = jnp.concatenate([head_own, head_near], axis=1)
    head_other = swap_col(head_pair)

    all_g = lax.all_gather(g_near, "dp", axis=0, tiled=False)
    w_proj_parts, _ = lax.optimization_barrier((w_proj_parts, head_out))
    proj_own = jnp.concatenate(
        [jnp.where(is_first, w_proj_parts[j], w_proj_parts[j ^ 2]) for j in range(row_count)],
        axis=0,
    )
    proj_other = jnp.roll(swap_col(proj_own), 2 * inner, axis=0)
    proj_all = jnp.concatenate([proj_own, proj_other], axis=1)
    g_other = swap_col(g_near)
    grads_in = jnp.concatenate([d_layer_late, swap_col(d_layer_late)], axis=1).astype(f32)

    heads = jnp.concatenate([head_pair, head_other], axis=1)
    middle = input_near + mm(heads, proj_all)
    scale_ffn = lax.rsqrt(jnp.mean(middle * middle, axis=-1, keepdims=True) + epsilon)
    hidden = middle * scale_ffn * gains
    x_slots = mm(placing, hidden[:, :half_width].astype(bf16)).astype(bf16).reshape(send_shape)
    got_x = all_to_all(x_slots)
    all_x = lax.all_gather(got_x, "dp", axis=0, tiled=False)
    out_slots, grad_slots, d_router = run_experts(
        at, got_x.reshape(block_shape), g_near, g_other, w_router, w_up, w_down
    )
    got_grad = all_to_all(grad_slots.reshape(send_shape)).reshape(slots_all, half_width)
    mine = mm(placing, got_grad, TN).astype(bf16)
    d_hidden = jnp.concatenate([mine, swap_col(mine)], axis=1).astype(f32)
    d_gain_ffn = 0.5 * both_halves(
        jnp.sum((middle * scale_ffn * d_hidden)[:, :half_width], axis=0),
        jnp.sum((middle * scale_ffn * d_hidden)[:, half_width:], axis=0),
        0,
    )
    scaled_ffn = d_hidden * gains
    d_middle = (
        grads_in
        + scale_ffn * scaled_ffn
        - middle * scale_ffn**3 * jnp.mean(scaled_ffn * middle, axis=-1, keepdims=True)
    )
    d_attn = d_middle.astype(bf16)
    d_heads = mm(d_attn, proj_all[: 2 * inner], NT).astype(bf16)
    d_head = in_sequence(d_heads[:, :inner], shift(d_heads[:, inner:], "row", 1))

    d_attn_late, d_heads = lax.optimization_barrier((d_attn, d_heads))
    d_proj = mm(heads, d_attn_late[:, :half_width], TN).astype(bf16)
    d_proj = d_proj.reshape(row_count, inner, half_width)
    d_proj, d_head, d_gain_ffn = lax.optimization_barrier((d_proj, d_head, d_gain_ffn))
    proj_parts = [
        shift(jnp.where(is_first, d_proj[j], d_proj[j ^ 2]), "row", j)
        for j in range(row_count)
    ]

    d_qkv, d_table = attend_backward(qkv, head_out, d_head, lse, table, segments, heads_dev)

    proj_parts, d_qkv, all_x, all_g = lax.optimization_barrier((proj_parts, d_qkv, all_x, all_g))
    all_g_other = swap_col(all_g)
    d_w = mm(normed, d_qkv, TN)
    d_w_low = d_w.astype(bf16)
    d_w_sent = jnp.where(is_first, d_w_low[half_width:], d_w_low[:half_width])
    d_w_first = grouped(d_w_sent, grads_first, (0, 1))
    d_w_second = grouped(d_w_low[half_width:], weights_second, (1,))
    gain_part = jnp.sum(d_w * w_all.astype(f32), axis=1) / gain_attn
    d_rel_part = jnp.einsum("ho,ob->hb", d_table[:, : 2 * length - 1], buckets, precision=highest)
    rel_whole = lax.dynamic_update_slice_in_dim(
        jnp.zeros((H, NB), f32), d_rel_part, heads_at * heads_dev, 0
    )
    rel_row = jnp.pad(rel_whole.reshape(1, H * NB), ((0, 0), (0, width - H * NB)))
    spare = jnp.zeros((-(experts_all + 3) % 16, width), f32)
    small = jnp.concatenate(
        [d_router, d_gain_ffn[None], gain_part[None], rel_row, spare], axis=0
    )
    small = total_over(total_over(small, "col"), "row")

    d_proj = sum(part.astype(f32) for part in proj_parts)
    d_proj = jnp.concatenate([d_proj, small[:, :half_width], small[:, half_width:]], axis=0)
    d_w = jnp.where(is_first, d_w[:half_width], d_w_second.astype(f32))
    d_w = (d_w + d_w_first.astype(f32)).astype(bf16)
    packed = (d_w, d_proj.astype(bf16))
    summed = lax.psum(packed, "dp")

    at, d_qkv, out_late, packed = lax.optimization_barrier((at, d_qkv, out_slots, packed))
    part_normed = mm(d_qkv, w_all, NT).astype(bf16).reshape(2, tok_dev, width)
    normed_near = shift(lax.dynamic_index_in_dim(part_normed, 1 - block_at, 0, False), "row", 1)
    out_parts = [shift(out_late[j], "row", j) for j in range(row_count)]
    at, part_normed = lax.optimization_barrier((at, part_normed))
    d_up, d_down = weight_grads(
        at,
        all_x.reshape((dp_count,) + block_shape),
        all_g,
        all_g_other,
        w_router,
        w_up,
        w_down,
    )
    hidden, normed_near, out_parts, d_up, d_down = lax.optimization_barrier(
        (hidden, normed_near, out_parts, d_up, d_down)
    )
    normed_own = lax.dynamic_index_in_dim(part_normed, block_at, 0, False)
    normed_sum = normed_own.astype(f32) + normed_near.astype(f32)
    normed_other = swap_col(other_half(normed_sum, 0).astype(bf16))
    gate_probs = jax.nn.softmax(jnp.dot(hidden, router, precision=highest), axis=-1)
    gating = jnp.sum(jnp.where(chosen, gate_probs, 0.0), axis=-1, keepdims=True)
    out_stack = jnp.stack(out_parts).reshape(row_count, col_count, slots_dev, half_width)
    out_other = swap_col(out_stack[:, 1])
    out_back = jnp.stack([out_stack[:, 0], out_other], axis=1).reshape(slots_all, half_width)
    layer_out = middle[:, :half_width] + gating * mm(placing_near, out_back, TN)
    d_normed = my_half(normed_sum, 0) + normed_other.astype(f32)
    own = own_tokens.astype(f32)
    scale_own = lax.rsqrt(jnp.mean(own * own, axis=-1, keepdims=True) + epsilon)
    scaled_attn = d_normed * gain_attn
    d_own = scale_own * scaled_attn - own * scale_own**3 * jnp.mean(
        scaled_attn * own, axis=-1, keepdims=True
    )
    d_middle_own = my_half(d_middle, 0)
    d_layer_in = both_halves(
        d_middle_own[:, :half_width] + my_half(d_own, 1),
        swap_col(d_middle_own[:, half_width:] + other_half(d_own, 1)),
        0,
    )
    summed, layer_out, d_layer_in = lax.optimization_barrier((summed, layer_out, d_layer_in))
    d_w, d_proj = (array.astype(f32) for array in summed)
    small = d_proj[inner:].reshape(2, -1, half_width)
    small = jnp.concatenate([small[0], small[1]], axis=1)
    d_proj = d_proj[:inner]
    d_w_qkv = jnp.stack([d_w[:, i * inner : (i + 1) * inner] for i in range(3)])
    d_w_router = small[:experts_all].T
    d_gain_ffn = small[experts_all]
    d_gain_attn = small[experts_all + 1]
    d_rel_bias = small[experts_all + 2, : H * NB].reshape(H, NB)
    return (
        layer_out,
        d_layer_in,
        d_w_qkv,
        d_proj,
        d_rel_bias,
        d_gain_attn,
        d_gain_ffn,
        d_w_router,
        d_up,
        d_down,
    )


def solution(mesh):
    placed = (
        P(("dp", "row"), None),
        P(None, "col", "row"),
        P("row", "col"),
        P(),
        P(),
        P(("dp", "col"), None),
        P(),
        P(),
        P(),
        P(("dp", "row"), None),
        P(("row", "col"), None, None),
        P(("row", "col"), None, None),
        P(("dp", "row"), "col"),
    )
    return jax.shard_map(
        shards,
        mesh=mesh,
        in_specs=placed,
        out_specs=(
            P(("dp", "row"), "col"),
            P(("dp", "row"), "col"),
            P(None, "col", "row"),
            P("row", "col"),
            P(),
            P(),
            P(),
            P(),
            P(("row", "col"), "dp", None),
            P(("row", "col"), "dp", None),
        ),
        check_vma=False,
    )
```

```python
from functools import partial

import jax
import jax.numpy as jnp
from jax import lax
from jax.experimental import pallas as pl
from jax.experimental.pallas import tpu as pltpu
from jax.sharding import PartitionSpec as P

H = 12
HD = 64
NB = 32
EXP_DEV = 2
SUB = 128

epsilon = 1e-06
highest = lax.Precision.HIGHEST
f32 = jnp.float32
bf16 = jnp.bfloat16
group = ("row", "col")

NT = (((1,), (1,)), ((), ()))
NN = (((1,), (0,)), ((), ()))
TN = (((0,), (0,)), ((), ()))


def mm(a, b, dims=NN):
    return lax.dot_general(a, b, dims, preferred_element_type=f32)


def fill_strip(table_ref, strip_ref):
    heads, _, span = strip_ref.shape
    for h in range(heads):
        rows = jnp.broadcast_to(table_ref[h : h + 1, :], (SUB, table_ref.shape[1]))
        rolled = pltpu.roll(rows, table_ref.shape[1] - (SUB - 1), 1, stride=1, stride_axis=0)
        strip_ref[h] = rolled[:, :span]


def strip_at(step, part, parts, keys_at, width, length):
    begin = length - SUB * (step * parts + part + 1) + keys_at
    return pl.ds(pl.multiple_of(begin, SUB), width)


def each_window(ids_ref, step, rows, length, body):
    tiles = length // rows
    first = ids_ref[step * rows]
    last = ids_ref[step * rows + rows - 1]
    lo = jnp.int32(0)
    hi = jnp.int32(0)
    for i in range(tiles):
        lo = lo + (ids_ref[i * rows + rows - 1] < first).astype(jnp.int32)
        hi = hi + (ids_ref[i * rows] <= last).astype(jnp.int32)
    count = hi - lo
    sizes = sorted({min(2, tiles), min(3, tiles), tiles})
    for i, size in enumerate(sizes):
        fits = count <= size if i == 0 else jnp.logical_and(count > sizes[i - 1], count <= size)

        @pl.when(fits)
        def _():
            begin = jnp.minimum(lo, tiles - size) * rows
            body(pl.multiple_of(begin, rows), size * rows)


def forward_kernel(
    ids_ref,
    qkv_ref,
    table_ref,
    seg_col_ref,
    seg_row_ref,
    out_ref,
    lse_ref,
    strip_ref,
    *,
    rows,
    heads,
):
    step = pl.program_id(0)
    length = qkv_ref.shape[0]
    inner = heads * HD
    parts = rows // SUB

    @pl.when(step == 0)
    def _():
        fill_strip(table_ref, strip_ref)

    here = pl.ds(pl.multiple_of(step * rows, rows), rows)

    def window(begin, width):
        there = pl.ds(begin, width)
        same = seg_col_ref[here, :] == seg_row_ref[:, there]
        q_all = qkv_ref[here, :inner] * jnp.asarray(HD**-0.5, bf16)
        lane = lax.broadcasted_iota(jnp.int32, lse_ref.shape, 1)
        lse = jnp.zeros(lse_ref.shape, f32)
        outs = []
        for h in range(heads):
            lo = h * HD
            keys = qkv_ref[there, inner + lo : inner + lo + HD]
            values = qkv_ref[there, 2 * inner + lo : 2 * inner + lo + HD]
            bias = jnp.concatenate(
                [
                    strip_ref[h, :, strip_at(step, u, parts, begin, width, length)]
                    for u in range(parts)
                ],
                axis=0,
            )
            scores = jnp.where(same, mm(q_all[:, lo : lo + HD], keys, NT) + bias, -1e9)
            top = jnp.max(scores, axis=1, keepdims=True)
            weights = jnp.exp(scores - top)
            total = jnp.sum(weights, axis=1, keepdims=True)
            outs.append(mm(weights.astype(bf16), values) / total)
            lse = jnp.where(lane == h, top + jnp.log(total), lse)
        out_ref[...] = jnp.concatenate(outs, axis=1).astype(bf16)
        lse_ref[...] = lse

    each_window(ids_ref, step, rows, length, window)


def whole(shape):
    return pl.BlockSpec(shape, lambda *_: (0,) * len(shape))


def attend_forward(qkv, table, segments, heads):
    length = qkv.shape[0]
    rows = min(256, length)
    inner = heads * HD
    return pl.pallas_call(
        partial(forward_kernel, rows=rows, heads=heads),
        grid_spec=pltpu.PrefetchScalarGridSpec(
            num_scalar_prefetch=1,
            grid=(length // rows,),
            in_specs=[
                whole(qkv.shape),
                whole(table.shape),
                whole((length, 1)),
                whole((1, length)),
            ],
            out_specs=[
                pl.BlockSpec((rows, inner), lambda i, ids: (i, 0)),
                pl.BlockSpec((rows, SUB), lambda i, ids: (i, 0)),
            ],
            scratch_shapes=[
                pltpu.VMEM((heads, SUB, 2 * length - SUB), f32),
            ],
        ),
        out_shape=[
            jax.ShapeDtypeStruct((length, inner), bf16),
            jax.ShapeDtypeStruct((length, SUB), f32),
        ],
        compiler_params=pltpu.CompilerParams(vmem_limit_bytes=40 * 1024 * 1024),
        cost_estimate=pl.CostEstimate(
            flops=4 * length * length * inner,
            bytes_accessed=10 * length * inner,
            transcendentals=length * length * heads,
        ),
        name="attend_forward",
    )(segments, qkv, table, segments[:, None], segments[None, :])


def backward_kernel(
    ids_ref,
    qkv_ref,
    out_in_ref,
    grad_ref,
    lse_ref,
    table_ref,
    seg_col_ref,
    seg_row_ref,
    out_ref,
    d_table_ref,
    strip_ref,
    d_strip_ref,
    d_keys_ref,
    d_values_ref,
    *,
    rows,
    heads,
):
    step = pl.program_id(0)
    length = qkv_ref.shape[0]
    inner = heads * HD
    parts = rows // SUB

    @pl.when(step == 0)
    def _():
        fill_strip(table_ref, strip_ref)
        d_strip_ref[...] = jnp.zeros_like(d_strip_ref)
        d_keys_ref[...] = jnp.zeros_like(d_keys_ref)
        d_values_ref[...] = jnp.zeros_like(d_values_ref)

    here = pl.ds(pl.multiple_of(step * rows, rows), rows)
    product = grad_ref[here, :].astype(f32) * out_in_ref[here, :].astype(f32)
    deltas = [
        jnp.sum(product[:, h * HD : (h + 1) * HD], axis=1, keepdims=True) for h in range(heads)
    ]

    def window(begin, width):
        there = pl.ds(begin, width)
        same = seg_col_ref[here, :] == seg_row_ref[:, there]
        q_all = qkv_ref[here, :inner] * jnp.asarray(HD**-0.5, bf16)
        d_queries = []
        for h in range(heads):
            lo = h * HD
            keys = qkv_ref[there, inner + lo : inner + lo + HD]
            values = qkv_ref[there, 2 * inner + lo : 2 * inner + lo + HD]
            grads = grad_ref[here, lo : lo + HD]
            queries = q_all[:, lo : lo + HD]
            bias = jnp.concatenate(
                [
                    strip_ref[h, :, strip_at(step, u, parts, begin, width, length)]
                    for u in range(parts)
                ],
                axis=0,
            )
            scores = mm(queries, keys, NT) + bias - lse_ref[:, h : h + 1]
            probs = jnp.exp(jnp.where(same, scores, -1e9))
            d_values_ref[lo : lo + HD, there] += mm(grads, probs.astype(bf16), TN)
            d_scores = probs * (mm(grads, values, NT) - deltas[h])
            for u in range(parts):
                span = strip_at(step, u, parts, begin, width, length)
                d_strip_ref[h, :, span] += d_scores[u * SUB : (u + 1) * SUB]
            d_raw = d_scores.astype(bf16)
            d_queries.append(mm(d_raw, keys) * HD**-0.5)
            d_keys_ref[lo : lo + HD, there] += mm(queries, d_raw, TN)
        out_ref[here, :inner] = jnp.concatenate(d_queries, axis=1).astype(bf16)

    each_window(ids_ref, step, rows, length, window)

    @pl.when(step == pl.num_programs(0) - 1)
    def _():
        for h in range(heads):
            lo = h * HD
            out_ref[:, inner + lo : inner + lo + HD] = d_keys_ref[lo : lo + HD, :].T.astype(bf16)
            out_ref[:, 2 * inner + lo : 2 * inner + lo + HD] = d_values_ref[
                lo : lo + HD, :
            ].T.astype(bf16)
            summed = jnp.concatenate([d_strip_ref[h], jnp.zeros((SUB, SUB), f32)], axis=1)
            count = SUB
            while count > 1:
                count //= 2
                summed = summed[count:] + pltpu.roll(summed[:count], count, 1)
            d_table_ref[h : h + 1, :] = summed


def attend_backward(qkv, head_out, d_head, lse, table, segments, heads):
    length = qkv.shape[0]
    rows = min(256, length)
    inner = heads * HD
    return pl.pallas_call(
        partial(backward_kernel, rows=rows, heads=heads),
        grid_spec=pltpu.PrefetchScalarGridSpec(
            num_scalar_prefetch=1,
            grid=(length // rows,),
            in_specs=[
                whole(qkv.shape),
                whole(head_out.shape),
                whole(d_head.shape),
                pl.BlockSpec((rows, SUB), lambda i, ids: (i, 0)),
                whole(table.shape),
                whole((length, 1)),
                whole((1, length)),
            ],
            out_specs=[whole(qkv.shape), whole(table.shape)],
            scratch_shapes=[
                pltpu.VMEM((heads, SUB, 2 * length - SUB), f32),
                pltpu.VMEM((heads, SUB, 2 * length - SUB), f32),
                pltpu.VMEM((inner, length), f32),
                pltpu.VMEM((inner, length), f32),
            ],
        ),
        out_shape=[
            jax.ShapeDtypeStruct(qkv.shape, bf16),
            jax.ShapeDtypeStruct(table.shape, f32),
        ],
        compiler_params=pltpu.CompilerParams(vmem_limit_bytes=48 * 1024 * 1024),
        cost_estimate=pl.CostEstimate(
            flops=10 * length * length * inner,
            bytes_accessed=16 * length * inner,
            transcendentals=length * length * heads,
        ),
        name="attend_backward",
    )(segments, qkv, head_out, d_head, lse, table, segments[:, None], segments[None, :])


def joined(block_ref, at):
    rows, cols, _, slots, half = block_ref.shape
    return jnp.concatenate(
        [
            jnp.concatenate([block_ref[at ^ j, c, 0] for c in range(cols)], axis=1)
            for j in range(rows)
        ],
        axis=0,
    )


def halves(own, other, col):
    return jnp.where(
        col == 0,
        jnp.concatenate([own, other], axis=1),
        jnp.concatenate([other, own], axis=1),
    )


def flat(block):
    return block.reshape(-1, block.shape[-1]).astype(f32)


GELU_A = 0.7978845608028654
GELU_B = 0.044715


def gelu_pair(u):
    square = u * u
    factor = 0.5 * jnp.tanh(u * (GELU_A + (GELU_A * GELU_B) * square)) + 0.5
    value = u * factor
    slope = factor + value * (1.0 - factor) * (2 * GELU_A + (6 * GELU_A * GELU_B) * square)
    return value, slope


def router_probs(x, router_ref):
    weights = router_ref[...]
    high = weights.astype(bf16)
    low = (weights - high.astype(f32)).astype(bf16)
    logits = mm(x, high, NT) + mm(x, low, NT)
    exped = jnp.exp(logits - jnp.max(logits, axis=1, keepdims=True))
    return exped / jnp.sum(exped, axis=1, keepdims=True)


def gate(probs, expert):
    picked = lax.broadcasted_iota(jnp.int32, probs.shape, 1) == expert
    return picked, jnp.sum(jnp.where(picked, probs, 0.0), axis=1, keepdims=True)


def expert_kernel(
    at_ref,
    x_in_ref,
    own_ref,
    other_ref,
    router_ref,
    up_ref,
    down_ref,
    out_ref,
    grad_ref,
    d_router_ref,
    x_ref,
    g_ref,
    scaled_ref,
    probs_ref,
    out_acc_ref,
    grad_acc_ref,
):
    expert = pl.program_id(0)
    step = pl.program_id(1)
    col = at_ref[1]
    row = at_ref[2]
    first = at_ref[3]

    @pl.when(step == 0)
    def _():
        x = joined(x_in_ref, row)
        probs = router_probs(x, router_ref)
        _, gating = gate(probs, first + expert)
        g = halves(flat(own_ref[:, 0, 0]), flat(other_ref[:, 0, 0]), col)
        x_ref[...] = x
        g_ref[...] = g
        scaled_ref[...] = (gating * g).astype(bf16)
        probs_ref[...] = probs
        out_acc_ref[...] = jnp.zeros_like(out_acc_ref)
        grad_acc_ref[...] = jnp.zeros_like(grad_acc_ref)

    parts = 3
    tile = up_ref.shape[1] // parts
    activated, d_pre = [], []
    for i in range(parts):
        here = slice(i * tile, (i + 1) * tile)
        value, slope = gelu_pair(mm(x_ref[...], up_ref[0, here], NT))
        activated.append(value.astype(bf16))
        d_pre.append((mm(scaled_ref[...], down_ref[0, here], NT) * slope).astype(bf16))
    out_acc_ref[...] += mm(jnp.concatenate(activated, axis=1), down_ref[0])
    grad_acc_ref[...] += mm(jnp.concatenate(d_pre, axis=1), up_ref[0])

    @pl.when(step == pl.num_programs(1) - 1)
    def _():
        out = out_acc_ref[...]
        probs = probs_ref[...]
        picked, gating = gate(probs, first + expert)
        d_gating = jnp.sum(g_ref[...] * out, axis=1, keepdims=True)
        d_logits = d_gating * probs * (picked.astype(f32) - gating)
        grad = grad_acc_ref[...] + lax.dot_general(
            d_logits, router_ref[...], NN, precision=highest, preferred_element_type=f32
        )
        d_router = lax.dot_general(
            d_logits,
            x_ref[...].astype(f32),
            TN,
            precision=highest,
            preferred_element_type=f32,
        )
        rows, cols, _, slots, half = grad_ref.shape
        out = out.astype(bf16)
        grad = grad.astype(bf16)
        first_half, last_half = out[:, :half], out[:, half:]
        own = jnp.where(col == 0, first_half, last_half)
        other = jnp.where(col == 0, last_half, first_half)
        out_ref[:, 0, 0] = own.reshape(rows, slots, half)
        out_ref[:, 1, 0] = other.reshape(rows, slots, half)
        for j in range(rows):
            for c in range(cols):
                grad_ref[row ^ j, c, 0] = grad[
                    j * slots : (j + 1) * slots, c * half : (c + 1) * half
                ]

        @pl.when(expert == 0)
        def _():
            d_router_ref[...] = d_router

        @pl.when(expert > 0)
        def _():
            d_router_ref[...] += d_router


def run_experts(at, got_x, g_own, g_other, w_router, w_up, w_down):
    rows, cols, experts, slots, half = got_x.shape
    hidden, width = w_up.shape[1:]
    tile = 768
    block = pl.BlockSpec((rows, cols, 1, slots, half), lambda e, f, at: (0, 0, e, 0, 0))
    part = pl.BlockSpec((rows, 1, 1, slots, half), lambda e, f, at: (0, 0, e, 0, 0))
    last = pl.BlockSpec((rows, 1, 1, slots, half), lambda e, f, at: (0, 1, e, 0, 0))
    weight = pl.BlockSpec((1, tile, width), lambda e, f, at: (e, f, 0))
    tokens = rows * slots
    shape = jax.ShapeDtypeStruct(got_x.shape, bf16)
    router_shape = w_router.shape
    return pl.pallas_call(
        expert_kernel,
        grid_spec=pltpu.PrefetchScalarGridSpec(
            num_scalar_prefetch=1,
            grid=(experts, hidden // tile),
            in_specs=[block, part, last, whole(w_router.shape), weight, weight],
            out_specs=[block, block, whole(router_shape)],
            scratch_shapes=[
                pltpu.VMEM((tokens, width), bf16),
                pltpu.VMEM((tokens, width), f32),
                pltpu.VMEM((tokens, width), bf16),
                pltpu.VMEM((tokens, w_router.shape[0]), f32),
                pltpu.VMEM((tokens, width), f32),
                pltpu.VMEM((tokens, width), f32),
            ],
        ),
        out_shape=[shape, shape, jax.ShapeDtypeStruct(router_shape, f32)],
        compiler_params=pltpu.CompilerParams(vmem_limit_bytes=56 * 1024 * 1024),
        cost_estimate=pl.CostEstimate(
            flops=8 * experts * tokens * hidden * width,
            bytes_accessed=4 * experts * hidden * width,
            transcendentals=experts * tokens * hidden,
        ),
        name="experts",
    )(at, got_x, g_own, g_other, w_router, w_up, w_down)


def weight_kernel(
    at_ref,
    x_in_ref,
    own_ref,
    other_ref,
    router_ref,
    up_ref,
    down_ref,
    d_up_ref,
    d_down_ref,
    x_ref,
    g_ref,
    x_turned_ref,
    g_turned_ref,
    *,
    steps,
):
    expert = pl.program_id(0)
    tile = pl.program_id(1)
    step = pl.program_id(2)
    parts = x_in_ref.shape[0]

    @pl.when(jnp.logical_or(tile == 0, steps > 1))
    def _():
        x = jnp.concatenate([joined(x_in_ref.at[i], at_ref[2]) for i in range(parts)], axis=0)
        g = halves(flat(own_ref[:, :, 0, 0]), flat(other_ref[:, :, 0, 0]), at_ref[1])
        _, gating = gate(router_probs(x, router_ref), at_ref[3] + expert)
        g = (gating * g).astype(bf16)
        x_ref[...] = x
        g_ref[...] = g
        x_turned_ref[...] = x.T
        g_turned_ref[...] = g.T

    value, slope = gelu_pair(mm(up_ref[0], x_turned_ref[...]))
    d_pre = (mm(down_ref[0], g_turned_ref[...]) * slope).astype(bf16)
    d_down = mm(value.astype(bf16), g_ref[...])
    d_up = mm(d_pre, x_ref[...])

    @pl.when(step == 0)
    def _():
        d_up_ref[0] = d_up
        d_down_ref[0] = d_down

    @pl.when(step > 0)
    def _():
        d_up_ref[0] += d_up
        d_down_ref[0] += d_down


def weight_grads(at, all_x, g_own, g_other, w_router, w_up, w_down):
    parts, rows, cols, experts, slots, half = all_x.shape
    hidden, width = w_up.shape[1:]
    own = hidden // parts
    tile = 256 if own % 256 == 0 else own
    tiles = own // tile
    each = min(4, parts)
    steps = parts // each
    tokens = each * rows * slots
    block = pl.BlockSpec(
        (each, rows, cols, 1, slots, half), lambda e, f, n, at: (n, 0, 0, e, 0, 0)
    )
    part = pl.BlockSpec(
        (each, rows, 1, 1, slots, half), lambda e, f, n, at: (n, 0, 0, e, 0, 0)
    )
    last = pl.BlockSpec(
        (each, rows, 1, 1, slots, half), lambda e, f, n, at: (n, 0, 1, e, 0, 0)
    )
    weight = pl.BlockSpec((1, tile, width), lambda e, f, n, at: (e, at[0] * tiles + f, 0))
    result = pl.BlockSpec((1, tile, width), lambda e, f, n, at: (e, f, 0))
    shape = jax.ShapeDtypeStruct((experts, own, width), f32)
    return pl.pallas_call(
        partial(weight_kernel, steps=steps),
        grid_spec=pltpu.PrefetchScalarGridSpec(
            num_scalar_prefetch=1,
            grid=(experts, tiles, steps),
            in_specs=[block, part, last, whole(w_router.shape), weight, weight],
            out_specs=[result, result],
            scratch_shapes=[
                pltpu.VMEM((tokens, width), bf16),
                pltpu.VMEM((tokens, width), bf16),
                pltpu.VMEM((width, tokens), bf16),
                pltpu.VMEM((width, tokens), bf16),
            ],
        ),
        out_shape=[shape, shape],
        compiler_params=pltpu.CompilerParams(vmem_limit_bytes=56 * 1024 * 1024),
        cost_estimate=pl.CostEstimate(
            flops=8 * experts * parts * rows * slots * own * width,
            bytes_accessed=12 * experts * own * width + 4 * all_x.size,
            transcendentals=experts * parts * rows * slots * own,
        ),
        name="weight_grads",
    )(at, all_x, g_own, g_other, w_router, w_up, w_down)


def weights_first(r, c):
    return (r, 0) if c == 1 else (r ^ 2, 1)


def weights_second(r, c):
    return (r ^ 2, 1)


def grouped(array, route, cores):
    pairs = []
    for r in range(4):
        for c in cores:
            to_row, to_col = route(r, c)
            pairs.append((r * 2 + c, to_row * 2 + to_col))
    return lax.ppermute(array, group, pairs)


def grads_first(r, c):
    return (r, 1) if c == 0 else (r ^ 2, 0)


def swap_col(array):
    return lax.ppermute(array, "col", [(0, 1), (1, 0)])


def shift(array, axis, bits):
    if bits == 0:
        return array
    count = lax.axis_size(axis)
    return lax.ppermute(array, axis, [(i, i ^ bits) for i in range(count)])


def total_over(array, axis):
    count = lax.axis_size(axis)
    stride = 1
    while stride < count:
        if 4 * stride <= count:
            near, far, last = (shift(array, axis, stride * i) for i in (1, 2, 3))
            array = (array + near) + (far + last)
            stride *= 4
        else:
            array = array + shift(array, axis, stride)
            stride *= 2
    return array


def shards(
    layer_in,
    w_qkv,
    w_proj,
    rel_bias,
    rel_bucket,
    segment_ids,
    gain_attn,
    gain_ffn,
    w_router,
    routes,
    w_up,
    w_down,
    d_layer,
):
    row_count = lax.axis_size("row")
    col_count = lax.axis_size("col")
    dp_count = lax.axis_size("dp")
    dp_at = lax.axis_index("dp")
    row_at = lax.axis_index("row")
    col_at = lax.axis_index("col")
    tok_dev, width = layer_in.shape
    slot_count = max(2, tok_dev // 8)
    half_width = width // col_count
    length = segment_ids.shape[1]
    inner = w_qkv.shape[2]
    heads_dev = inner // HD
    experts_all = EXP_DEV * row_count * col_count
    block_at = row_at % 2
    heads_at = row_at ^ (2 * col_at)
    is_first = col_at == 0

    def both_halves(mine, other, axis):
        return jnp.where(
            is_first,
            jnp.concatenate([mine, other], axis),
            jnp.concatenate([other, mine], axis),
        )

    def my_half(array, axis):
        size = array.shape[axis] // 2
        return lax.dynamic_slice_in_dim(array, col_at * size, size, axis)

    def other_half(array, axis):
        size = array.shape[axis] // 2
        return lax.dynamic_slice_in_dim(array, (1 - col_at) * size, size, axis)

    def own_first(array, axis):
        return jnp.concatenate([my_half(array, axis), other_half(array, axis)], axis)

    def in_sequence(mine, other):
        return jnp.where(
            block_at == 0,
            jnp.concatenate([mine, other], axis=0),
            jnp.concatenate([other, mine], axis=0),
        )

    own_tokens = my_half(layer_in, 0)
    near_tokens = shift(own_tokens, "row", 1)
    w_first = grouped(w_qkv, weights_first, (0, 1))
    w_second = grouped(w_qkv, weights_second, (1,))
    segments_other = swap_col(segment_ids)

    me = row_at * col_count + col_at
    first = me * EXP_DEV
    at = jnp.stack([dp_at, col_at, row_at, first])
    routed = routes[:, 0]
    chosen = routed[:, None] == jnp.arange(experts_all, dtype=jnp.int32)[None, :]
    counts = jnp.cumsum(chosen.astype(jnp.int32), axis=0)
    slot_index = jnp.sum(jnp.where(chosen, counts, 0), axis=-1) - 1
    slots_all = experts_all * slot_count
    slots_dev = EXP_DEV * slot_count
    send_shape = (row_count * col_count, EXP_DEV, slot_count, half_width)
    block_shape = (row_count, col_count, EXP_DEV, slot_count, half_width)

    def one_hot(devices):
        placed = (devices * EXP_DEV + routed % EXP_DEV) * slot_count + slot_index
        slots = jnp.arange(slots_all, dtype=jnp.int32)[:, None]
        return (slots == placed[None, :]).astype(bf16)

    placing = one_hot(routed // EXP_DEV)
    placing_near = one_hot((routed // EXP_DEV) ^ me)

    def all_to_all(array):
        return lax.all_to_all(array, group, split_axis=0, concat_axis=0, tiled=True)

    g_slots = mm(placing_near, d_layer).astype(bf16)
    g_slots = g_slots.reshape(row_count, col_count * slots_dev, half_width)
    g_send = [g_slots[j] for j in range(row_count)]
    g_parts = [shift(g_send[j], "row", j) for j in range(row_count)]
    g_parts[1], w_proj = lax.optimization_barrier((g_parts[1], w_proj))
    w_proj_parts = [shift(w_proj, "row", j) for j in range(row_count)]
    gains = own_first(gain_ffn, 0)
    router = own_first(w_router, 0)
    input_near = own_first(layer_in, 1).astype(f32)

    near_block = both_halves(near_tokens, swap_col(near_tokens), 0)
    tokens_seq = in_sequence(layer_in, near_block).astype(f32)
    w_pair = jnp.concatenate(
        [jnp.where(is_first, w_qkv, w_first), jnp.where(is_first, w_first, w_second)], axis=1
    )
    w_all = jnp.concatenate([w_pair[0], w_pair[1], w_pair[2]], axis=1)
    scale_seq = lax.rsqrt(jnp.mean(tokens_seq * tokens_seq, axis=-1, keepdims=True) + epsilon)
    normed = (tokens_seq * scale_seq * gain_attn).astype(bf16)
    qkv = mm(normed, w_all).astype(bf16)

    buckets = (rel_bucket[:, None] == jnp.arange(NB, dtype=jnp.int32)[None, :]).astype(f32)
    bias_rows = lax.dynamic_slice_in_dim(rel_bias, heads_at * heads_dev, heads_dev, 0)
    bias_table = jnp.einsum("hb,ob->ho", bias_rows, buckets, precision=highest)
    table = jnp.pad(bias_table, ((0, 0), (0, 1)))
    segments = jnp.where(row_at // 2 == col_at, segment_ids, segments_other)[0]

    g_near = jnp.stack(g_parts).reshape(block_shape)
    qkv, g_near, d_layer_late, at = lax.optimization_barrier((qkv, g_near, d_layer, at))
    head_out, lse = attend_forward(qkv, table, segments, heads_dev)

    head_blocks = head_out.reshape(2, tok_dev, inner)
    head_own = lax.dynamic_index_in_dim(head_blocks, block_at, 0, False)
    head_near = shift(lax.dynamic_index_in_dim(head_blocks, 1 - block_at, 0, False), "row", 1)
    head_pair = jnp.concatenate([head_own, head_near], axis=1)
    head_other = swap_col(head_pair)

    all_g = lax.all_gather(g_near, "dp", axis=0, tiled=False)
    w_proj_parts, _ = lax.optimization_barrier((w_proj_parts, head_out))
    proj_own = jnp.concatenate(
        [jnp.where(is_first, w_proj_parts[j], w_proj_parts[j ^ 2]) for j in range(row_count)],
        axis=0,
    )
    proj_other = jnp.roll(swap_col(proj_own), 2 * inner, axis=0)
    proj_all = jnp.concatenate([proj_own, proj_other], axis=1)
    g_other = swap_col(g_near)
    grads_in = jnp.concatenate([d_layer_late, swap_col(d_layer_late)], axis=1).astype(f32)

    heads = jnp.concatenate([head_pair, head_other], axis=1)
    middle = input_near + mm(heads, proj_all)
    scale_ffn = lax.rsqrt(jnp.mean(middle * middle, axis=-1, keepdims=True) + epsilon)
    hidden = middle * scale_ffn * gains
    x_slots = mm(placing, hidden[:, :half_width].astype(bf16)).astype(bf16).reshape(send_shape)
    got_x = all_to_all(x_slots)
    all_x = lax.all_gather(got_x, "dp", axis=0, tiled=False)
    out_slots, grad_slots, d_router = run_experts(
        at, got_x.reshape(block_shape), g_near, g_other, w_router.T, w_up, w_down
    )
    got_grad = all_to_all(grad_slots.reshape(send_shape)).reshape(slots_all, half_width)
    mine = mm(placing, got_grad, TN).astype(bf16)
    d_hidden = jnp.concatenate([mine, swap_col(mine)], axis=1).astype(f32)
    d_gain_ffn = 0.5 * both_halves(
        jnp.sum((middle * scale_ffn * d_hidden)[:, :half_width], axis=0),
        jnp.sum((middle * scale_ffn * d_hidden)[:, half_width:], axis=0),
        0,
    )
    scaled_ffn = d_hidden * gains
    d_middle = (
        grads_in
        + scale_ffn * scaled_ffn
        - middle * scale_ffn**3 * jnp.mean(scaled_ffn * middle, axis=-1, keepdims=True)
    )
    d_attn = d_middle.astype(bf16)
    d_heads = mm(d_attn, proj_all[: 2 * inner], NT).astype(bf16)
    d_head = in_sequence(d_heads[:, :inner], shift(d_heads[:, inner:], "row", 1))

    d_attn_late, d_heads = lax.optimization_barrier((d_attn, d_heads))
    d_proj = mm(heads, d_attn_late[:, :half_width], TN).astype(bf16)
    d_proj = d_proj.reshape(row_count, inner, half_width)
    d_head, d_gain_ffn = lax.optimization_barrier((d_head, d_gain_ffn))
    proj_parts = [
        shift(jnp.where(is_first, d_proj[j], d_proj[j ^ 2]), "row", j)
        for j in range(row_count)
    ]

    d_qkv, d_table = attend_backward(qkv, head_out, d_head, lse, table, segments, heads_dev)

    proj_parts, d_qkv, all_g = lax.optimization_barrier((proj_parts, d_qkv, all_g))
    all_g_other = swap_col(all_g)
    d_w = mm(normed, d_qkv, TN)
    d_w_low = d_w.astype(bf16)
    d_w_sent = jnp.where(is_first, d_w_low[half_width:], d_w_low[:half_width])
    d_w_first = grouped(d_w_sent, grads_first, (0, 1))
    d_w_second = grouped(d_w_low[half_width:], weights_second, (1,))
    gain_part = jnp.sum(d_w * w_all.astype(f32), axis=1) / gain_attn
    d_rel_part = jnp.einsum("ho,ob->hb", d_table[:, : 2 * length - 1], buckets, precision=highest)
    rel_whole = lax.dynamic_update_slice_in_dim(
        jnp.zeros((H, NB), f32), d_rel_part, heads_at * heads_dev, 0
    )
    rel_row = jnp.pad(rel_whole.reshape(1, H * NB), ((0, 0), (0, width - H * NB)))
    spare = jnp.zeros((-(experts_all + 3) % 8, width), f32)
    small = jnp.concatenate(
        [d_router, d_gain_ffn[None], gain_part[None], rel_row, spare], axis=0
    )
    small = total_over(small, "col")
    small, d_w_first, all_x = lax.optimization_barrier((small, d_w_first, all_x))
    small = total_over(small, "row")

    d_proj = sum(part.astype(f32) for part in proj_parts)
    d_proj = jnp.concatenate([d_proj, small[:, :half_width], small[:, half_width:]], axis=0)
    d_w = jnp.where(is_first, d_w[:half_width], d_w_second.astype(f32))
    d_w = (d_w + d_w_first.astype(f32)).astype(bf16)
    packed = (d_w, d_proj.astype(bf16))
    summed = lax.psum(packed, "dp")

    at, d_qkv, out_late, packed = lax.optimization_barrier((at, d_qkv, out_slots, packed))
    part_normed = mm(d_qkv, w_all, NT).astype(bf16).reshape(2, tok_dev, width)
    normed_near = shift(lax.dynamic_index_in_dim(part_normed, 1 - block_at, 0, False), "row", 1)
    out_parts = [shift(out_late[j], "row", j) for j in range(row_count)]
    at, part_normed = lax.optimization_barrier((at, part_normed))
    d_up, d_down = weight_grads(
        at,
        all_x.reshape((dp_count,) + block_shape),
        all_g,
        all_g_other,
        w_router.T,
        w_up,
        w_down,
    )
    hidden, normed_near, out_parts, d_up, d_down = lax.optimization_barrier(
        (hidden, normed_near, out_parts, d_up, d_down)
    )
    normed_own = lax.dynamic_index_in_dim(part_normed, block_at, 0, False)
    normed_sum = normed_own.astype(f32) + normed_near.astype(f32)
    normed_other = swap_col(other_half(normed_sum, 0).astype(bf16))
    gate_probs = jax.nn.softmax(jnp.dot(hidden, router, precision=highest), axis=-1)
    gating = jnp.sum(jnp.where(chosen, gate_probs, 0.0), axis=-1, keepdims=True)
    out_stack = jnp.stack(out_parts).reshape(row_count, col_count, slots_dev, half_width)
    out_other = swap_col(out_stack[:, 1])
    out_back = jnp.stack([out_stack[:, 0], out_other], axis=1).reshape(slots_all, half_width)
    layer_out = middle[:, :half_width] + gating * mm(placing_near, out_back, TN)
    d_normed = my_half(normed_sum, 0) + normed_other.astype(f32)
    own = own_tokens.astype(f32)
    scale_own = lax.rsqrt(jnp.mean(own * own, axis=-1, keepdims=True) + epsilon)
    scaled_attn = d_normed * gain_attn
    d_own = scale_own * scaled_attn - own * scale_own**3 * jnp.mean(
        scaled_attn * own, axis=-1, keepdims=True
    )
    d_middle_own = my_half(d_middle, 0)
    d_layer_in = both_halves(
        d_middle_own[:, :half_width] + my_half(d_own, 1),
        swap_col(d_middle_own[:, half_width:] + other_half(d_own, 1)),
        0,
    )
    summed, layer_out, d_layer_in = lax.optimization_barrier((summed, layer_out, d_layer_in))
    d_w, d_proj = (array.astype(f32) for array in summed)
    small = d_proj[inner:].reshape(2, -1, half_width)
    small = jnp.concatenate([small[0], small[1]], axis=1)
    d_proj = d_proj[:inner]
    d_w_qkv = jnp.stack([d_w[:, i * inner : (i + 1) * inner] for i in range(3)])
    d_w_router = small[:experts_all].T
    d_gain_ffn = small[experts_all]
    d_gain_attn = small[experts_all + 1]
    d_rel_bias = small[experts_all + 2, : H * NB].reshape(H, NB)
    return (
        layer_out,
        d_layer_in,
        d_w_qkv,
        d_proj,
        d_rel_bias,
        d_gain_attn,
        d_gain_ffn,
        d_w_router,
        d_up,
        d_down,
    )


def solution(mesh):
    placed = (
        P(("dp", "row"), None),
        P(None, "col", "row"),
        P("row", "col"),
        P(),
        P(),
        P(("dp", "col"), None),
        P(),
        P(),
        P(),
        P(("dp", "row"), None),
        P(("row", "col"), None, None),
        P(("row", "col"), None, None),
        P(("dp", "row"), "col"),
    )
    return jax.shard_map(
        shards,
        mesh=mesh,
        in_specs=placed,
        out_specs=(
            P(("dp", "row"), "col"),
            P(("dp", "row"), "col"),
            P(None, "col", "row"),
            P("row", "col"),
            P(),
            P(),
            P(),
            P(),
            P(("row", "col"), "dp", None),
            P(("row", "col"), "dp", None),
        ),
        check_vma=False,
    )
```

```python
from functools import partial

import jax
import jax.numpy as jnp
from jax import lax
from jax.experimental import pallas as pl
from jax.experimental.pallas import tpu as pltpu
from jax.sharding import PartitionSpec as P

H = 12
HD = 64
NB = 32
EXP_DEV = 2
SUB = 128

epsilon = 1e-06
highest = lax.Precision.HIGHEST
f32 = jnp.float32
bf16 = jnp.bfloat16
group = ("row", "col")

NT = (((1,), (1,)), ((), ()))
NN = (((1,), (0,)), ((), ()))
TN = (((0,), (0,)), ((), ()))


def mm(a, b, dims=NN):
    return lax.dot_general(a, b, dims, preferred_element_type=f32)


def fill_strip(table_ref, strip_ref):
    heads, _, span = strip_ref.shape
    for h in range(heads):
        rows = jnp.broadcast_to(table_ref[h : h + 1, :], (SUB, table_ref.shape[1]))
        rolled = pltpu.roll(rows, table_ref.shape[1] - (SUB - 1), 1, stride=1, stride_axis=0)
        strip_ref[h] = rolled[:, :span]


def strip_at(step, part, parts, keys_at, width, length):
    begin = length - SUB * (step * parts + part + 1) + keys_at
    return pl.ds(pl.multiple_of(begin, SUB), width)


def each_window(ids_ref, step, rows, length, body):
    tiles = length // rows
    first = ids_ref[step * rows]
    last = ids_ref[step * rows + rows - 1]
    lo = jnp.int32(0)
    hi = jnp.int32(0)
    for i in range(tiles):
        lo = lo + (ids_ref[i * rows + rows - 1] < first).astype(jnp.int32)
        hi = hi + (ids_ref[i * rows] <= last).astype(jnp.int32)
    count = hi - lo
    sizes = sorted({min(2, tiles), min(3, tiles), tiles})
    for i, size in enumerate(sizes):
        fits = count <= size if i == 0 else jnp.logical_and(count > sizes[i - 1], count <= size)

        @pl.when(fits)
        def _():
            begin = jnp.minimum(lo, tiles - size) * rows
            body(pl.multiple_of(begin, rows), size * rows)


def forward_kernel(
    ids_ref,
    qkv_ref,
    table_ref,
    seg_col_ref,
    seg_row_ref,
    out_ref,
    lse_ref,
    strip_ref,
    *,
    rows,
    heads,
):
    step = pl.program_id(0)
    length = qkv_ref.shape[0]
    inner = heads * HD
    parts = rows // SUB

    @pl.when(step == 0)
    def _():
        fill_strip(table_ref, strip_ref)

    here = pl.ds(pl.multiple_of(step * rows, rows), rows)

    def window(begin, width):
        there = pl.ds(begin, width)
        same = seg_col_ref[here, :] == seg_row_ref[:, there]
        q_all = qkv_ref[here, :inner] * jnp.asarray(HD**-0.5, bf16)
        lane = lax.broadcasted_iota(jnp.int32, lse_ref.shape, 1)
        lse = jnp.zeros(lse_ref.shape, f32)
        outs = []
        for h in range(heads):
            lo = h * HD
            keys = qkv_ref[there, inner + lo : inner + lo + HD]
            values = qkv_ref[there, 2 * inner + lo : 2 * inner + lo + HD]
            bias = jnp.concatenate(
                [
                    strip_ref[h, :, strip_at(step, u, parts, begin, width, length)]
                    for u in range(parts)
                ],
                axis=0,
            )
            scores = jnp.where(same, mm(q_all[:, lo : lo + HD], keys, NT) + bias, -1e9)
            top = jnp.max(scores, axis=1, keepdims=True)
            weights = jnp.exp(scores - top)
            total = jnp.sum(weights, axis=1, keepdims=True)
            outs.append(mm(weights.astype(bf16), values) / total)
            lse = jnp.where(lane == h, top + jnp.log(total), lse)
        out_ref[...] = jnp.concatenate(outs, axis=1).astype(bf16)
        lse_ref[...] = lse

    each_window(ids_ref, step, rows, length, window)


def whole(shape):
    return pl.BlockSpec(shape, lambda *_: (0,) * len(shape))


def attend_forward(qkv, table, segments, heads):
    length = qkv.shape[0]
    rows = min(256, length)
    inner = heads * HD
    return pl.pallas_call(
        partial(forward_kernel, rows=rows, heads=heads),
        grid_spec=pltpu.PrefetchScalarGridSpec(
            num_scalar_prefetch=1,
            grid=(length // rows,),
            in_specs=[
                whole(qkv.shape),
                whole(table.shape),
                whole((length, 1)),
                whole((1, length)),
            ],
            out_specs=[
                pl.BlockSpec((rows, inner), lambda i, ids: (i, 0)),
                pl.BlockSpec((rows, SUB), lambda i, ids: (i, 0)),
            ],
            scratch_shapes=[
                pltpu.VMEM((heads, SUB, 2 * length - SUB), f32),
            ],
        ),
        out_shape=[
            jax.ShapeDtypeStruct((length, inner), bf16),
            jax.ShapeDtypeStruct((length, SUB), f32),
        ],
        compiler_params=pltpu.CompilerParams(vmem_limit_bytes=40 * 1024 * 1024),
        cost_estimate=pl.CostEstimate(
            flops=4 * length * length * inner,
            bytes_accessed=10 * length * inner,
            transcendentals=length * length * heads,
        ),
        name="attend_forward",
    )(segments, qkv, table, segments[:, None], segments[None, :])


def backward_kernel(
    ids_ref,
    qkv_ref,
    out_in_ref,
    grad_ref,
    lse_ref,
    table_ref,
    seg_col_ref,
    seg_row_ref,
    out_ref,
    d_table_ref,
    strip_ref,
    d_strip_ref,
    d_keys_ref,
    d_values_ref,
    *,
    rows,
    heads,
):
    step = pl.program_id(0)
    length = qkv_ref.shape[0]
    inner = heads * HD
    parts = rows // SUB

    @pl.when(step == 0)
    def _():
        fill_strip(table_ref, strip_ref)
        d_strip_ref[...] = jnp.zeros_like(d_strip_ref)
        d_keys_ref[...] = jnp.zeros_like(d_keys_ref)
        d_values_ref[...] = jnp.zeros_like(d_values_ref)

    here = pl.ds(pl.multiple_of(step * rows, rows), rows)
    product = grad_ref[here, :].astype(f32) * out_in_ref[here, :].astype(f32)
    deltas = [
        jnp.sum(product[:, h * HD : (h + 1) * HD], axis=1, keepdims=True) for h in range(heads)
    ]

    def window(begin, width):
        there = pl.ds(begin, width)
        same = seg_col_ref[here, :] == seg_row_ref[:, there]
        q_all = qkv_ref[here, :inner] * jnp.asarray(HD**-0.5, bf16)
        d_queries = []
        for h in range(heads):
            lo = h * HD
            keys = qkv_ref[there, inner + lo : inner + lo + HD]
            values = qkv_ref[there, 2 * inner + lo : 2 * inner + lo + HD]
            grads = grad_ref[here, lo : lo + HD]
            queries = q_all[:, lo : lo + HD]
            bias = jnp.concatenate(
                [
                    strip_ref[h, :, strip_at(step, u, parts, begin, width, length)]
                    for u in range(parts)
                ],
                axis=0,
            )
            scores = mm(queries, keys, NT) + bias - lse_ref[:, h : h + 1]
            probs = jnp.exp(jnp.where(same, scores, -1e9))
            d_values_ref[lo : lo + HD, there] += mm(grads, probs.astype(bf16), TN)
            d_scores = probs * (mm(grads, values, NT) - deltas[h])
            for u in range(parts):
                span = strip_at(step, u, parts, begin, width, length)
                d_strip_ref[h, :, span] += d_scores[u * SUB : (u + 1) * SUB]
            d_raw = d_scores.astype(bf16)
            d_queries.append(mm(d_raw, keys) * HD**-0.5)
            d_keys_ref[lo : lo + HD, there] += mm(queries, d_raw, TN)
        out_ref[here, :inner] = jnp.concatenate(d_queries, axis=1).astype(bf16)

    each_window(ids_ref, step, rows, length, window)

    @pl.when(step == pl.num_programs(0) - 1)
    def _():
        for h in range(heads):
            lo = h * HD
            out_ref[:, inner + lo : inner + lo + HD] = d_keys_ref[lo : lo + HD, :].T.astype(bf16)
            out_ref[:, 2 * inner + lo : 2 * inner + lo + HD] = d_values_ref[
                lo : lo + HD, :
            ].T.astype(bf16)
            summed = jnp.concatenate([d_strip_ref[h], jnp.zeros((SUB, SUB), f32)], axis=1)
            count = SUB
            while count > 1:
                count //= 2
                summed = summed[count:] + pltpu.roll(summed[:count], count, 1)
            d_table_ref[h : h + 1, :] = summed


def attend_backward(qkv, head_out, d_head, lse, table, segments, heads):
    length = qkv.shape[0]
    rows = min(256, length)
    inner = heads * HD
    return pl.pallas_call(
        partial(backward_kernel, rows=rows, heads=heads),
        grid_spec=pltpu.PrefetchScalarGridSpec(
            num_scalar_prefetch=1,
            grid=(length // rows,),
            in_specs=[
                whole(qkv.shape),
                whole(head_out.shape),
                whole(d_head.shape),
                pl.BlockSpec((rows, SUB), lambda i, ids: (i, 0)),
                whole(table.shape),
                whole((length, 1)),
                whole((1, length)),
            ],
            out_specs=[whole(qkv.shape), whole(table.shape)],
            scratch_shapes=[
                pltpu.VMEM((heads, SUB, 2 * length - SUB), f32),
                pltpu.VMEM((heads, SUB, 2 * length - SUB), f32),
                pltpu.VMEM((inner, length), f32),
                pltpu.VMEM((inner, length), f32),
            ],
        ),
        out_shape=[
            jax.ShapeDtypeStruct(qkv.shape, bf16),
            jax.ShapeDtypeStruct(table.shape, f32),
        ],
        compiler_params=pltpu.CompilerParams(vmem_limit_bytes=48 * 1024 * 1024),
        cost_estimate=pl.CostEstimate(
            flops=10 * length * length * inner,
            bytes_accessed=16 * length * inner,
            transcendentals=length * length * heads,
        ),
        name="attend_backward",
    )(segments, qkv, head_out, d_head, lse, table, segments[:, None], segments[None, :])


def joined(block_ref, at):
    rows, cols, _, slots, half = block_ref.shape
    return jnp.concatenate(
        [
            jnp.concatenate([block_ref[at ^ j, c, 0] for c in range(cols)], axis=1)
            for j in range(rows)
        ],
        axis=0,
    )


def halves(own, other, col):
    return jnp.where(
        col == 0,
        jnp.concatenate([own, other], axis=1),
        jnp.concatenate([other, own], axis=1),
    )


def flat(block):
    return block.reshape(-1, block.shape[-1]).astype(f32)


GELU_A = 0.7978845608028654
GELU_B = 0.044715


def gelu_pair(u):
    square = u * u
    factor = 0.5 * jnp.tanh(u * (GELU_A + (GELU_A * GELU_B) * square)) + 0.5
    value = u * factor
    slope = factor + value * (1.0 - factor) * (2 * GELU_A + (6 * GELU_A * GELU_B) * square)
    return value, slope


def router_probs(x, router_ref):
    weights = router_ref[...]
    high = weights.astype(bf16)
    low = (weights - high.astype(f32)).astype(bf16)
    logits = mm(x, high, NT) + mm(x, low, NT)
    exped = jnp.exp(logits - jnp.max(logits, axis=1, keepdims=True))
    return exped / jnp.sum(exped, axis=1, keepdims=True)


def gate(probs, expert):
    picked = lax.broadcasted_iota(jnp.int32, probs.shape, 1) == expert
    return picked, jnp.sum(jnp.where(picked, probs, 0.0), axis=1, keepdims=True)


def expert_kernel(
    at_ref,
    x_in_ref,
    own_ref,
    other_ref,
    router_ref,
    up_ref,
    down_ref,
    out_ref,
    grad_ref,
    d_router_ref,
    x_ref,
    g_ref,
    scaled_ref,
    probs_ref,
    out_acc_ref,
    grad_acc_ref,
):
    expert = pl.program_id(0)
    step = pl.program_id(1)
    col = at_ref[1]
    row = at_ref[2]
    first = at_ref[3]

    @pl.when(step == 0)
    def _():
        x = joined(x_in_ref, row)
        probs = router_probs(x, router_ref)
        _, gating = gate(probs, first + expert)
        g = halves(flat(own_ref[:, 0, 0]), flat(other_ref[:, 0, 0]), col)
        x_ref[...] = x
        g_ref[...] = g
        scaled_ref[...] = (gating * g).astype(bf16)
        probs_ref[...] = probs
        out_acc_ref[...] = jnp.zeros_like(out_acc_ref)
        grad_acc_ref[...] = jnp.zeros_like(grad_acc_ref)

    parts = 3
    tile = up_ref.shape[1] // parts
    activated, d_pre = [], []
    for i in range(parts):
        here = slice(i * tile, (i + 1) * tile)
        value, slope = gelu_pair(mm(x_ref[...], up_ref[0, here], NT))
        activated.append(value.astype(bf16))
        d_pre.append((mm(scaled_ref[...], down_ref[0, here], NT) * slope).astype(bf16))
    out_acc_ref[...] += mm(jnp.concatenate(activated, axis=1), down_ref[0])
    grad_acc_ref[...] += mm(jnp.concatenate(d_pre, axis=1), up_ref[0])

    @pl.when(step == pl.num_programs(1) - 1)
    def _():
        out = out_acc_ref[...]
        probs = probs_ref[...]
        picked, gating = gate(probs, first + expert)
        d_gating = jnp.sum(g_ref[...] * out, axis=1, keepdims=True)
        d_logits = d_gating * probs * (picked.astype(f32) - gating)
        grad = grad_acc_ref[...] + lax.dot_general(
            d_logits, router_ref[...], NN, precision=highest, preferred_element_type=f32
        )
        d_router = lax.dot_general(
            d_logits,
            x_ref[...].astype(f32),
            TN,
            precision=highest,
            preferred_element_type=f32,
        )
        rows, cols, _, slots, half = grad_ref.shape
        out = out.astype(bf16)
        grad = grad.astype(bf16)
        first_half, last_half = out[:, :half], out[:, half:]
        own = jnp.where(col == 0, first_half, last_half)
        other = jnp.where(col == 0, last_half, first_half)
        out_ref[:, 0, 0] = own.reshape(rows, slots, half)
        out_ref[:, 1, 0] = other.reshape(rows, slots, half)
        for j in range(rows):
            for c in range(cols):
                grad_ref[row ^ j, c, 0] = grad[
                    j * slots : (j + 1) * slots, c * half : (c + 1) * half
                ]

        @pl.when(expert == 0)
        def _():
            d_router_ref[...] = d_router

        @pl.when(expert > 0)
        def _():
            d_router_ref[...] += d_router


def run_experts(at, got_x, g_own, g_other, w_router, w_up, w_down):
    rows, cols, experts, slots, half = got_x.shape
    hidden, width = w_up.shape[1:]
    tile = 768
    block = pl.BlockSpec((rows, cols, 1, slots, half), lambda e, f, at: (0, 0, e, 0, 0))
    part = pl.BlockSpec((rows, 1, 1, slots, half), lambda e, f, at: (0, 0, e, 0, 0))
    last = pl.BlockSpec((rows, 1, 1, slots, half), lambda e, f, at: (0, 1, e, 0, 0))
    weight = pl.BlockSpec((1, tile, width), lambda e, f, at: (e, f, 0))
    tokens = rows * slots
    shape = jax.ShapeDtypeStruct(got_x.shape, bf16)
    router_shape = w_router.shape
    return pl.pallas_call(
        expert_kernel,
        grid_spec=pltpu.PrefetchScalarGridSpec(
            num_scalar_prefetch=1,
            grid=(experts, hidden // tile),
            in_specs=[block, part, last, whole(w_router.shape), weight, weight],
            out_specs=[block, block, whole(router_shape)],
            scratch_shapes=[
                pltpu.VMEM((tokens, width), bf16),
                pltpu.VMEM((tokens, width), f32),
                pltpu.VMEM((tokens, width), bf16),
                pltpu.VMEM((tokens, w_router.shape[0]), f32),
                pltpu.VMEM((tokens, width), f32),
                pltpu.VMEM((tokens, width), f32),
            ],
        ),
        out_shape=[shape, shape, jax.ShapeDtypeStruct(router_shape, f32)],
        compiler_params=pltpu.CompilerParams(vmem_limit_bytes=56 * 1024 * 1024),
        cost_estimate=pl.CostEstimate(
            flops=8 * experts * tokens * hidden * width,
            bytes_accessed=4 * experts * hidden * width,
            transcendentals=experts * tokens * hidden,
        ),
        name="experts",
    )(at, got_x, g_own, g_other, w_router, w_up, w_down)


def weight_kernel(
    at_ref,
    x_in_ref,
    own_ref,
    other_ref,
    router_ref,
    up_ref,
    down_ref,
    d_up_ref,
    d_down_ref,
    x_ref,
    g_ref,
    x_turned_ref,
    g_turned_ref,
    *,
    steps,
):
    expert = pl.program_id(0)
    tile = pl.program_id(1)
    step = pl.program_id(2)
    parts = x_in_ref.shape[0]

    @pl.when(jnp.logical_or(tile == 0, steps > 1))
    def _():
        x = jnp.concatenate([joined(x_in_ref.at[i], at_ref[2]) for i in range(parts)], axis=0)
        g = halves(flat(own_ref[:, :, 0, 0]), flat(other_ref[:, :, 0, 0]), at_ref[1])
        _, gating = gate(router_probs(x, router_ref), at_ref[3] + expert)
        g = (gating * g).astype(bf16)
        x_ref[...] = x
        g_ref[...] = g
        x_turned_ref[...] = x.T
        g_turned_ref[...] = g.T

    value, slope = gelu_pair(mm(up_ref[0], x_turned_ref[...]))
    d_pre = (mm(down_ref[0], g_turned_ref[...]) * slope).astype(bf16)
    d_down = mm(value.astype(bf16), g_ref[...])
    d_up = mm(d_pre, x_ref[...])

    @pl.when(step == 0)
    def _():
        d_up_ref[0] = d_up
        d_down_ref[0] = d_down

    @pl.when(step > 0)
    def _():
        d_up_ref[0] += d_up
        d_down_ref[0] += d_down


def weight_grads(at, all_x, g_own, g_other, w_router, w_up, w_down):
    parts, rows, cols, experts, slots, half = all_x.shape
    hidden, width = w_up.shape[1:]
    own = hidden // parts
    tile = 256 if own % 256 == 0 else own
    tiles = own // tile
    each = min(4, parts)
    steps = parts // each
    tokens = each * rows * slots
    block = pl.BlockSpec(
        (each, rows, cols, 1, slots, half), lambda e, f, n, at: (n, 0, 0, e, 0, 0)
    )
    part = pl.BlockSpec(
        (each, rows, 1, 1, slots, half), lambda e, f, n, at: (n, 0, 0, e, 0, 0)
    )
    last = pl.BlockSpec(
        (each, rows, 1, 1, slots, half), lambda e, f, n, at: (n, 0, 1, e, 0, 0)
    )
    weight = pl.BlockSpec((1, tile, width), lambda e, f, n, at: (e, at[0] * tiles + f, 0))
    result = pl.BlockSpec((1, tile, width), lambda e, f, n, at: (e, f, 0))
    shape = jax.ShapeDtypeStruct((experts, own, width), f32)
    return pl.pallas_call(
        partial(weight_kernel, steps=steps),
        grid_spec=pltpu.PrefetchScalarGridSpec(
            num_scalar_prefetch=1,
            grid=(experts, tiles, steps),
            in_specs=[block, part, last, whole(w_router.shape), weight, weight],
            out_specs=[result, result],
            scratch_shapes=[
                pltpu.VMEM((tokens, width), bf16),
                pltpu.VMEM((tokens, width), bf16),
                pltpu.VMEM((width, tokens), bf16),
                pltpu.VMEM((width, tokens), bf16),
            ],
        ),
        out_shape=[shape, shape],
        compiler_params=pltpu.CompilerParams(vmem_limit_bytes=56 * 1024 * 1024),
        cost_estimate=pl.CostEstimate(
            flops=8 * experts * parts * rows * slots * own * width,
            bytes_accessed=12 * experts * own * width + 4 * all_x.size,
            transcendentals=experts * parts * rows * slots * own,
        ),
        name="weight_grads",
    )(at, all_x, g_own, g_other, w_router, w_up, w_down)


def weights_first(r, c):
    return (r, 0) if c == 1 else (r ^ 2, 1)


def weights_second(r, c):
    return (r ^ 2, 1)


def grouped(array, route, cores):
    pairs = []
    for r in range(4):
        for c in cores:
            to_row, to_col = route(r, c)
            pairs.append((r * 2 + c, to_row * 2 + to_col))
    return lax.ppermute(array, group, pairs)


def grads_first(r, c):
    return (r, 1) if c == 0 else (r ^ 2, 0)


def swap_col(array):
    return lax.ppermute(array, "col", [(0, 1), (1, 0)])


def shift(array, axis, bits):
    if bits == 0:
        return array
    count = lax.axis_size(axis)
    return lax.ppermute(array, axis, [(i, i ^ bits) for i in range(count)])


def total_over(array, axis):
    count = lax.axis_size(axis)
    stride = 1
    while stride < count:
        if 4 * stride <= count:
            near, far, last = (shift(array, axis, stride * i) for i in (1, 2, 3))
            array = (array + near) + (far + last)
            stride *= 4
        else:
            array = array + shift(array, axis, stride)
            stride *= 2
    return array


def shards(
    layer_in,
    w_qkv,
    w_proj,
    rel_bias,
    rel_bucket,
    segment_ids,
    gain_attn,
    gain_ffn,
    w_router,
    routes,
    w_up,
    w_down,
    d_layer,
):
    row_count = lax.axis_size("row")
    col_count = lax.axis_size("col")
    dp_count = lax.axis_size("dp")
    dp_at = lax.axis_index("dp")
    row_at = lax.axis_index("row")
    col_at = lax.axis_index("col")
    tok_dev, width = layer_in.shape
    slot_count = max(2, tok_dev // 8)
    half_width = width // col_count
    length = segment_ids.shape[1]
    inner = w_qkv.shape[2]
    heads_dev = inner // HD
    experts_all = EXP_DEV * row_count * col_count
    block_at = row_at % 2
    heads_at = row_at ^ (2 * col_at)
    is_first = col_at == 0

    def both_halves(mine, other, axis):
        return jnp.where(
            is_first,
            jnp.concatenate([mine, other], axis),
            jnp.concatenate([other, mine], axis),
        )

    def my_half(array, axis):
        size = array.shape[axis] // 2
        return lax.dynamic_slice_in_dim(array, col_at * size, size, axis)

    def other_half(array, axis):
        size = array.shape[axis] // 2
        return lax.dynamic_slice_in_dim(array, (1 - col_at) * size, size, axis)

    def own_first(array, axis):
        return jnp.concatenate([my_half(array, axis), other_half(array, axis)], axis)

    def in_sequence(mine, other):
        return jnp.where(
            block_at == 0,
            jnp.concatenate([mine, other], axis=0),
            jnp.concatenate([other, mine], axis=0),
        )

    own_tokens = my_half(layer_in, 0)
    near_tokens = shift(own_tokens, "row", 1)
    w_first = grouped(w_qkv, weights_first, (0, 1))
    w_second = grouped(w_qkv, weights_second, (1,))
    segments_other = swap_col(segment_ids)

    me = row_at * col_count + col_at
    first = me * EXP_DEV
    at = jnp.stack([dp_at, col_at, row_at, first])
    routed = routes[:, 0]
    chosen = routed[:, None] == jnp.arange(experts_all, dtype=jnp.int32)[None, :]
    counts = jnp.cumsum(chosen.astype(jnp.int32), axis=0)
    slot_index = jnp.sum(jnp.where(chosen, counts, 0), axis=-1) - 1
    slots_all = experts_all * slot_count
    slots_dev = EXP_DEV * slot_count
    send_shape = (row_count * col_count, EXP_DEV, slot_count, half_width)
    block_shape = (row_count, col_count, EXP_DEV, slot_count, half_width)

    def one_hot(devices):
        placed = (devices * EXP_DEV + routed % EXP_DEV) * slot_count + slot_index
        slots = jnp.arange(slots_all, dtype=jnp.int32)[:, None]
        return (slots == placed[None, :]).astype(bf16)

    placing = one_hot(routed // EXP_DEV)
    placing_near = one_hot((routed // EXP_DEV) ^ me)

    def all_to_all(array):
        return lax.all_to_all(array, group, split_axis=0, concat_axis=0, tiled=True)

    g_slots = mm(placing_near, d_layer).astype(bf16)
    g_slots = g_slots.reshape(row_count, col_count * slots_dev, half_width)
    g_send = [g_slots[j] for j in range(row_count)]
    near_tokens, g_send = lax.optimization_barrier((near_tokens, g_send))
    g_parts = [shift(g_send[j], "row", j) for j in range(row_count)]
    g_parts[1], w_proj = lax.optimization_barrier((g_parts[1], w_proj))
    w_proj_parts = [shift(w_proj, "row", j) for j in range(row_count)]
    gains = own_first(gain_ffn, 0)
    router = own_first(w_router, 0)
    input_near = own_first(layer_in, 1).astype(f32)

    near_block = both_halves(near_tokens, swap_col(near_tokens), 0)
    tokens_seq = in_sequence(layer_in, near_block).astype(f32)
    w_pair = jnp.concatenate(
        [jnp.where(is_first, w_qkv, w_first), jnp.where(is_first, w_first, w_second)], axis=1
    )
    w_all = jnp.concatenate([w_pair[0], w_pair[1], w_pair[2]], axis=1)
    scale_seq = lax.rsqrt(jnp.mean(tokens_seq * tokens_seq, axis=-1, keepdims=True) + epsilon)
    normed = (tokens_seq * scale_seq * gain_attn).astype(bf16)
    qkv = mm(normed, w_all).astype(bf16)

    buckets = (rel_bucket[:, None] == jnp.arange(NB, dtype=jnp.int32)[None, :]).astype(f32)
    bias_rows = lax.dynamic_slice_in_dim(rel_bias, heads_at * heads_dev, heads_dev, 0)
    bias_table = jnp.einsum("hb,ob->ho", bias_rows, buckets, precision=highest)
    table = jnp.pad(bias_table, ((0, 0), (0, 1)))
    segments = jnp.where(row_at // 2 == col_at, segment_ids, segments_other)[0]

    g_near = jnp.stack(g_parts).reshape(block_shape)
    qkv, g_near, d_layer_late, at = lax.optimization_barrier((qkv, g_near, d_layer, at))
    head_out, lse = attend_forward(qkv, table, segments, heads_dev)

    head_blocks = head_out.reshape(2, tok_dev, inner)
    head_own = lax.dynamic_index_in_dim(head_blocks, block_at, 0, False)
    head_near = shift(lax.dynamic_index_in_dim(head_blocks, 1 - block_at, 0, False), "row", 1)
    head_pair = jnp.concatenate([head_own, head_near], axis=1)
    head_other = swap_col(head_pair)

    all_g = lax.all_gather(g_near, "dp", axis=0, tiled=False)
    w_proj_parts, _ = lax.optimization_barrier((w_proj_parts, head_out))
    proj_own = jnp.concatenate(
        [jnp.where(is_first, w_proj_parts[j], w_proj_parts[j ^ 2]) for j in range(row_count)],
        axis=0,
    )
    proj_other = jnp.roll(swap_col(proj_own), 2 * inner, axis=0)
    proj_all = jnp.concatenate([proj_own, proj_other], axis=1)
    g_other = swap_col(g_near)
    grads_in = jnp.concatenate([d_layer_late, swap_col(d_layer_late)], axis=1).astype(f32)

    heads = jnp.concatenate([head_pair, head_other], axis=1)
    middle = input_near + mm(heads, proj_all)
    scale_ffn = lax.rsqrt(jnp.mean(middle * middle, axis=-1, keepdims=True) + epsilon)
    hidden = middle * scale_ffn * gains
    x_slots = mm(placing, hidden[:, :half_width].astype(bf16)).astype(bf16).reshape(send_shape)
    got_x = all_to_all(x_slots)
    all_x = lax.all_gather(got_x, "dp", axis=0, tiled=False)
    out_slots, grad_slots, d_router = run_experts(
        at, got_x.reshape(block_shape), g_near, g_other, w_router.T, w_up, w_down
    )
    got_grad = all_to_all(grad_slots.reshape(send_shape)).reshape(slots_all, half_width)
    mine = mm(placing, got_grad, TN).astype(bf16)
    d_hidden = jnp.concatenate([mine, swap_col(mine)], axis=1).astype(f32)
    d_gain_ffn = 0.5 * both_halves(
        jnp.sum((middle * scale_ffn * d_hidden)[:, :half_width], axis=0),
        jnp.sum((middle * scale_ffn * d_hidden)[:, half_width:], axis=0),
        0,
    )
    scaled_ffn = d_hidden * gains
    d_middle = (
        grads_in
        + scale_ffn * scaled_ffn
        - middle * scale_ffn**3 * jnp.mean(scaled_ffn * middle, axis=-1, keepdims=True)
    )
    d_attn = d_middle.astype(bf16)
    d_heads = mm(d_attn, proj_all[: 2 * inner], NT).astype(bf16)
    d_head = in_sequence(d_heads[:, :inner], shift(d_heads[:, inner:], "row", 1))

    d_attn_late, d_heads = lax.optimization_barrier((d_attn, d_heads))
    d_proj = mm(heads, d_attn_late[:, :half_width], TN).astype(bf16)
    d_proj = d_proj.reshape(row_count, inner, half_width)
    d_head, d_gain_ffn = lax.optimization_barrier((d_head, d_gain_ffn))
    proj_parts = [
        shift(jnp.where(is_first, d_proj[j], d_proj[j ^ 2]), "row", j)
        for j in range(row_count)
    ]

    d_qkv, d_table = attend_backward(qkv, head_out, d_head, lse, table, segments, heads_dev)

    proj_parts, d_qkv, all_g = lax.optimization_barrier((proj_parts, d_qkv, all_g))
    all_g_other = swap_col(all_g)
    d_w = mm(normed, d_qkv, TN)
    d_w_low = d_w.astype(bf16)
    d_w_sent = jnp.where(is_first, d_w_low[half_width:], d_w_low[:half_width])
    d_w_first = grouped(d_w_sent, grads_first, (0, 1))
    d_w_second = grouped(d_w_low[half_width:], weights_second, (1,))
    gain_part = jnp.sum(d_w * w_all.astype(f32), axis=1) / gain_attn
    d_rel_part = jnp.einsum("ho,ob->hb", d_table[:, : 2 * length - 1], buckets, precision=highest)
    rel_whole = lax.dynamic_update_slice_in_dim(
        jnp.zeros((H, NB), f32), d_rel_part, heads_at * heads_dev, 0
    )
    rel_row = jnp.pad(rel_whole.reshape(1, H * NB), ((0, 0), (0, width - H * NB)))
    spare = jnp.zeros((-(experts_all + 3) % 8, width), f32)
    small = jnp.concatenate(
        [d_router, d_gain_ffn[None], gain_part[None], rel_row, spare], axis=0
    )
    small, all_x = lax.optimization_barrier((small, all_x))
    small = total_over(small, "col")
    small, d_w_first = lax.optimization_barrier((small, d_w_first))
    small = total_over(small, "row")

    d_proj = sum(part.astype(f32) for part in proj_parts)
    d_proj = jnp.concatenate([d_proj, small[:, :half_width], small[:, half_width:]], axis=0)
    d_w = jnp.where(is_first, d_w[:half_width], d_w_second.astype(f32))
    d_w = (d_w + d_w_first.astype(f32)).astype(bf16)
    packed = (d_w, d_proj.astype(bf16))
    summed = lax.psum(packed, "dp")

    at, d_qkv, out_late, packed = lax.optimization_barrier((at, d_qkv, out_slots, packed))
    part_normed = mm(d_qkv, w_all, NT).astype(bf16).reshape(2, tok_dev, width)
    normed_near = shift(lax.dynamic_index_in_dim(part_normed, 1 - block_at, 0, False), "row", 1)
    out_parts = [shift(out_late[j], "row", j) for j in range(row_count)]
    at, part_normed = lax.optimization_barrier((at, part_normed))
    d_up, d_down = weight_grads(
        at,
        all_x.reshape((dp_count,) + block_shape),
        all_g,
        all_g_other,
        w_router.T,
        w_up,
        w_down,
    )
    hidden, normed_near, out_parts, d_up, d_down = lax.optimization_barrier(
        (hidden, normed_near, out_parts, d_up, d_down)
    )
    normed_own = lax.dynamic_index_in_dim(part_normed, block_at, 0, False)
    normed_sum = normed_own.astype(f32) + normed_near.astype(f32)
    normed_other = swap_col(other_half(normed_sum, 0).astype(bf16))
    gate_probs = jax.nn.softmax(jnp.dot(hidden, router, precision=highest), axis=-1)
    gating = jnp.sum(jnp.where(chosen, gate_probs, 0.0), axis=-1, keepdims=True)
    out_stack = jnp.stack(out_parts).reshape(row_count, col_count, slots_dev, half_width)
    out_other = swap_col(out_stack[:, 1])
    out_back = jnp.stack([out_stack[:, 0], out_other], axis=1).reshape(slots_all, half_width)
    layer_out = middle[:, :half_width] + gating * mm(placing_near, out_back, TN)
    d_normed = my_half(normed_sum, 0) + normed_other.astype(f32)
    own = own_tokens.astype(f32)
    scale_own = lax.rsqrt(jnp.mean(own * own, axis=-1, keepdims=True) + epsilon)
    scaled_attn = d_normed * gain_attn
    d_own = scale_own * scaled_attn - own * scale_own**3 * jnp.mean(
        scaled_attn * own, axis=-1, keepdims=True
    )
    d_middle_own = my_half(d_middle, 0)
    d_layer_in = both_halves(
        d_middle_own[:, :half_width] + my_half(d_own, 1),
        swap_col(d_middle_own[:, half_width:] + other_half(d_own, 1)),
        0,
    )
    summed, layer_out, d_layer_in = lax.optimization_barrier((summed, layer_out, d_layer_in))
    d_w, d_proj = (array.astype(f32) for array in summed)
    small = d_proj[inner:].reshape(2, -1, half_width)
    small = jnp.concatenate([small[0], small[1]], axis=1)
    d_proj = d_proj[:inner]
    d_w_qkv = jnp.stack([d_w[:, i * inner : (i + 1) * inner] for i in range(3)])
    d_w_router = small[:experts_all].T
    d_gain_ffn = small[experts_all]
    d_gain_attn = small[experts_all + 1]
    d_rel_bias = small[experts_all + 2, : H * NB].reshape(H, NB)
    return (
        layer_out,
        d_layer_in,
        d_w_qkv,
        d_proj,
        d_rel_bias,
        d_gain_attn,
        d_gain_ffn,
        d_w_router,
        d_up,
        d_down,
    )


def solution(mesh):
    placed = (
        P(("dp", "row"), None),
        P(None, "col", "row"),
        P("row", "col"),
        P(),
        P(),
        P(("dp", "col"), None),
        P(),
        P(),
        P(),
        P(("dp", "row"), None),
        P(("row", "col"), None, None),
        P(("row", "col"), None, None),
        P(("dp", "row"), "col"),
    )
    return jax.shard_map(
        shards,
        mesh=mesh,
        in_specs=placed,
        out_specs=(
            P(("dp", "row"), "col"),
            P(("dp", "row"), "col"),
            P(None, "col", "row"),
            P("row", "col"),
            P(),
            P(),
            P(),
            P(),
            P(("row", "col"), "dp", None),
            P(("row", "col"), "dp", None),
        ),
        check_vma=False,
    )
```

```python
from functools import partial

import jax
import jax.numpy as jnp
from jax import lax
from jax.experimental import pallas as pl
from jax.experimental.pallas import tpu as pltpu
from jax.sharding import PartitionSpec as P

H = 12
HD = 64
NB = 32
EXP_DEV = 2
SUB = 128

epsilon = 1e-06
highest = lax.Precision.HIGHEST
f32 = jnp.float32
bf16 = jnp.bfloat16
group = ("row", "col")

NT = (((1,), (1,)), ((), ()))
NN = (((1,), (0,)), ((), ()))
TN = (((0,), (0,)), ((), ()))


def mm(a, b, dims=NN):
    return lax.dot_general(a, b, dims, preferred_element_type=f32)


def fill_strip(table_ref, strip_ref):
    heads, _, span = strip_ref.shape
    for h in range(heads):
        rows = jnp.broadcast_to(table_ref[h : h + 1, :], (SUB, table_ref.shape[1]))
        rolled = pltpu.roll(rows, table_ref.shape[1] - (SUB - 1), 1, stride=1, stride_axis=0)
        strip_ref[h] = rolled[:, :span]


def strip_at(step, part, parts, keys_at, width, length):
    begin = length - SUB * (step * parts + part + 1) + keys_at
    return pl.ds(pl.multiple_of(begin, SUB), width)


def each_window(ids_ref, step, rows, length, body):
    tiles = length // rows
    first = ids_ref[step * rows]
    last = ids_ref[step * rows + rows - 1]
    lo = jnp.int32(0)
    hi = jnp.int32(0)
    for i in range(tiles):
        lo = lo + (ids_ref[i * rows + rows - 1] < first).astype(jnp.int32)
        hi = hi + (ids_ref[i * rows] <= last).astype(jnp.int32)
    count = hi - lo
    sizes = sorted({min(2, tiles), min(3, tiles), tiles})
    for i, size in enumerate(sizes):
        fits = count <= size if i == 0 else jnp.logical_and(count > sizes[i - 1], count <= size)

        @pl.when(fits)
        def _():
            begin = jnp.minimum(lo, tiles - size) * rows
            body(pl.multiple_of(begin, rows), size * rows)


def forward_kernel(
    ids_ref,
    qkv_ref,
    table_ref,
    seg_col_ref,
    seg_row_ref,
    out_ref,
    lse_ref,
    strip_ref,
    *,
    rows,
    heads,
):
    step = pl.program_id(0)
    length = qkv_ref.shape[0]
    inner = heads * HD
    parts = rows // SUB

    @pl.when(step == 0)
    def _():
        fill_strip(table_ref, strip_ref)

    here = pl.ds(pl.multiple_of(step * rows, rows), rows)

    def window(begin, width):
        there = pl.ds(begin, width)
        same = seg_col_ref[here, :] == seg_row_ref[:, there]
        q_all = qkv_ref[here, :inner] * jnp.asarray(HD**-0.5, bf16)
        lane = lax.broadcasted_iota(jnp.int32, lse_ref.shape, 1)
        lse = jnp.zeros(lse_ref.shape, f32)
        outs = []
        for h in range(heads):
            lo = h * HD
            keys = qkv_ref[there, inner + lo : inner + lo + HD]
            values = qkv_ref[there, 2 * inner + lo : 2 * inner + lo + HD]
            bias = jnp.concatenate(
                [
                    strip_ref[h, :, strip_at(step, u, parts, begin, width, length)]
                    for u in range(parts)
                ],
                axis=0,
            )
            scores = jnp.where(same, mm(q_all[:, lo : lo + HD], keys, NT) + bias, -1e9)
            top = jnp.max(scores, axis=1, keepdims=True)
            weights = jnp.exp(scores - top)
            total = jnp.sum(weights, axis=1, keepdims=True)
            outs.append(mm(weights.astype(bf16), values) / total)
            lse = jnp.where(lane == h, top + jnp.log(total), lse)
        out_ref[...] = jnp.concatenate(outs, axis=1).astype(bf16)
        lse_ref[...] = lse

    each_window(ids_ref, step, rows, length, window)


def whole(shape):
    return pl.BlockSpec(shape, lambda *_: (0,) * len(shape))


def attend_forward(qkv, table, segments, heads):
    length = qkv.shape[0]
    rows = min(256, length)
    inner = heads * HD
    return pl.pallas_call(
        partial(forward_kernel, rows=rows, heads=heads),
        grid_spec=pltpu.PrefetchScalarGridSpec(
            num_scalar_prefetch=1,
            grid=(length // rows,),
            in_specs=[
                whole(qkv.shape),
                whole(table.shape),
                whole((length, 1)),
                whole((1, length)),
            ],
            out_specs=[
                pl.BlockSpec((rows, inner), lambda i, ids: (i, 0)),
                pl.BlockSpec((rows, SUB), lambda i, ids: (i, 0)),
            ],
            scratch_shapes=[
                pltpu.VMEM((heads, SUB, 2 * length - SUB), f32),
            ],
        ),
        out_shape=[
            jax.ShapeDtypeStruct((length, inner), bf16),
            jax.ShapeDtypeStruct((length, SUB), f32),
        ],
        compiler_params=pltpu.CompilerParams(vmem_limit_bytes=40 * 1024 * 1024),
        cost_estimate=pl.CostEstimate(
            flops=4 * length * length * inner,
            bytes_accessed=10 * length * inner,
            transcendentals=length * length * heads,
        ),
        name="attend_forward",
    )(segments, qkv, table, segments[:, None], segments[None, :])


def backward_kernel(
    ids_ref,
    qkv_ref,
    out_in_ref,
    grad_ref,
    lse_ref,
    table_ref,
    seg_col_ref,
    seg_row_ref,
    out_ref,
    d_table_ref,
    strip_ref,
    d_strip_ref,
    d_keys_ref,
    d_values_ref,
    *,
    rows,
    heads,
):
    step = pl.program_id(0)
    length = qkv_ref.shape[0]
    inner = heads * HD
    parts = rows // SUB

    @pl.when(step == 0)
    def _():
        fill_strip(table_ref, strip_ref)
        d_strip_ref[...] = jnp.zeros_like(d_strip_ref)
        d_keys_ref[...] = jnp.zeros_like(d_keys_ref)
        d_values_ref[...] = jnp.zeros_like(d_values_ref)

    here = pl.ds(pl.multiple_of(step * rows, rows), rows)
    product = grad_ref[here, :].astype(f32) * out_in_ref[here, :].astype(f32)
    deltas = [
        jnp.sum(product[:, h * HD : (h + 1) * HD], axis=1, keepdims=True) for h in range(heads)
    ]

    def window(begin, width):
        there = pl.ds(begin, width)
        same = seg_col_ref[here, :] == seg_row_ref[:, there]
        q_all = qkv_ref[here, :inner] * jnp.asarray(HD**-0.5, bf16)
        d_queries = []
        for h in range(heads):
            lo = h * HD
            keys = qkv_ref[there, inner + lo : inner + lo + HD]
            values = qkv_ref[there, 2 * inner + lo : 2 * inner + lo + HD]
            grads = grad_ref[here, lo : lo + HD]
            queries = q_all[:, lo : lo + HD]
            bias = jnp.concatenate(
                [
                    strip_ref[h, :, strip_at(step, u, parts, begin, width, length)]
                    for u in range(parts)
                ],
                axis=0,
            )
            scores = mm(queries, keys, NT) + bias - lse_ref[:, h : h + 1]
            probs = jnp.exp(jnp.where(same, scores, -1e9))
            d_values_ref[lo : lo + HD, there] += mm(grads, probs.astype(bf16), TN)
            d_scores = probs * (mm(grads, values, NT) - deltas[h])
            for u in range(parts):
                span = strip_at(step, u, parts, begin, width, length)
                d_strip_ref[h, :, span] += d_scores[u * SUB : (u + 1) * SUB]
            d_raw = d_scores.astype(bf16)
            d_queries.append(mm(d_raw, keys) * HD**-0.5)
            d_keys_ref[lo : lo + HD, there] += mm(queries, d_raw, TN)
        out_ref[here, :inner] = jnp.concatenate(d_queries, axis=1).astype(bf16)

    each_window(ids_ref, step, rows, length, window)

    @pl.when(step == pl.num_programs(0) - 1)
    def _():
        for h in range(heads):
            lo = h * HD
            out_ref[:, inner + lo : inner + lo + HD] = d_keys_ref[lo : lo + HD, :].T.astype(bf16)
            out_ref[:, 2 * inner + lo : 2 * inner + lo + HD] = d_values_ref[
                lo : lo + HD, :
            ].T.astype(bf16)
            summed = jnp.concatenate([d_strip_ref[h], jnp.zeros((SUB, SUB), f32)], axis=1)
            count = SUB
            while count > 1:
                count //= 2
                summed = summed[count:] + pltpu.roll(summed[:count], count, 1)
            d_table_ref[h : h + 1, :] = summed


def attend_backward(qkv, head_out, d_head, lse, table, segments, heads):
    length = qkv.shape[0]
    rows = min(256, length)
    inner = heads * HD
    return pl.pallas_call(
        partial(backward_kernel, rows=rows, heads=heads),
        grid_spec=pltpu.PrefetchScalarGridSpec(
            num_scalar_prefetch=1,
            grid=(length // rows,),
            in_specs=[
                whole(qkv.shape),
                whole(head_out.shape),
                whole(d_head.shape),
                pl.BlockSpec((rows, SUB), lambda i, ids: (i, 0)),
                whole(table.shape),
                whole((length, 1)),
                whole((1, length)),
            ],
            out_specs=[whole(qkv.shape), whole(table.shape)],
            scratch_shapes=[
                pltpu.VMEM((heads, SUB, 2 * length - SUB), f32),
                pltpu.VMEM((heads, SUB, 2 * length - SUB), f32),
                pltpu.VMEM((inner, length), f32),
                pltpu.VMEM((inner, length), f32),
            ],
        ),
        out_shape=[
            jax.ShapeDtypeStruct(qkv.shape, bf16),
            jax.ShapeDtypeStruct(table.shape, f32),
        ],
        compiler_params=pltpu.CompilerParams(vmem_limit_bytes=48 * 1024 * 1024),
        cost_estimate=pl.CostEstimate(
            flops=10 * length * length * inner,
            bytes_accessed=16 * length * inner,
            transcendentals=length * length * heads,
        ),
        name="attend_backward",
    )(segments, qkv, head_out, d_head, lse, table, segments[:, None], segments[None, :])


def joined(block_ref, at):
    rows, cols, _, slots, half = block_ref.shape
    return jnp.concatenate(
        [
            jnp.concatenate([block_ref[at ^ j, c, 0] for c in range(cols)], axis=1)
            for j in range(rows)
        ],
        axis=0,
    )


def halves(own, other, col):
    return jnp.where(
        col == 0,
        jnp.concatenate([own, other], axis=1),
        jnp.concatenate([other, own], axis=1),
    )


def flat(block):
    return block.reshape(-1, block.shape[-1]).astype(f32)


GELU_A = 0.7978845608028654
GELU_B = 0.044715


def gelu_pair(u):
    square = u * u
    factor = 0.5 * jnp.tanh(u * (GELU_A + (GELU_A * GELU_B) * square)) + 0.5
    value = u * factor
    slope = factor + value * (1.0 - factor) * (2 * GELU_A + (6 * GELU_A * GELU_B) * square)
    return value, slope


def router_probs(x, router_ref):
    weights = router_ref[...]
    high = weights.astype(bf16)
    low = (weights - high.astype(f32)).astype(bf16)
    logits = mm(x, high, NT) + mm(x, low, NT)
    exped = jnp.exp(logits - jnp.max(logits, axis=1, keepdims=True))
    return exped / jnp.sum(exped, axis=1, keepdims=True)


def gate(probs, expert):
    picked = lax.broadcasted_iota(jnp.int32, probs.shape, 1) == expert
    return picked, jnp.sum(jnp.where(picked, probs, 0.0), axis=1, keepdims=True)


def expert_kernel(
    at_ref,
    x_in_ref,
    own_ref,
    other_ref,
    router_ref,
    up_ref,
    down_ref,
    out_ref,
    grad_ref,
    d_router_ref,
    x_ref,
    g_ref,
    scaled_ref,
    probs_ref,
    out_acc_ref,
    grad_acc_ref,
):
    expert = pl.program_id(0)
    step = pl.program_id(1)
    col = at_ref[1]
    row = at_ref[2]
    first = at_ref[3]

    @pl.when(step == 0)
    def _():
        x = joined(x_in_ref, row)
        probs = router_probs(x, router_ref)
        _, gating = gate(probs, first + expert)
        g = halves(flat(own_ref[:, 0, 0]), flat(other_ref[:, 0, 0]), col)
        x_ref[...] = x
        g_ref[...] = g
        scaled_ref[...] = (gating * g).astype(bf16)
        probs_ref[...] = probs
        out_acc_ref[...] = jnp.zeros_like(out_acc_ref)
        grad_acc_ref[...] = jnp.zeros_like(grad_acc_ref)

    parts = 3
    tile = up_ref.shape[1] // parts
    activated, d_pre = [], []
    for i in range(parts):
        here = slice(i * tile, (i + 1) * tile)
        value, slope = gelu_pair(mm(x_ref[...], up_ref[0, here], NT))
        activated.append(value.astype(bf16))
        d_pre.append((mm(scaled_ref[...], down_ref[0, here], NT) * slope).astype(bf16))
    out_acc_ref[...] += mm(jnp.concatenate(activated, axis=1), down_ref[0])
    grad_acc_ref[...] += mm(jnp.concatenate(d_pre, axis=1), up_ref[0])

    @pl.when(step == pl.num_programs(1) - 1)
    def _():
        out = out_acc_ref[...]
        probs = probs_ref[...]
        picked, gating = gate(probs, first + expert)
        d_gating = jnp.sum(g_ref[...] * out, axis=1, keepdims=True)
        d_logits = d_gating * probs * (picked.astype(f32) - gating)
        grad = grad_acc_ref[...] + lax.dot_general(
            d_logits, router_ref[...], NN, precision=highest, preferred_element_type=f32
        )
        d_router = lax.dot_general(
            d_logits,
            x_ref[...].astype(f32),
            TN,
            precision=highest,
            preferred_element_type=f32,
        )
        rows, cols, _, slots, half = grad_ref.shape
        out = out.astype(bf16)
        grad = grad.astype(bf16)
        first_half, last_half = out[:, :half], out[:, half:]
        own = jnp.where(col == 0, first_half, last_half)
        other = jnp.where(col == 0, last_half, first_half)
        out_ref[:, 0, 0] = own.reshape(rows, slots, half)
        out_ref[:, 1, 0] = other.reshape(rows, slots, half)
        for j in range(rows):
            for c in range(cols):
                grad_ref[row ^ j, c, 0] = grad[
                    j * slots : (j + 1) * slots, c * half : (c + 1) * half
                ]

        @pl.when(expert == 0)
        def _():
            d_router_ref[...] = d_router

        @pl.when(expert > 0)
        def _():
            d_router_ref[...] += d_router


def run_experts(at, got_x, g_own, g_other, w_router, w_up, w_down):
    rows, cols, experts, slots, half = got_x.shape
    hidden, width = w_up.shape[1:]
    tile = 768
    block = pl.BlockSpec((rows, cols, 1, slots, half), lambda e, f, at: (0, 0, e, 0, 0))
    part = pl.BlockSpec((rows, 1, 1, slots, half), lambda e, f, at: (0, 0, e, 0, 0))
    last = pl.BlockSpec((rows, 1, 1, slots, half), lambda e, f, at: (0, 1, e, 0, 0))
    weight = pl.BlockSpec((1, tile, width), lambda e, f, at: (e, f, 0))
    tokens = rows * slots
    shape = jax.ShapeDtypeStruct(got_x.shape, bf16)
    router_shape = w_router.shape
    return pl.pallas_call(
        expert_kernel,
        grid_spec=pltpu.PrefetchScalarGridSpec(
            num_scalar_prefetch=1,
            grid=(experts, hidden // tile),
            in_specs=[block, part, last, whole(w_router.shape), weight, weight],
            out_specs=[block, block, whole(router_shape)],
            scratch_shapes=[
                pltpu.VMEM((tokens, width), bf16),
                pltpu.VMEM((tokens, width), f32),
                pltpu.VMEM((tokens, width), bf16),
                pltpu.VMEM((tokens, w_router.shape[0]), f32),
                pltpu.VMEM((tokens, width), f32),
                pltpu.VMEM((tokens, width), f32),
            ],
        ),
        out_shape=[shape, shape, jax.ShapeDtypeStruct(router_shape, f32)],
        compiler_params=pltpu.CompilerParams(vmem_limit_bytes=56 * 1024 * 1024),
        cost_estimate=pl.CostEstimate(
            flops=8 * experts * tokens * hidden * width,
            bytes_accessed=4 * experts * hidden * width,
            transcendentals=experts * tokens * hidden,
        ),
        name="experts",
    )(at, got_x, g_own, g_other, w_router, w_up, w_down)


def weight_kernel(
    at_ref,
    x_in_ref,
    own_ref,
    other_ref,
    router_ref,
    up_ref,
    down_ref,
    d_up_ref,
    d_down_ref,
    x_ref,
    g_ref,
    x_turned_ref,
    g_turned_ref,
    *,
    steps,
):
    expert = pl.program_id(0)
    tile = pl.program_id(1)
    step = pl.program_id(2)
    parts = x_in_ref.shape[0]

    @pl.when(jnp.logical_or(tile == 0, steps > 1))
    def _():
        x = jnp.concatenate([joined(x_in_ref.at[i], at_ref[2]) for i in range(parts)], axis=0)
        g = halves(flat(own_ref[:, :, 0, 0]), flat(other_ref[:, :, 0, 0]), at_ref[1])
        _, gating = gate(router_probs(x, router_ref), at_ref[3] + expert)
        g = (gating * g).astype(bf16)
        x_ref[...] = x
        g_ref[...] = g
        x_turned_ref[...] = x.T
        g_turned_ref[...] = g.T

    value, slope = gelu_pair(mm(up_ref[0], x_turned_ref[...]))
    d_pre = (mm(down_ref[0], g_turned_ref[...]) * slope).astype(bf16)
    d_down = mm(value.astype(bf16), g_ref[...])
    d_up = mm(d_pre, x_ref[...])

    @pl.when(step == 0)
    def _():
        d_up_ref[0] = d_up
        d_down_ref[0] = d_down

    @pl.when(step > 0)
    def _():
        d_up_ref[0] += d_up
        d_down_ref[0] += d_down


def weight_grads(at, all_x, g_own, g_other, w_router, w_up, w_down):
    parts, rows, cols, experts, slots, half = all_x.shape
    hidden, width = w_up.shape[1:]
    own = hidden // parts
    tile = 256 if own % 256 == 0 else own
    tiles = own // tile
    each = min(4, parts)
    steps = parts // each
    tokens = each * rows * slots
    block = pl.BlockSpec(
        (each, rows, cols, 1, slots, half), lambda e, f, n, at: (n, 0, 0, e, 0, 0)
    )
    part = pl.BlockSpec(
        (each, rows, 1, 1, slots, half), lambda e, f, n, at: (n, 0, 0, e, 0, 0)
    )
    last = pl.BlockSpec(
        (each, rows, 1, 1, slots, half), lambda e, f, n, at: (n, 0, 1, e, 0, 0)
    )
    weight = pl.BlockSpec((1, tile, width), lambda e, f, n, at: (e, at[0] * tiles + f, 0))
    result = pl.BlockSpec((1, tile, width), lambda e, f, n, at: (e, f, 0))
    shape = jax.ShapeDtypeStruct((experts, own, width), f32)
    return pl.pallas_call(
        partial(weight_kernel, steps=steps),
        grid_spec=pltpu.PrefetchScalarGridSpec(
            num_scalar_prefetch=1,
            grid=(experts, tiles, steps),
            in_specs=[block, part, last, whole(w_router.shape), weight, weight],
            out_specs=[result, result],
            scratch_shapes=[
                pltpu.VMEM((tokens, width), bf16),
                pltpu.VMEM((tokens, width), bf16),
                pltpu.VMEM((width, tokens), bf16),
                pltpu.VMEM((width, tokens), bf16),
            ],
        ),
        out_shape=[shape, shape],
        compiler_params=pltpu.CompilerParams(vmem_limit_bytes=56 * 1024 * 1024),
        cost_estimate=pl.CostEstimate(
            flops=8 * experts * parts * rows * slots * own * width,
            bytes_accessed=12 * experts * own * width + 4 * all_x.size,
            transcendentals=experts * parts * rows * slots * own,
        ),
        name="weight_grads",
    )(at, all_x, g_own, g_other, w_router, w_up, w_down)


def weights_first(r, c):
    return (r, 0) if c == 1 else (r ^ 2, 1)


def weights_second(r, c):
    return (r ^ 2, 1)


def grouped(array, route, cores):
    pairs = []
    for r in range(4):
        for c in cores:
            to_row, to_col = route(r, c)
            pairs.append((r * 2 + c, to_row * 2 + to_col))
    return lax.ppermute(array, group, pairs)


def grads_first(r, c):
    return (r, 1) if c == 0 else (r ^ 2, 0)


def swap_col(array):
    return lax.ppermute(array, "col", [(0, 1), (1, 0)])


def shift(array, axis, bits):
    if bits == 0:
        return array
    count = lax.axis_size(axis)
    return lax.ppermute(array, axis, [(i, i ^ bits) for i in range(count)])


def total_over(array, axis):
    count = lax.axis_size(axis)
    stride = 1
    while stride < count:
        if 4 * stride <= count:
            near, far, last = (shift(array, axis, stride * i) for i in (1, 2, 3))
            array = (array + near) + (far + last)
            stride *= 4
        else:
            array = array + shift(array, axis, stride)
            stride *= 2
    return array


def shards(
    layer_in,
    w_qkv,
    w_proj,
    rel_bias,
    rel_bucket,
    segment_ids,
    gain_attn,
    gain_ffn,
    w_router,
    routes,
    w_up,
    w_down,
    d_layer,
):
    row_count = lax.axis_size("row")
    col_count = lax.axis_size("col")
    dp_count = lax.axis_size("dp")
    dp_at = lax.axis_index("dp")
    row_at = lax.axis_index("row")
    col_at = lax.axis_index("col")
    tok_dev, width = layer_in.shape
    slot_count = max(2, tok_dev // 8)
    half_width = width // col_count
    length = segment_ids.shape[1]
    inner = w_qkv.shape[2]
    heads_dev = inner // HD
    experts_all = EXP_DEV * row_count * col_count
    block_at = row_at % 2
    heads_at = row_at ^ (2 * col_at)
    is_first = col_at == 0

    def both_halves(mine, other, axis):
        return jnp.where(
            is_first,
            jnp.concatenate([mine, other], axis),
            jnp.concatenate([other, mine], axis),
        )

    def my_half(array, axis):
        size = array.shape[axis] // 2
        return lax.dynamic_slice_in_dim(array, col_at * size, size, axis)

    def other_half(array, axis):
        size = array.shape[axis] // 2
        return lax.dynamic_slice_in_dim(array, (1 - col_at) * size, size, axis)

    def own_first(array, axis):
        return jnp.concatenate([my_half(array, axis), other_half(array, axis)], axis)

    def in_sequence(mine, other):
        return jnp.where(
            block_at == 0,
            jnp.concatenate([mine, other], axis=0),
            jnp.concatenate([other, mine], axis=0),
        )

    own_tokens = my_half(layer_in, 0)
    near_tokens = shift(own_tokens, "row", 1)
    w_first = grouped(w_qkv, weights_first, (0, 1))
    w_second = grouped(w_qkv, weights_second, (1,))
    segments_other = swap_col(segment_ids)

    me = row_at * col_count + col_at
    first = me * EXP_DEV
    at = jnp.stack([dp_at, col_at, row_at, first])
    routed = routes[:, 0]
    chosen = routed[:, None] == jnp.arange(experts_all, dtype=jnp.int32)[None, :]
    counts = jnp.cumsum(chosen.astype(jnp.int32), axis=0)
    slot_index = jnp.sum(jnp.where(chosen, counts, 0), axis=-1) - 1
    slots_all = experts_all * slot_count
    slots_dev = EXP_DEV * slot_count
    send_shape = (row_count * col_count, EXP_DEV, slot_count, half_width)
    block_shape = (row_count, col_count, EXP_DEV, slot_count, half_width)

    def one_hot(devices):
        placed = (devices * EXP_DEV + routed % EXP_DEV) * slot_count + slot_index
        slots = jnp.arange(slots_all, dtype=jnp.int32)[:, None]
        return (slots == placed[None, :]).astype(bf16)

    placing = one_hot(routed // EXP_DEV)
    placing_near = one_hot((routed // EXP_DEV) ^ me)

    def all_to_all(array):
        return lax.all_to_all(array, group, split_axis=0, concat_axis=0, tiled=True)

    g_slots = mm(placing_near, d_layer).astype(bf16)
    g_slots = g_slots.reshape(row_count, col_count * slots_dev, half_width)
    g_send = [g_slots[j] for j in range(row_count)]
    near_tokens, g_send = lax.optimization_barrier((near_tokens, g_send))
    g_parts = [shift(g_send[j], "row", j) for j in range(row_count)]
    g_parts[1], w_proj = lax.optimization_barrier((g_parts[1], w_proj))
    w_proj_parts = [shift(w_proj, "row", j) for j in range(row_count)]
    gains = own_first(gain_ffn, 0)
    router = own_first(w_router, 0)
    input_near = own_first(layer_in, 1).astype(f32)

    near_block = both_halves(near_tokens, swap_col(near_tokens), 0)
    tokens_seq = in_sequence(layer_in, near_block).astype(f32)
    w_pair = jnp.concatenate(
        [jnp.where(is_first, w_qkv, w_first), jnp.where(is_first, w_first, w_second)], axis=1
    )
    w_all = jnp.concatenate([w_pair[0], w_pair[1], w_pair[2]], axis=1)
    scale_seq = lax.rsqrt(jnp.mean(tokens_seq * tokens_seq, axis=-1, keepdims=True) + epsilon)
    normed = (tokens_seq * scale_seq * gain_attn).astype(bf16)
    qkv = mm(normed, w_all).astype(bf16)

    buckets = (rel_bucket[:, None] == jnp.arange(NB, dtype=jnp.int32)[None, :]).astype(f32)
    bias_rows = lax.dynamic_slice_in_dim(rel_bias, heads_at * heads_dev, heads_dev, 0)
    bias_table = jnp.einsum("hb,ob->ho", bias_rows, buckets, precision=highest)
    table = jnp.pad(bias_table, ((0, 0), (0, 1)))
    segments = jnp.where(row_at // 2 == col_at, segment_ids, segments_other)[0]

    g_near = jnp.stack(g_parts).reshape(block_shape)
    qkv, g_near, d_layer_late, at = lax.optimization_barrier((qkv, g_near, d_layer, at))
    head_out, lse = attend_forward(qkv, table, segments, heads_dev)

    head_blocks = head_out.reshape(2, tok_dev, inner)
    head_own = lax.dynamic_index_in_dim(head_blocks, block_at, 0, False)
    head_near = shift(lax.dynamic_index_in_dim(head_blocks, 1 - block_at, 0, False), "row", 1)
    head_pair = jnp.concatenate([head_own, head_near], axis=1)
    head_other = swap_col(head_pair)

    all_g = lax.all_gather(g_near, "dp", axis=0, tiled=False)
    w_proj_parts, _ = lax.optimization_barrier((w_proj_parts, head_out))
    proj_own = jnp.concatenate(
        [jnp.where(is_first, w_proj_parts[j], w_proj_parts[j ^ 2]) for j in range(row_count)],
        axis=0,
    )
    proj_other = jnp.roll(swap_col(proj_own), 2 * inner, axis=0)
    proj_all = jnp.concatenate([proj_own, proj_other], axis=1)
    g_other = swap_col(g_near)
    grads_in = jnp.concatenate([d_layer_late, swap_col(d_layer_late)], axis=1).astype(f32)

    heads = jnp.concatenate([head_pair, head_other], axis=1)
    middle = input_near + mm(heads, proj_all)
    scale_ffn = lax.rsqrt(jnp.mean(middle * middle, axis=-1, keepdims=True) + epsilon)
    hidden = middle * scale_ffn * gains
    x_slots = mm(placing, hidden[:, :half_width].astype(bf16)).astype(bf16).reshape(send_shape)
    got_x = all_to_all(x_slots)
    all_x = lax.all_gather(got_x, "dp", axis=0, tiled=False)
    out_slots, grad_slots, d_router = run_experts(
        at, got_x.reshape(block_shape), g_near, g_other, w_router.T, w_up, w_down
    )
    got_grad = all_to_all(grad_slots.reshape(send_shape)).reshape(slots_all, half_width)
    mine = mm(placing, got_grad, TN).astype(bf16)
    d_hidden = jnp.concatenate([mine, swap_col(mine)], axis=1).astype(f32)
    d_gain_ffn = 0.5 * both_halves(
        jnp.sum((middle * scale_ffn * d_hidden)[:, :half_width], axis=0),
        jnp.sum((middle * scale_ffn * d_hidden)[:, half_width:], axis=0),
        0,
    )
    scaled_ffn = d_hidden * gains
    d_middle = (
        grads_in
        + scale_ffn * scaled_ffn
        - middle * scale_ffn**3 * jnp.mean(scaled_ffn * middle, axis=-1, keepdims=True)
    )
    d_attn = d_middle.astype(bf16)
    d_heads = mm(d_attn, proj_all[: 2 * inner], NT).astype(bf16)
    d_head = in_sequence(d_heads[:, :inner], shift(d_heads[:, inner:], "row", 1))

    d_attn_late, d_heads = lax.optimization_barrier((d_attn, d_heads))
    d_proj = mm(heads, d_attn_late[:, :half_width], TN).astype(bf16)
    d_proj = d_proj.reshape(row_count, inner, half_width)
    d_head, d_gain_ffn = lax.optimization_barrier((d_head, d_gain_ffn))
    proj_parts = [
        shift(jnp.where(is_first, d_proj[j], d_proj[j ^ 2]), "row", j)
        for j in range(row_count)
    ]

    d_qkv, d_table = attend_backward(qkv, head_out, d_head, lse, table, segments, heads_dev)

    proj_parts, d_qkv, all_g = lax.optimization_barrier((proj_parts, d_qkv, all_g))
    all_g_other = swap_col(all_g)
    d_w = mm(normed, d_qkv, TN)
    d_w_low = d_w.astype(bf16)
    d_w_sent = jnp.where(is_first, d_w_low[half_width:], d_w_low[:half_width])
    d_w_sent, d_w_low, all_x = lax.optimization_barrier((d_w_sent, d_w_low, all_x))
    d_w_first = grouped(d_w_sent, grads_first, (0, 1))
    d_w_second = grouped(d_w_low[half_width:], weights_second, (1,))
    gain_part = jnp.sum(d_w * w_all.astype(f32), axis=1) / gain_attn
    d_rel_part = jnp.einsum("ho,ob->hb", d_table[:, : 2 * length - 1], buckets, precision=highest)
    rel_whole = lax.dynamic_update_slice_in_dim(
        jnp.zeros((H, NB), f32), d_rel_part, heads_at * heads_dev, 0
    )
    rel_row = jnp.pad(rel_whole.reshape(1, H * NB), ((0, 0), (0, width - H * NB)))
    spare = jnp.zeros((-(experts_all + 3) % 8, width), f32)
    small = jnp.concatenate(
        [d_router, d_gain_ffn[None], gain_part[None], rel_row, spare], axis=0
    )
    small = total_over(small, "col")
    small, d_w_first = lax.optimization_barrier((small, d_w_first))
    small = total_over(small, "row")

    d_proj = sum(part.astype(f32) for part in proj_parts)
    d_proj = jnp.concatenate([d_proj, small[:, :half_width], small[:, half_width:]], axis=0)
    d_w = jnp.where(is_first, d_w[:half_width], d_w_second.astype(f32))
    d_w = (d_w + d_w_first.astype(f32)).astype(bf16)
    packed = (d_w, d_proj.astype(bf16))
    summed = lax.psum(packed, "dp")

    at, d_qkv, out_late, packed = lax.optimization_barrier((at, d_qkv, out_slots, packed))
    part_normed = mm(d_qkv, w_all, NT).astype(bf16).reshape(2, tok_dev, width)
    normed_near = shift(lax.dynamic_index_in_dim(part_normed, 1 - block_at, 0, False), "row", 1)
    out_parts = [shift(out_late[j], "row", j) for j in range(row_count)]
    at, part_normed = lax.optimization_barrier((at, part_normed))
    d_up, d_down = weight_grads(
        at,
        all_x.reshape((dp_count,) + block_shape),
        all_g,
        all_g_other,
        w_router.T,
        w_up,
        w_down,
    )
    hidden, normed_near, out_parts, d_up, d_down = lax.optimization_barrier(
        (hidden, normed_near, out_parts, d_up, d_down)
    )
    normed_own = lax.dynamic_index_in_dim(part_normed, block_at, 0, False)
    normed_sum = normed_own.astype(f32) + normed_near.astype(f32)
    normed_other = swap_col(other_half(normed_sum, 0).astype(bf16))
    gate_probs = jax.nn.softmax(jnp.dot(hidden, router, precision=highest), axis=-1)
    gating = jnp.sum(jnp.where(chosen, gate_probs, 0.0), axis=-1, keepdims=True)
    out_stack = jnp.stack(out_parts).reshape(row_count, col_count, slots_dev, half_width)
    out_other = swap_col(out_stack[:, 1])
    out_back = jnp.stack([out_stack[:, 0], out_other], axis=1).reshape(slots_all, half_width)
    layer_out = middle[:, :half_width] + gating * mm(placing_near, out_back, TN)
    d_normed = my_half(normed_sum, 0) + normed_other.astype(f32)
    own = own_tokens.astype(f32)
    scale_own = lax.rsqrt(jnp.mean(own * own, axis=-1, keepdims=True) + epsilon)
    scaled_attn = d_normed * gain_attn
    d_own = scale_own * scaled_attn - own * scale_own**3 * jnp.mean(
        scaled_attn * own, axis=-1, keepdims=True
    )
    d_middle_own = my_half(d_middle, 0)
    d_layer_in = both_halves(
        d_middle_own[:, :half_width] + my_half(d_own, 1),
        swap_col(d_middle_own[:, half_width:] + other_half(d_own, 1)),
        0,
    )
    summed, layer_out, d_layer_in = lax.optimization_barrier((summed, layer_out, d_layer_in))
    d_w, d_proj = (array.astype(f32) for array in summed)
    small = d_proj[inner:].reshape(2, -1, half_width)
    small = jnp.concatenate([small[0], small[1]], axis=1)
    d_proj = d_proj[:inner]
    d_w_qkv = jnp.stack([d_w[:, i * inner : (i + 1) * inner] for i in range(3)])
    d_w_router = small[:experts_all].T
    d_gain_ffn = small[experts_all]
    d_gain_attn = small[experts_all + 1]
    d_rel_bias = small[experts_all + 2, : H * NB].reshape(H, NB)
    return (
        layer_out,
        d_layer_in,
        d_w_qkv,
        d_proj,
        d_rel_bias,
        d_gain_attn,
        d_gain_ffn,
        d_w_router,
        d_up,
        d_down,
    )


def solution(mesh):
    placed = (
        P(("dp", "row"), None),
        P(None, "col", "row"),
        P("row", "col"),
        P(),
        P(),
        P(("dp", "col"), None),
        P(),
        P(),
        P(),
        P(("dp", "row"), None),
        P(("row", "col"), None, None),
        P(("row", "col"), None, None),
        P(("dp", "row"), "col"),
    )
    return jax.shard_map(
        shards,
        mesh=mesh,
        in_specs=placed,
        out_specs=(
            P(("dp", "row"), "col"),
            P(("dp", "row"), "col"),
            P(None, "col", "row"),
            P("row", "col"),
            P(),
            P(),
            P(),
            P(),
            P(("row", "col"), "dp", None),
            P(("row", "col"), "dp", None),
        ),
        check_vma=False,
    )
```
